32 devices in a mesh: rows: 4 (over y, x), heads: 8 (over z, core).
Axes of the slice: x: 2, y: 2, z: 4, core: 2. Of those that a mesh axis runs over, the one named last changes fastest.
Arguments:
- tokens: bfloat16 [1408, 8, 1152], P('heads', 'rows'), may hold values from -6 to 6
- cond: bfloat16 [8, 11, 1152], P('rows'), may hold values from -6 to 6
- lengths: int32 [8, 11], P('rows'), may hold values from 0 to 512, as said below
- pads: int32 [8, 11], P('rows'), may hold values from 0 to 128, as said below
- timesteps: int32 [8, 11], P('rows'), may hold values from 0 to 999
- head_mask: int32 [8, 11, 16], P('rows'), may hold values 0 or 1
- group_mask: int32 [8, 11, 16], P('rows'), may hold values 0 or 1
- keep: int32 [1408, 8], P('heads', 'rows'), may hold values 0 or 1
- ada_w: bfloat16 [1152, 6912], P(None, 'heads'), may hold values from -0.1875 to 0.1875
- ada_b: bfloat16 [6912], P('heads'), may hold values from -1.5 to 1.5
- w_qkv: bfloat16 [1152, 3456], P(None, 'heads'), may hold values from -0.1875 to 0.1875
- b_qv: bfloat16 [2304], P('heads'), may hold values from -1.5 to 1.5
- w_out: bfloat16 [1152, 1152], P('heads'), may hold values from -1.5 to 1.5
- b_out: bfloat16 [1152], replicated, may hold values from -1.5 to 1.5
- w_up: bfloat16 [1152, 4608], P(None, 'heads'), may hold values from -0.1875 to 0.1875
- b_up: bfloat16 [4608], P('heads'), may hold values from -1.5 to 1.5
- w_down: bfloat16 [4608, 1152], P('heads'), may hold values from -0.1875 to 0.1875
- b_down: bfloat16 [1152], replicated, may hold values from -1.5 to 1.5
- w_route: bfloat16 [1152], replicated, may hold values from -0.1875 to 0.1875
- grad_out: bfloat16 [1408, 8, 1152], P('heads', 'rows'), may hold values from -6 to 6
Outputs:
- final: bfloat16 [1408, 8, 1152], P('heads', 'rows')
- grad_tokens: float32 [1408, 8, 1152], P('heads', 'rows')
- grad_cond: float32 [8, 11, 1152], P('rows')
- grad_ada_w: float32 [1152, 6912], P(None, 'heads')
- grad_ada_b: float32 [6912], P('heads')
- grad_w_qkv: float32 [1152, 3456], P(None, 'heads')
- grad_b_qv: float32 [2304], P('heads')
- grad_w_out: float32 [1152, 1152], P('heads')
- grad_b_out: float32 [1152], P('heads')
- grad_w_up: float32 [1152, 4608], P(None, 'heads')
- grad_b_up: float32 [4608], P('heads')
- grad_w_down: float32 [4608, 1152], P('heads')
- grad_b_down: float32 [1152], P('heads')
- grad_w_route: float32 [1152], P('heads')
The draws below stay inside these ranges and needn't reach their ends.
Inputs may be any that keep to these rules, and one draw needn't show every extreme that they name: Each row's nonzero crop lengths are multiples of 64 from 128 to 512, fill the leading slots, are followed by zeros, and sum to 1408. `pads`: at most a quarter of the crop's length; 0 in empty slots.
All inputs are finite; a program needn't handle non-finite values. No bound on the sum of `head_mask` or of `group_mask` or of `keep` on one device may be relied on, other than what follows from the above.
Results may differ from the reference program's by a relative error of at most 0.015.
The reference program's roundings to bfloat16 on the way count: a program that leaves them out, or rounds other values in their place, can miss the bound.
Values may be sent and summed in bfloat16 or wider, within the bound.
A program may use at most 256 MiB of HBM per device.

```python
import math
import jax
import jax.numpy as jnp
from jax import lax

D = 1152
H = 16
HD = 72
FF = 4608
GW = 288
UNIT = 64
SEQ = 1408
CROPS = 11
BATCH = 8


def crop_units(key):
    picked_units = jax.random.randint(key, (BATCH, CROPS), 2, 9)
    remain = jnp.full((BATCH,), 22, jnp.int32)
    first_row = jnp.arange(BATCH, dtype=jnp.int32) == 0
    unit_list = []
    for slot_index in range(CROPS):
        chosen = picked_units[:, slot_index]
        if slot_index == 0:
            chosen = jnp.where(first_row, 8, chosen)
        chosen = jnp.minimum(chosen, remain)
        leftover = remain - chosen
        chosen = jnp.where((leftover > 0) & (leftover < 2), jnp.where(remain <= 8, remain, remain - 2), chosen)
        unit_list.append(chosen)
        remain = remain - chosen
    return jnp.stack(unit_list, axis=1).astype(jnp.int32)


def draw_lengths(key, part):
    units_all = crop_units(key)
    return (units_all * UNIT).astype(jnp.int32)


def draw_pads(key, part):
    units_all = crop_units(key)
    key = jax.random.fold_in(key, 2)
    most_pads = units_all * UNIT // 4
    drawn = jax.random.randint(key, (BATCH, CROPS), 0, most_pads + 1)
    first_slot = (jnp.arange(BATCH, dtype=jnp.int32)[:, None] == 0) & (jnp.arange(CROPS, dtype=jnp.int32)[None, :] == 0)
    return jnp.where(first_slot, most_pads, drawn).astype(jnp.int32)


def touch_ends(result, key, smallest, largest):
    shape = result.shape
    place = [jax.random.randint(jax.random.fold_in(key, axis), (), 0, shape[axis]) for axis in range(len(shape))]
    result = result.at[tuple(place)].set(smallest)
    longest = shape.index(max(shape))
    place[longest] = (place[longest] + 1) % shape[longest]
    return result.at[tuple(place)].set(largest)


def block_levels(stream_key, shape, shards, smallest, largest):
    loudness = 1.0
    for axis_at, parts in shards:
        steps = jax.random.uniform(jax.random.fold_in(jax.random.fold_in(stream_key, 6), axis_at), (parts,), jnp.float32, smallest / len(shards), largest / len(shards))
        loudness = loudness * jnp.repeat(jnp.exp(steps), shape[axis_at] // parts).reshape((-1,) + (1,) * (len(shape) - 1 - axis_at))
    return loudness


def bell_draw(stream_key, shape, scale, reach, pieces=(), held_as=jnp.bfloat16):
    factor_of = block_levels(stream_key, shape, pieces, -0.22, 0.18) if pieces else 1.0
    values = jax.random.normal(stream_key, shape, jnp.float32) * scale * factor_of
    return jnp.minimum(jnp.maximum(values, -reach), reach).astype(held_as)


def setup_inputs(seed: int = 0) -> dict:
    keys = jax.random.split(jax.random.key(seed), 21)
    return {
        "tokens": bell_draw(keys[0], (SEQ, BATCH, D), 1.0, 6.0, ((0, 8), (1, 4))),
        "cond": bell_draw(keys[1], (BATCH, CROPS, D), 1.0, 6.0, ((0, 4),)),
        "lengths": draw_lengths(jax.random.fold_in(keys[20], 71), 0),
        "pads": draw_pads(jax.random.fold_in(keys[20], 71), 0),
        "timesteps": touch_ends(jax.random.randint(keys[4], (BATCH, CROPS), 0, 1000), jax.random.fold_in(keys[4], 1), 0, 999).astype(jnp.int32),
        "head_mask": touch_ends((jax.random.randint(keys[5], (BATCH, CROPS, H), 0, 4) < 3).astype(jnp.int32), jax.random.fold_in(keys[5], 1), 0, 1),
        "group_mask": touch_ends((jax.random.randint(keys[6], (BATCH, CROPS, H), 0, 4) < 3).astype(jnp.int32), jax.random.fold_in(keys[6], 1), 0, 1),
        "keep": touch_ends((jax.random.randint(keys[7], (SEQ, BATCH), 0, 3) < 2).astype(jnp.int32), jax.random.fold_in(keys[7], 1), 0, 1),
        "ada_w": bell_draw(keys[8], (D, 6 * D), D ** -0.5, 0.1875, ((1, 8),)),
        "ada_b": bell_draw(keys[9], (6 * D,), 0.3, 1.5, ((0, 8),)),
        "w_qkv": bell_draw(keys[10], (D, 3 * D), D ** -0.5, 0.1875, ((1, 8),)),
        "b_qv": bell_draw(keys[11], (2 * D,), 0.3, 1.5, ((0, 8),)),
        "w_out": bell_draw(keys[12], (D, D), (D // 64) ** -0.5, 1.5, ((0, 8),)),
        "b_out": bell_draw(keys[13], (D,), 0.3, 1.5),
        "w_up": bell_draw(keys[14], (D, FF), D ** -0.5, 0.1875, ((1, 8),)),
        "b_up": bell_draw(keys[15], (FF,), 0.3, 1.5, ((0, 8),)),
        "w_down": bell_draw(keys[16], (FF, D), (FF // 4) ** -0.5, 0.1875, ((0, 8),)),
        "b_down": bell_draw(keys[17], (D,), 0.3, 1.5),
        "w_route": bell_draw(keys[18], (D,), D ** -0.5, 0.1875),
        "grad_out": bell_draw(keys[19], (SEQ, BATCH, D), 1.0, 6.0, ((0, 8), (1, 4))),
    }


@jax.custom_vjp
def low(v):
    return lax.optimization_barrier(v.astype(jnp.bfloat16)).astype(jnp.float32)

@jax.custom_vjp
def low_back(v):
    return v

def low_keep(v):
    return (low(v), None)

def low_pass(kept, grad):
    return (grad,)

def back_keep(v):
    return (v, None)

def back_low(kept, grad):
    return (low(grad),)
low.defvjp(low_keep, low_pass)
low_back.defvjp(back_keep, back_low)
EPSILON = 1e-06
MASKED_SCORE = -1000000000.0

def time_embed(timesteps):
    halves = D // 2
    frequency = jnp.exp(-math.log(10000.0) * jnp.arange(halves, dtype=jnp.float32) / halves)
    angles = timesteps.astype(jnp.float32)[..., None] * frequency
    return jnp.concatenate([jnp.cos(angles), jnp.sin(angles)], axis=-1)

def gelu_tanh(values):
    return 0.5 * values * (1.0 + jnp.tanh(0.7978845608028654 * (values + 0.044715 * values * values * values)))

def layer_norm(values):
    average = lax.optimization_barrier(jnp.mean(values, axis=-1, keepdims=True))
    centred = values - average
    inverse_dev = lax.rsqrt(lax.optimization_barrier(jnp.mean(centred * centred, axis=-1, keepdims=True)) + EPSILON)
    return centred * inverse_dev

def matmul(left, right):
    return jnp.dot(left, right, precision=lax.Precision.HIGHEST)

def attend(queries, key_rows, values, item_ids, key_live):
    highest = lax.Precision.HIGHEST
    raw = low_back(jnp.einsum('shd,thd->hst', queries, key_rows, precision=highest))
    allowed = (item_ids[:, None] == item_ids[None, :]) & key_live[None, :]
    scores = jnp.where(allowed[None], raw * HD ** (-0.5), MASKED_SCORE)
    row_top = lax.optimization_barrier(jnp.max(scores, axis=-1, keepdims=True))
    log_total = row_top + jnp.log(lax.optimization_barrier(jnp.sum(jnp.exp(scores - row_top), axis=-1, keepdims=True)))
    probability = jnp.exp(scores - log_total)
    return jnp.einsum('hst,thd->shd', low(probability), values, precision=highest)

def layer_row(params, row_inputs):
    ada_w, ada_b, w_qkv, b_qv, w_out, b_out, w_up, b_up, w_down, b_down, w_route = params
    tokens, cond, embedding, item_ids, valid, head_tok, group_tok, keep_tok = row_inputs
    cond_all = cond + embedding
    activ = cond_all * lax.logistic(cond_all)
    modulation = low_back(matmul(low(activ), ada_w) + ada_b)
    token_mod = modulation[item_ids]
    shift_one, scale_one, gate_one, shift_two, scale_two, gate_two = jnp.split(token_mod, 6, axis=-1)
    hidden_one = low(layer_norm(tokens) * (1.0 + scale_one) + shift_one)
    bias_pairs = b_qv.reshape(H, 2, HD)
    bias_full = jnp.stack([bias_pairs[:, 0], jnp.zeros((H, HD), jnp.float32), bias_pairs[:, 1]], axis=1).reshape(3 * D)
    triple = low(low_back(matmul(hidden_one, w_qkv) + bias_full)).reshape(SEQ, H, 3, HD)
    attended = attend(triple[:, :, 0], triple[:, :, 1], triple[:, :, 2], item_ids, valid > 0.5)
    attended = attended * head_tok[:, :, None] * valid[:, None, None]
    attended = low(low_back(attended.reshape(SEQ, D)))
    projected = low_back(matmul(attended, w_out))
    mixed = tokens + gate_one * (projected + b_out)
    hidden_two = layer_norm(mixed) * (1.0 + scale_two) + shift_two
    route = lax.logistic(matmul(hidden_two, w_route))
    upper = low_back(matmul(low(hidden_two), w_up) + b_up)
    active = low((gelu_tanh(upper).reshape(SEQ, H, GW) * group_tok[:, :, None]).reshape(SEQ, FF))
    lowered = low_back(matmul(active, w_down))
    return mixed + gate_two * (keep_tok * route)[:, None] * (lowered + b_down)

def reference(tokens, cond, lengths, pads, timesteps, head_mask, group_mask, keep, ada_w, ada_b, w_qkv, b_qv, w_out, b_out, w_up, b_up, w_down, b_down, w_route, grad_out):
    crop_ends = jnp.cumsum(lengths, axis=1)
    starts = crop_ends - lengths
    places = jnp.arange(SEQ, dtype=jnp.int32)
    inside = (places[None, :, None] >= starts[:, None, :]) & (places[None, :, None] < crop_ends[:, None, :])
    live_part = places[None, :, None] < (crop_ends - pads)[:, None, :]
    item_ids = lax.optimization_barrier(jnp.sum(inside.astype(jnp.int32) * jnp.arange(CROPS, dtype=jnp.int32), axis=2)).astype(jnp.int32)
    valid = lax.optimization_barrier(jnp.sum((inside & live_part).astype(jnp.float32), axis=2))
    batch_index = jnp.arange(BATCH, dtype=jnp.int32)[:, None]
    head_tok = head_mask[batch_index, item_ids].astype(jnp.float32)
    group_tok = group_mask[batch_index, item_ids].astype(jnp.float32)
    keep_tok = jnp.transpose(keep).astype(jnp.float32)
    embedding = time_embed(timesteps)
    params = (ada_w.astype(jnp.float32), ada_b.astype(jnp.float32), w_qkv.astype(jnp.float32), b_qv.astype(jnp.float32), w_out.astype(jnp.float32), b_out.astype(jnp.float32), w_up.astype(jnp.float32), b_up.astype(jnp.float32), w_down.astype(jnp.float32), b_down.astype(jnp.float32), w_route.astype(jnp.float32))
    row_tokens = jnp.transpose(tokens, (1, 0, 2)).astype(jnp.float32)
    row_cond = cond.astype(jnp.float32)
    checked = jax.checkpoint(layer_row)

    def whole(weights, token_rows, cond_rows):
        rows_in = (token_rows, cond_rows, embedding, item_ids, valid, head_tok, group_tok, keep_tok)
        return lax.map(lambda row_data: checked(weights, row_data), rows_in)
    out_rows, pullback = jax.vjp(whole, params, row_tokens, row_cond)
    grad_params, grad_rows, grad_cond = pullback(jnp.transpose(grad_out, (1, 0, 2)).astype(jnp.float32))
    g_ada_w, g_ada_b, g_w_qkv, g_b_qv, g_w_out, g_b_out, g_w_up, g_b_up, g_w_down, g_b_down, g_w_route = grad_params
    final = jnp.transpose(out_rows, (1, 0, 2)).astype(jnp.bfloat16)
    grad_tokens = jnp.transpose(grad_rows, (1, 0, 2))
    return (final, grad_tokens, grad_cond, g_ada_w, g_ada_b, g_w_qkv, g_b_qv, g_w_out, g_b_out, g_w_up, g_b_up, g_w_down, g_b_down, g_w_route)
```

```python
import math

import jax
import jax.numpy as jnp
import numpy as np
from jax import lax
from jax.experimental import pallas as pl
from jax.experimental.pallas import tpu as pltpu
from jax.sharding import Mesh
from jax.sharding import PartitionSpec as P

D = 1152
H = 16
HD = 72
GW = 288
SEQ = 1408
CROPS = 11
UNIT = 64
LANES = 128
EPSILON = 1e-06
MASKED_SCORE = -1000000000.0
MESH = pl.DeviceIdType.MESH
SWAP = [(0, 1), (1, 0)]
F32 = jnp.float32
BF16 = jnp.bfloat16
SCALE = HD ** (-0.5)


def time_embed(timesteps):
    halves = D // 2
    frequency = jnp.exp(-math.log(10000.0) * jnp.arange(halves, dtype=jnp.float32) / halves)
    angles = timesteps.astype(jnp.float32)[..., None] * frequency
    return jnp.concatenate([jnp.cos(angles), jnp.sin(angles)], axis=-1)


def gelu_tanh(values):
    return (
        0.5
        * values
        * (1.0 + jnp.tanh(0.7978845608028654 * (values + 0.044715 * values * values * values)))
    )


def norm_rows(values):
    average = jnp.mean(values, axis=-1, keepdims=True)
    centred = values - average
    inverse_dev = lax.rsqrt(jnp.mean(centred * centred, axis=-1, keepdims=True) + EPSILON)
    return (centred * inverse_dev, inverse_dev)


def norm_back(grad_normed, normed, inverse_dev):
    first_mean = jnp.mean(grad_normed, axis=-1, keepdims=True)
    second_mean = jnp.mean(grad_normed * normed, axis=-1, keepdims=True)
    return inverse_dev * (grad_normed - first_mean - normed * second_mean)


def crop_layout(lengths, pads, offset, amount):
    crop_ends = jnp.cumsum(lengths, axis=1)
    starts = crop_ends - lengths
    places = offset + jnp.arange(amount, dtype=jnp.int32)
    inside = (places[:, None, None] >= starts[None]) & (places[:, None, None] < crop_ends[None])
    live_part = places[:, None, None] < (crop_ends - pads)[None]
    one_hot = inside.astype(jnp.float32)
    item_ids = jnp.sum(
        inside.astype(jnp.int32) * jnp.arange(lengths.shape[1], dtype=jnp.int32), axis=2
    )
    valid = jnp.sum((inside & live_part).astype(jnp.float32), axis=2)
    return (one_hot, item_ids, valid)


def masked_scores(queries, key_rows, item_row, key_live, score_scale):
    raw = jnp.einsum("shd,thd->hst", queries, key_rows, preferred_element_type=jnp.float32)
    allowed = (item_row[:, None] == item_row[None, :]) & key_live[None, :]
    return jnp.where(allowed[None], raw * score_scale, MASKED_SCORE)


def attend_row(triple_row, item_row, key_live, score_scale):
    queries = triple_row[:, :, 0]
    key_rows = triple_row[:, :, 1]
    values = triple_row[:, :, 2]
    scores = masked_scores(queries, key_rows, item_row, key_live, score_scale)
    row_top = jnp.max(scores, axis=-1, keepdims=True)
    log_total = row_top + jnp.log(jnp.sum(jnp.exp(scores - row_top), axis=-1, keepdims=True))
    probability = jnp.exp(scores - log_total).astype(jnp.bfloat16)
    attended = jnp.einsum("hst,thd->shd", probability, values, preferred_element_type=jnp.float32)
    return (attended, log_total)


def attend_back(triple_row, grad_row, total_row, item_row, key_live, score_scale):
    queries = triple_row[:, :, 0]
    key_rows = triple_row[:, :, 1]
    values = triple_row[:, :, 2]
    scores = masked_scores(queries, key_rows, item_row, key_live, score_scale)
    probability = jnp.exp(scores - total_row)
    grad_prob = jnp.einsum("shd,thd->hst", grad_row, values, preferred_element_type=jnp.float32)
    grad_values = jnp.einsum(
        "hst,shd->thd",
        probability.astype(jnp.bfloat16),
        grad_row,
        preferred_element_type=jnp.float32,
    )
    inner = jnp.sum(probability * grad_prob, axis=-1, keepdims=True)
    grad_raw = (probability * (grad_prob - inner) * score_scale).astype(jnp.bfloat16)
    grad_queries = jnp.einsum(
        "hst,thd->shd", grad_raw, key_rows, preferred_element_type=jnp.float32
    )
    grad_keys = jnp.einsum("hst,shd->thd", grad_raw, queries, preferred_element_type=jnp.float32)
    return jnp.stack([grad_queries, grad_keys, grad_values], axis=2).astype(jnp.bfloat16)


def project_rows(source, weight):
    return jnp.einsum("sbk,kd->sbd", source, weight, preferred_element_type=jnp.float32)


def back_rows(source, weight):
    return jnp.einsum("sbk,dk->sbd", source, weight, preferred_element_type=jnp.float32)


def per_device(
    tokens,
    cond,
    lengths,
    pads,
    timesteps,
    head_mask,
    group_mask,
    keep,
    ada_w,
    ada_b,
    w_qkv,
    b_qv,
    w_out,
    b_out,
    w_up,
    b_up,
    w_down,
    b_down,
    w_route,
    grad_out,
):
    highest = lax.Precision.HIGHEST
    groups = lax.axis_size("heads")
    head_rank = lax.axis_index("heads")
    shard_len = tokens.shape[0]
    batch_local = tokens.shape[1]
    local_heads = H // groups
    score_scale = HD ** (-0.5)
    local_hot, local_items, local_valid = crop_layout(
        lengths, pads, head_rank * shard_len, shard_len
    )
    full_hot, full_items, full_valid = crop_layout(lengths, pads, 0, SEQ)
    cond_all = cond.astype(jnp.float32) + time_embed(timesteps)
    sigmoid_cond = lax.logistic(cond_all)
    silu_low = (cond_all * sigmoid_cond).astype(jnp.bfloat16)
    modulation_part = jnp.einsum(
        "bcd,dm->bcm", silu_low, ada_w, preferred_element_type=jnp.float32
    ) + ada_b.astype(jnp.float32)
    modulation = lax.all_gather(modulation_part, "heads", axis=2, tiled=True)
    token_mod = jnp.einsum("sbc,bcm->sbm", local_hot, modulation, precision=highest)
    shift_one, scale_one, gate_one, shift_two, scale_two, gate_two = jnp.split(
        token_mod, 6, axis=-1
    )
    token_values = tokens.astype(jnp.float32)
    normed_one, inverse_one = norm_rows(token_values)
    hidden_one = (normed_one * (1.0 + scale_one) + shift_one).astype(jnp.bfloat16)
    hidden_all = lax.all_gather(hidden_one, "heads", axis=0, tiled=True)
    bias_pairs = b_qv.astype(jnp.float32).reshape(local_heads, 2, HD)
    bias_triple = jnp.stack(
        [bias_pairs[:, 0], jnp.zeros_like(bias_pairs[:, 0]), bias_pairs[:, 1]], axis=1
    ).reshape(-1)
    triple_all = (
        jnp.einsum("sbd,dm->sbm", hidden_all, w_qkv, preferred_element_type=jnp.float32)
        + bias_triple
    ).astype(jnp.bfloat16)
    triple_rows = jnp.moveaxis(triple_all.reshape(SEQ, batch_local, local_heads, 3, HD), 1, 0)
    item_rows = jnp.transpose(full_items)
    live_rows = jnp.transpose(full_valid > 0.5)
    attended, totals = lax.map(
        lambda packed: attend_row(packed[0], packed[1], packed[2], score_scale),
        (triple_rows, item_rows, live_rows),
    )
    head_table = lax.dynamic_slice_in_dim(
        head_mask, head_rank * local_heads, local_heads, 2
    ).astype(jnp.float32)
    head_full = jnp.einsum("sbc,bch->sbh", full_hot, head_table, precision=highest)
    out_mask = head_full * full_valid[..., None]
    attn_low = (
        (jnp.moveaxis(attended, 0, 1) * out_mask[..., None])
        .reshape(SEQ, batch_local, local_heads * HD)
        .astype(jnp.bfloat16)
    )
    projected = lax.psum_scatter(
        project_rows(attn_low, w_out), "heads", scatter_dimension=0, tiled=True
    )
    b_out_values = b_out.astype(jnp.float32)
    mixed = token_values + gate_one * (projected + b_out_values)
    normed_two, inverse_two = norm_rows(mixed)
    hidden_two = normed_two * (1.0 + scale_two) + shift_two
    hidden_two_low = hidden_two.astype(jnp.bfloat16)
    route_values = w_route.astype(jnp.float32)
    route = lax.logistic(jnp.einsum("sbd,d->sb", hidden_two, route_values, precision=highest))
    keep_values = keep.astype(jnp.float32)
    route_keep = keep_values * route
    group_table = lax.dynamic_slice_in_dim(
        group_mask, head_rank * local_heads, local_heads, 2
    ).astype(jnp.float32)
    hidden_two_all = lax.all_gather(hidden_two_low, "heads", axis=0, tiled=True)
    group_tok = jnp.einsum("sbc,bch->sbh", full_hot, group_table, precision=highest)
    upper = jnp.einsum(
        "sbd,dk->sbk", hidden_two_all, w_up, preferred_element_type=jnp.float32
    ) + b_up.astype(jnp.float32)
    active, gelu_back = jax.vjp(gelu_tanh, upper)
    group_wide = jnp.repeat(group_tok, GW, axis=-1)
    active_low = (active * group_wide).astype(jnp.bfloat16)
    lowered = lax.psum_scatter(
        project_rows(active_low, w_down), "heads", scatter_dimension=0, tiled=True
    )
    branch = lowered + b_down.astype(jnp.float32)
    final = mixed + gate_two * route_keep[..., None] * branch
    grad_final = grad_out.astype(jnp.float32)
    grad_branch = grad_final * gate_two * route_keep[..., None]
    grad_gate_two = grad_final * route_keep[..., None] * branch
    grad_route = jnp.sum(grad_final * gate_two * branch, axis=-1) * keep_values
    grad_logit = grad_route * route * (1.0 - route)
    part_route = jnp.einsum("sb,sbd->d", grad_logit, hidden_two, precision=highest)
    part_b_down = jnp.sum(grad_branch, axis=(0, 1))
    grad_low = grad_branch.astype(jnp.bfloat16)
    grad_all = lax.all_gather(grad_low, "heads", axis=0, tiled=True)
    grad_active = jnp.einsum("sbd,kd->sbk", grad_all, w_down, preferred_element_type=jnp.float32)
    (grad_upper,) = gelu_back(grad_active * group_wide)
    upper_low = grad_upper.astype(jnp.bfloat16)
    grad_w_up = jnp.einsum(
        "sbd,sbk->dk", hidden_two_all, upper_low, preferred_element_type=jnp.float32
    )
    grad_b_up = jnp.sum(upper_low, axis=(0, 1), dtype=jnp.float32)
    grad_w_down = jnp.einsum(
        "sbk,sbd->kd", active_low, grad_all, preferred_element_type=jnp.float32
    )
    grad_hidden_two = lax.psum_scatter(
        back_rows(upper_low, w_up), "heads", scatter_dimension=0, tiled=True
    )
    grad_hidden_two = grad_hidden_two + grad_logit[..., None] * route_values
    grad_scale_two = grad_hidden_two * normed_two
    grad_mixed = grad_final + norm_back(
        grad_hidden_two * (1.0 + scale_two), normed_two, inverse_two
    )
    grad_gate_one = grad_mixed * (projected + b_out_values)
    grad_projected = grad_mixed * gate_one
    part_b_out = jnp.sum(grad_projected, axis=(0, 1))
    projected_low = grad_projected.astype(jnp.bfloat16)
    grad_proj_all = lax.all_gather(projected_low, "heads", axis=0, tiled=True)
    grad_attn = jnp.einsum(
        "sbd,kd->sbk", grad_proj_all, w_out, preferred_element_type=jnp.float32
    ).astype(jnp.bfloat16)
    grad_w_out = jnp.einsum(
        "sbk,sbd->kd", attn_low, grad_proj_all, preferred_element_type=jnp.float32
    )
    grad_masked = grad_attn.reshape(SEQ, batch_local, local_heads, HD) * out_mask[..., None].astype(
        jnp.bfloat16
    )
    grad_rows = jnp.moveaxis(grad_masked, 1, 0)
    grad_triple_rows = lax.map(
        lambda packed: attend_back(
            packed[0], packed[1], packed[2], packed[3], packed[4], score_scale
        ),
        (triple_rows, grad_rows, totals, item_rows, live_rows),
    )
    grad_triple = jnp.moveaxis(grad_triple_rows, 0, 1).reshape(
        SEQ, batch_local, local_heads * 3 * HD
    )
    grad_w_qkv = jnp.einsum(
        "sbd,sbm->dm", hidden_all, grad_triple, preferred_element_type=jnp.float32
    )
    bias_sums = jnp.sum(grad_triple, axis=(0, 1), dtype=jnp.float32).reshape(local_heads, 3, HD)
    grad_b_qv = jnp.stack([bias_sums[:, 0], bias_sums[:, 2]], axis=1).reshape(-1)
    grad_hidden_one = lax.psum_scatter(
        back_rows(grad_triple, w_qkv), "heads", scatter_dimension=0, tiled=True
    )
    grad_tokens = grad_mixed + norm_back(
        grad_hidden_one * (1.0 + scale_one), normed_one, inverse_one
    )
    grad_token_mod = jnp.concatenate(
        [
            grad_hidden_one,
            grad_hidden_one * normed_one,
            grad_gate_one,
            grad_hidden_two,
            grad_scale_two,
            grad_gate_two,
        ],
        axis=-1,
    )
    part_mod = jnp.einsum("sbc,sbm->bcm", local_hot, grad_token_mod, precision=highest)
    grad_mod, share_b_out, share_b_down, share_route = (
        lax.psum_scatter(part_mod, "heads", scatter_dimension=2, tiled=True),
        lax.psum_scatter(part_b_out, "heads", scatter_dimension=0, tiled=True),
        lax.psum_scatter(part_b_down, "heads", scatter_dimension=0, tiled=True),
        lax.psum_scatter(part_route, "heads", scatter_dimension=0, tiled=True),
    )
    mod_low = grad_mod.astype(jnp.bfloat16)
    grad_ada_w = jnp.einsum("bcd,bcm->dm", silu_low, mod_low, preferred_element_type=jnp.float32)
    grad_ada_b = jnp.sum(mod_low, axis=(0, 1), dtype=jnp.float32)
    part_activ = jnp.einsum("bcm,dm->bcd", mod_low, ada_w, preferred_element_type=jnp.float32)
    grad_activ = lax.psum(part_activ.astype(jnp.bfloat16), "heads").astype(jnp.float32)
    grad_cond = grad_activ * sigmoid_cond * (1.0 + cond_all * (1.0 - sigmoid_cond))
    summed = (
        lax.psum(grad_ada_w.astype(jnp.bfloat16), "rows").astype(jnp.float32),
        lax.psum(grad_ada_b.astype(jnp.bfloat16), "rows").astype(jnp.float32),
        lax.psum(grad_w_qkv.astype(jnp.bfloat16), "rows").astype(jnp.float32),
        lax.psum(grad_b_qv.astype(jnp.bfloat16), "rows").astype(jnp.float32),
        lax.psum(grad_w_out.astype(jnp.bfloat16), "rows").astype(jnp.float32),
        lax.psum(share_b_out.astype(jnp.bfloat16), "rows").astype(jnp.float32),
        lax.psum(grad_w_up.astype(jnp.bfloat16), "rows").astype(jnp.float32),
        lax.psum(grad_b_up.astype(jnp.bfloat16), "rows").astype(jnp.float32),
        lax.psum(grad_w_down.astype(jnp.bfloat16), "rows").astype(jnp.float32),
        lax.psum(share_b_down.astype(jnp.bfloat16), "rows").astype(jnp.float32),
        lax.psum(share_route.astype(jnp.bfloat16), "rows").astype(jnp.float32),
    )
    return (
        final.astype(jnp.bfloat16),
        grad_tokens,
        grad_cond,
        summed[0],
        summed[1],
        summed[2],
        summed[3],
        summed[4],
        summed[5],
        summed[6],
        summed[7],
        summed[8],
        summed[9],
        summed[10],
    )


BLK = 176
NH = 4
HALF = SEQ // 2


def block_place(scal, dq, dc, slot):
    q = lax.rem(scal[0] + dq, 2)
    c = lax.rem(scal[1] + dc, 2)
    return pl.multiple_of(slot * HALF + q * (2 * BLK) + c * BLK, 16)


def load_blocks(scal, refs, buf, sem):
    copies = []
    for dq in range(2):
        for dc in range(2):
            for slot in range(2):
                copies.append(
                    pltpu.make_async_copy(
                        refs[dq].at[dc, slot],
                        buf.at[pl.ds(block_place(scal, dq, dc, slot), BLK)],
                        sem.at[dq * 4 + dc * 2 + slot],
                    )
                )
    for copy in copies:
        copy.start()
    return copies


def store_blocks(scal, buf, refs, sem):
    copies = []
    for dq in range(2):
        for dc in range(2):
            for slot in range(2):
                copies.append(
                    pltpu.make_async_copy(
                        buf.at[pl.ds(block_place(scal, dq, dc, slot), BLK)],
                        refs[dq].at[dc, slot],
                        sem.at[dq * 4 + dc * 2 + slot],
                    )
                )
    for copy in copies:
        copy.start()
    for copy in copies:
        copy.wait()


def each_crop(scal, body):
    def step(item, carry):
        units = scal[2 + CROPS + item]
        for count in range(2, 9):

            @pl.when(units == count)
            def _():
                body(item, pl.multiple_of(scal[2 + item], UNIT), count * UNIT)

        return carry

    lax.fori_loop(0, CROPS, step, 0)


def nt(a, b):
    return lax.dot_general(a, b, (((1,), (1,)), ((), ())), preferred_element_type=F32)


def tn(a, b):
    return lax.dot_general(a, b, (((0,), (0,)), ((), ())), preferred_element_type=F32)


def attn_fwd_kernel(scal, t0, t1, pack, o0, o1, lse, buf, obuf, sem):
    for copy in load_blocks(scal, (t0, t1), buf, sem):
        copy.wait()
    lane = lax.broadcasted_iota(jnp.int32, (1, LANES), 1)

    def body(item, start, size):
        live = scal[2 + 2 * CROPS + item]
        keys_live = lax.broadcasted_iota(jnp.int32, (1, size), 1) < live
        rows_live = (lax.broadcasted_iota(jnp.int32, (size, 1), 0) < live).astype(F32)
        window = pl.ds(start, size)
        packed = jnp.zeros((size, NH * HD), F32)
        totals = jnp.zeros((size, LANES), F32)
        for head in range(NH):
            at = head * 3 * LANES
            queries = buf[window, at : at + LANES]
            keys = buf[window, at + LANES : at + 2 * LANES]
            values = buf[window, at + 2 * LANES : at + 3 * LANES]
            scores = jnp.where(keys_live, nt(queries, keys) * SCALE, MASKED_SCORE)
            top = jnp.max(scores, axis=1, keepdims=True)
            expo = jnp.exp(scores - top)
            total = jnp.sum(expo, axis=1, keepdims=True)
            prob = (expo * (1.0 / total)).astype(BF16)
            mixed = jnp.dot(prob, values, preferred_element_type=F32)
            mask = scal[2 + 3 * CROPS + item * NH + head].astype(F32)
            mixed = (mixed * (rows_live * mask)).astype(BF16)
            packed += jnp.dot(
                mixed, pack[head * LANES : (head + 1) * LANES, :], preferred_element_type=F32
            )
            totals = jnp.where(lane == head, top + jnp.log(total), totals)
        obuf[window, :] = packed.astype(BF16)
        lse[window, :] = totals

    each_crop(scal, body)
    store_blocks(scal, obuf, (o0, o1), sem)


def attn_bwd_kernel(scal, t0, t1, g0, g1, lse, pack, d0, d1, buf, gbuf, dbuf, sem, gsem):
    first = load_blocks(scal, (t0, t1), buf, sem)
    second = load_blocks(scal, (g0, g1), gbuf, gsem)
    for copy in first + second:
        copy.wait()

    def body(item, start, size):
        live = scal[2 + 2 * CROPS + item]
        keys_live = lax.broadcasted_iota(jnp.int32, (1, size), 1) < live
        rows_live = lax.broadcasted_iota(jnp.int32, (size, 1), 0) < live
        window = pl.ds(start, size)
        grads = gbuf[window, :]
        grads = jnp.where(rows_live, grads.astype(F32), 0.0).astype(BF16)
        for head in range(NH):
            at = head * 3 * LANES
            queries = buf[window, at : at + LANES]
            keys = buf[window, at + LANES : at + 2 * LANES]
            values = buf[window, at + 2 * LANES : at + 3 * LANES]
            mask = scal[2 + 3 * CROPS + item * NH + head].astype(F32)
            grad = (nt(grads, pack[head * LANES : (head + 1) * LANES, :]) * mask).astype(BF16)
            scores = jnp.where(keys_live, nt(queries, keys) * SCALE, MASKED_SCORE)
            prob = jnp.exp(scores - lse[window, head : head + 1])
            grad_prob = nt(grad, values)
            grad_values = tn(prob.astype(BF16), grad)
            inner = jnp.sum(prob * grad_prob, axis=1, keepdims=True)
            grad_raw = (prob * (grad_prob - inner) * SCALE).astype(BF16)
            dbuf[window, at : at + LANES] = jnp.dot(
                grad_raw, keys, preferred_element_type=F32
            ).astype(BF16)
            dbuf[window, at + LANES : at + 2 * LANES] = tn(grad_raw, queries).astype(BF16)
            dbuf[window, at + 2 * LANES : at + 3 * LANES] = grad_values.astype(BF16)

    each_crop(scal, body)
    store_blocks(scal, dbuf, (d0, d1), sem)


WIDE = NH * 3 * LANES
SMEM_SPEC = pl.BlockSpec(memory_space=pltpu.SMEM)
VMEM_SPEC = pl.BlockSpec(memory_space=pltpu.VMEM)
ANY_SPEC = pl.BlockSpec(memory_space=pl.ANY)


def attn_fwd(scal, t0, t1, pack):
    return pl.pallas_call(
        attn_fwd_kernel,
        out_shape=(
            jax.ShapeDtypeStruct((2, 2, BLK, NH * HD), BF16),
            jax.ShapeDtypeStruct((2, 2, BLK, NH * HD), BF16),
            jax.ShapeDtypeStruct((SEQ, LANES), F32),
        ),
        in_specs=[SMEM_SPEC, ANY_SPEC, ANY_SPEC, VMEM_SPEC],
        out_specs=(ANY_SPEC, ANY_SPEC, VMEM_SPEC),
        scratch_shapes=[
            pltpu.VMEM((SEQ, WIDE), BF16),
            pltpu.VMEM((SEQ, NH * HD), BF16),
            pltpu.SemaphoreType.DMA((8,)),
        ],
        compiler_params=pltpu.CompilerParams(vmem_limit_bytes=48 * 2**20),
        cost_estimate=pl.CostEstimate(
            flops=4 * 10**9, bytes_accessed=6 * 10**6, transcendentals=4 * 10**6
        ),
        name="attn_fwd",
    )(scal, t0, t1, pack)


def attn_bwd(scal, t0, t1, g0, g1, lse, pack):
    return pl.pallas_call(
        attn_bwd_kernel,
        out_shape=(
            jax.ShapeDtypeStruct((2, 2, BLK, WIDE), BF16),
            jax.ShapeDtypeStruct((2, 2, BLK, WIDE), BF16),
        ),
        in_specs=[SMEM_SPEC] + [ANY_SPEC] * 4 + [VMEM_SPEC] * 2,
        out_specs=(ANY_SPEC, ANY_SPEC),
        scratch_shapes=[
            pltpu.VMEM((SEQ, WIDE), BF16),
            pltpu.VMEM((SEQ, NH * HD), BF16),
            pltpu.VMEM((SEQ, WIDE), BF16),
            pltpu.SemaphoreType.DMA((8,)),
            pltpu.SemaphoreType.DMA((8,)),
        ],
        compiler_params=pltpu.CompilerParams(vmem_limit_bytes=48 * 2**20),
        cost_estimate=pl.CostEstimate(
            flops=12 * 10**9, bytes_accessed=12 * 10**6, transcendentals=4 * 10**6
        ),
        name="attn_bwd",
    )(scal, t0, t1, g0, g1, lse, pack)


def line_kernel(pick, src, out, send_sem, recv_sem, loc_sem):
    p, q, c = lax.axis_index("p"), lax.axis_index("q"), lax.axis_index("c")
    me = p * 4 + q * 2 + c
    peers = []
    for k in range(1, 8):
        pp, qq, cc = lax.rem(p + k // 4, 2), lax.rem(q + (k // 2) % 2, 2), lax.rem(c + k % 2, 2)
        peers.append((pp, qq, cc))
    barrier = pltpu.get_barrier_semaphore()
    for pp, qq, cc in peers:
        pl.semaphore_signal(
            barrier, inc=1, device_id={"p": pp, "q": qq, "c": cc}, device_id_type=MESH
        )
    pl.semaphore_wait(barrier, 7)

    def source(pp, qq, cc):
        if pick == "row":
            return src.at[pp]
        if pick == "all":
            return src
        return src.at[pp * 4 + qq * 2 + cc]

    copies = []
    for k, (pp, qq, cc) in enumerate(peers):
        copy = pltpu.make_async_remote_copy(
            src_ref=source(pp, qq, cc),
            dst_ref=out.at[me],
            send_sem=send_sem.at[k],
            recv_sem=recv_sem.at[k],
            device_id={"p": pp, "q": qq, "c": cc},
            device_id_type=MESH,
        )
        copy.start()
        copies.append(copy)
    own = pltpu.make_async_copy(source(p, q, c), out.at[me], loc_sem)
    own.start()
    own.wait()
    for copy in copies:
        copy.wait()


def line_exchange(src, pick, collective_id, name):
    shape = src.shape if pick == "all" else src.shape[1:]
    return pl.pallas_call(
        lambda *refs: line_kernel(pick, *refs),
        out_shape=jax.ShapeDtypeStruct((8,) + shape, src.dtype),
        in_specs=[VMEM_SPEC],
        out_specs=VMEM_SPEC,
        scratch_shapes=[
            pltpu.SemaphoreType.DMA((7,)),
            pltpu.SemaphoreType.DMA((7,)),
            pltpu.SemaphoreType.DMA,
        ],
        compiler_params=pltpu.CompilerParams(collective_id=collective_id, has_side_effects=True),
        name=name,
    )(src)


def plane_kernel(src, out, send_sem, recv_sem, loc_sem):
    y, x = lax.axis_index("y"), lax.axis_index("x")
    me = y * 2 + x
    peers = [(lax.rem(y + k // 2, 2), lax.rem(x + k % 2, 2)) for k in range(1, 4)]
    barrier = pltpu.get_barrier_semaphore()
    for yy, xx in peers:
        pl.semaphore_signal(barrier, inc=1, device_id={"y": yy, "x": xx}, device_id_type=MESH)
    pl.semaphore_wait(barrier, 3)
    copies = []
    for k, (yy, xx) in enumerate(peers):
        copy = pltpu.make_async_remote_copy(
            src_ref=src,
            dst_ref=out.at[me],
            send_sem=send_sem.at[k],
            recv_sem=recv_sem.at[k],
            device_id={"y": yy, "x": xx},
            device_id_type=MESH,
        )
        copy.start()
        copies.append(copy)
    own = pltpu.make_async_copy(src, out.at[me], loc_sem)
    own.start()
    own.wait()
    for copy in copies:
        copy.wait()


def plane_exchange(src, collective_id, name):
    return pl.pallas_call(
        plane_kernel,
        out_shape=jax.ShapeDtypeStruct((4,) + src.shape, src.dtype),
        in_specs=[VMEM_SPEC],
        out_specs=VMEM_SPEC,
        scratch_shapes=[
            pltpu.SemaphoreType.DMA((3,)),
            pltpu.SemaphoreType.DMA((3,)),
            pltpu.SemaphoreType.DMA,
        ],
        compiler_params=pltpu.CompilerParams(collective_id=collective_id, has_side_effects=True),
        name=name,
    )(src)


def swap(values, axis):
    return lax.ppermute(values, axis, SWAP)


def at_index(stacked, index):
    return lax.dynamic_index_in_dim(stacked, index, 0, keepdims=False)


def plane_gather(part, rank):
    half = part.shape[0] // 2
    by_x = swap(part, "x")
    by_y = swap(part, "y")
    far = jnp.concatenate([swap(by_x[:half], "y"), swap(by_y[half:], "x")], axis=0)
    out = jnp.zeros((4,) + part.shape, part.dtype)
    for k, block in enumerate((part, by_x, by_y, far)):
        out = lax.dynamic_update_index_in_dim(out, block, rank ^ k, 0)
    return out


def plane_scatter(parts, rank):
    half = parts.shape[1] // 2
    rel = [at_index(parts, rank ^ k) for k in range(4)]
    low = [v[:half] for v in rel]
    high = [v[half:] for v in rel]
    in_x = swap(jnp.stack([low[1], low[3]]), "x").astype(F32)
    in_y = swap(jnp.stack([high[2], high[3]]), "y").astype(F32)
    low_own = low[0].astype(F32) + in_x[0]
    high_own = high[0].astype(F32) + in_y[0]
    low_rest = (low[2].astype(F32) + in_x[1]).astype(BF16)
    high_rest = (high[1].astype(F32) + in_y[1]).astype(BF16)
    low_own = low_own + swap(low_rest, "y").astype(F32)
    high_own = high_own + swap(high_rest, "x").astype(F32)
    return jnp.concatenate([low_own, high_own], axis=0)


def layer_device(
    tokens, cond, lengths, pads, timesteps, head_mask, group_mask, keep, ada_w, ada_b, w_qkv, b_qv,
    w_out, b_out, w_up, b_up, w_down, b_down, w_route, grad_out,
):
    highest = lax.Precision.HIGHEST
    y, x, p, q, c = (lax.axis_index(name) for name in "yxpqc")
    rank = y * 2 + x
    first = p == 0
    shard = p * 4 + q * 2 + c
    partner = shard ^ 4

    def to_rows(values):
        mine = jnp.where(first, values[:, 0], values[:, 1])
        other = swap(jnp.where(first, values[:, 1], values[:, 0]), "p")
        return jnp.stack([jnp.where(first, mine, other), jnp.where(first, other, mine)])

    def other_shard(weight):
        quarter = weight.shape[0] // 4
        mine = lax.dynamic_slice_in_dim(weight, rank * quarter, quarter, 0)
        return plane_gather(swap(mine, "p"), rank).reshape(weight.shape)

    token_low = to_rows(tokens)
    spread = np.zeros((6 * HD, 6 * LANES), np.float32)
    for unit in range(6):
        spread[np.arange(HD) + unit * HD, np.arange(HD) + unit * LANES] = 1.0
    spread = jnp.asarray(spread, BF16)
    qkv_other = other_shard(w_qkv)
    w_qkv_wide = jnp.concatenate(
        [
            jnp.dot(w_qkv, spread, preferred_element_type=F32).astype(BF16),
            jnp.dot(qkv_other, spread, preferred_element_type=F32).astype(BF16),
        ],
        axis=1,
    )
    biases = jnp.concatenate([b_up, b_qv])
    biases_other = swap(biases, "p")
    pairs = jnp.stack([b_qv, biases_other[2 * GW :]]).reshape(4, 2, HD).astype(F32)
    bias_wide = jnp.pad(
        jnp.stack([pairs[:, 0], jnp.zeros_like(pairs[:, 0]), pairs[:, 1]], axis=1),
        ((0, 0), (0, 0), (0, LANES - HD)),
    ).reshape(WIDE)

    cvec = cond.astype(F32) + time_embed(timesteps)
    sig = lax.logistic(cvec)
    act_low = jnp.pad((cvec * sig).astype(BF16), ((0, 0), (0, 5), (0, 0)))
    mod_part = jnp.einsum("bcd,dm->bcm", act_low, ada_w, preferred_element_type=F32) + ada_b.astype(
        F32
    )
    mod = line_exchange(mod_part, "row", 1, "mod_exchange")
    mod = jnp.transpose(mod, (1, 0, 2)).reshape(16, 6 * D)

    def row_of(values):
        return jnp.where(first, values[0], values[1])

    row_len = row_of(lengths)
    row_pad = row_of(pads)
    ends = jnp.cumsum(row_len)
    starts = ends - row_len

    def group_hot(dq, dc):
        base = (q ^ dq) * (2 * BLK) + (c ^ dc) * BLK
        places = base + jnp.arange(2)[:, None] * HALF + jnp.arange(BLK // 16)[None, :] * 16
        inside = (places[..., None] >= starts) & (places[..., None] < ends)
        return jnp.pad(inside.astype(F32), ((0, 0), (0, 0), (0, 5)))

    hot = group_hot(0, 0)
    mod_groups = jnp.einsum("sgc,cm->sgm", hot, mod, precision=highest)
    shift_one, scale_one, gate_one, shift_two, scale_two, gate_two = (
        mod_groups[:, :, None, k * D : (k + 1) * D] for k in range(6)
    )

    def grouped(values):
        return values.reshape(2, BLK // 16, 16, -1)

    def flat(values):
        return values.reshape(2, BLK, -1)

    token_values = grouped(token_low.astype(F32))
    normed_one, inverse_one = norm_rows(token_values)
    hidden_one = flat((normed_one * (1.0 + scale_one) + shift_one).astype(BF16))

    def group_gather(block):
        far = swap(block, "q")
        near = swap(block, "c")
        far_near = swap(far, "c")
        return (
            jnp.stack([block, near]).reshape(4 * BLK, -1),
            jnp.stack([far, far_near]).reshape(4 * BLK, -1),
        )

    def group_scatter(near_part, far_part):
        far_sum = (far_part[0].astype(F32) + swap(far_part[1], "c").astype(F32)).astype(BF16)
        far_in = swap(far_sum, "q")
        near_sum = near_part[0].astype(F32) + swap(near_part[1], "c").astype(F32)
        return near_sum + far_in.astype(F32)

    h1_near, h1_far = group_gather(hidden_one)

    def project(h):
        return (
            (jnp.dot(h, w_qkv_wide, preferred_element_type=F32) + bias_wide)
            .astype(BF16)
            .reshape(2, 2, BLK, WIDE)
        )

    t_near, t_far = project(h1_near), project(h1_far)

    head_row = row_of(head_mask)
    heads_here = jnp.concatenate(
        [
            lax.dynamic_slice_in_dim(head_row, shard * 2, 2, 1),
            lax.dynamic_slice_in_dim(head_row, partner * 2, 2, 1),
        ],
        axis=1,
    )
    scal = jnp.concatenate(
        [
            jnp.stack([q, c]).astype(jnp.int32),
            starts,
            row_len // UNIT,
            row_len - row_pad,
            heads_here.reshape(-1),
        ]
    ).astype(jnp.int32)
    pack = np.zeros((NH * LANES, NH * HD), np.float32)
    for head in range(NH):
        pack[np.arange(HD) + head * LANES, np.arange(HD) + head * HD] = 1.0
    pack = jnp.asarray(pack, BF16)
    o_near, o_far, lse = attn_fwd(scal, t_near, t_far, pack)

    w_out_two = jnp.concatenate([w_out, other_shard(w_out)], axis=0)
    w_out_far = swap(w_out_two, "q")
    o_mine = o_near.reshape(4 * BLK, NH * HD)
    o_in = swap(o_far, "q").reshape(4 * BLK, NH * HD)
    y_part = jnp.dot(o_mine, w_out_two, preferred_element_type=F32) + jnp.dot(
        o_in, w_out_far, preferred_element_type=F32
    )
    y_part = y_part.astype(BF16).reshape(2, 2, BLK, D)
    projected = grouped(y_part[0].astype(F32) + swap(y_part[1], "c").astype(F32))
    branch_one = projected + b_out.astype(F32)
    mixed = token_values + gate_one * branch_one
    normed_two, inverse_two = norm_rows(mixed)
    hidden_two = normed_two * (1.0 + scale_two) + shift_two
    route_w = w_route.astype(F32)
    route = lax.logistic(jnp.sum(hidden_two * route_w, axis=-1, keepdims=True))
    keep_values = grouped(to_rows(keep.astype(F32)[..., None]))
    route_keep = keep_values * route
    grad_low = to_rows(grad_out)
    grad_final = grouped(grad_low.astype(F32))
    grad_branch = grad_final * gate_two * route_keep
    h2_near, h2_far = group_gather(flat(hidden_two.astype(BF16)))
    dz_near, dz_far = group_gather(flat(grad_branch.astype(BF16)))

    w_up_two = jnp.concatenate([w_up, other_shard(w_up)], axis=1)
    w_down_two = jnp.concatenate([w_down, other_shard(w_down)], axis=0)
    b_up_two = jnp.concatenate([b_up, biases_other[: 2 * GW]]).astype(F32)
    group_row = row_of(group_mask)
    groups_here = jnp.concatenate(
        [
            lax.dynamic_slice_in_dim(group_row, shard * 2, 2, 1),
            lax.dynamic_slice_in_dim(group_row, partner * 2, 2, 1),
        ],
        axis=1,
    ).astype(F32)
    groups_here = jnp.pad(groups_here, ((0, 5), (0, 0)))

    def feed(h2, dz, dq):
        hots = jnp.stack([group_hot(dq, 0), group_hot(dq, 1)])
        mask = jnp.einsum("usgc,ch->usgh", hots, groups_here, precision=highest)
        mask = jnp.repeat(mask, GW, axis=-1)[:, :, :, None, :]

        def spread_mask(values):
            return (values.reshape(2, 2, BLK // 16, 16, 4 * GW) * mask).reshape(4 * BLK, 4 * GW)

        upper = jnp.dot(h2, w_up_two, preferred_element_type=F32) + b_up_two
        active, back = jax.vjp(gelu_tanh, upper)
        active_low = spread_mask(active).astype(BF16)
        z_part = jnp.dot(active_low, w_down_two, preferred_element_type=F32).astype(BF16)
        grad_active = lax.dot_general(
            dz, w_down_two, (((1,), (1,)), ((), ())), preferred_element_type=F32
        )
        (grad_upper,) = back(spread_mask(grad_active))
        upper_low = grad_upper.astype(BF16)
        dh_part = lax.dot_general(
            upper_low, w_up_two, (((1,), (1,)), ((), ())), preferred_element_type=F32
        ).astype(BF16)
        return active_low, upper_low, z_part.reshape(2, 2, BLK, D), dh_part.reshape(2, 2, BLK, D)

    a_far, u_far, z_far, dh_far = feed(h2_far, dz_far, 1)
    a_near, u_near, z_near, dh_near = feed(h2_near, dz_near, 0)
    lowered = grouped(group_scatter(z_near, z_far))
    grad_hidden_two = grouped(group_scatter(dh_near, dh_far))
    grad_w_up = tn(h2_near, u_near) + tn(h2_far, u_far)
    grad_w_down = tn(a_near, dz_near) + tn(a_far, dz_far)
    grad_b_up = jnp.sum(u_near, axis=0, dtype=F32) + jnp.sum(u_far, axis=0, dtype=F32)

    branch = lowered + b_down.astype(F32)
    final = mixed + gate_two * route_keep * branch
    grad_gate_two = grad_final * route_keep * branch
    grad_logit = (
        jnp.sum(grad_final * gate_two * branch, axis=-1, keepdims=True)
        * keep_values
        * route
        * (1.0 - route)
    )
    part_route = jnp.sum(grad_logit * hidden_two, axis=(0, 1, 2))
    part_b_down = jnp.sum(grad_branch, axis=(0, 1, 2))
    grad_hidden_two = grad_hidden_two + grad_logit * route_w
    grad_scale_two = grad_hidden_two * normed_two
    grad_mixed = grad_final + norm_back(
        grad_hidden_two * (1.0 + scale_two), normed_two, inverse_two
    )
    grad_gate_one = grad_mixed * branch_one
    grad_projected = grad_mixed * gate_one
    part_b_out = jnp.sum(grad_projected, axis=(0, 1, 2))
    dy_own = flat(grad_projected.astype(BF16))
    dy = jnp.stack([dy_own, swap(dy_own, "c")]).reshape(4 * BLK, D)
    do_out = nt(dy, w_out_far).astype(BF16).reshape(2, 2, BLK, NH * HD)
    do_far = swap(do_out, "q")
    do_near = nt(dy, w_out_two).astype(BF16).reshape(2, 2, BLK, NH * HD)
    d_near, d_far = attn_bwd(scal, t_near, t_far, do_near, do_far, lse, pack)
    d_near = d_near.reshape(4 * BLK, WIDE)
    d_far = d_far.reshape(4 * BLK, WIDE)
    dh1_far = nt(d_far, w_qkv_wide).astype(BF16).reshape(2, 2, BLK, D)
    dh1_near = nt(d_near, w_qkv_wide).astype(BF16).reshape(2, 2, BLK, D)
    grad_hidden_one = grouped(group_scatter(dh1_near, dh1_far))

    def reduce_pair(mine, other):
        both = plane_scatter(jnp.concatenate([mine, other], axis=2), rank)
        width = mine.shape[2]
        total = both[:, :width] + swap(both[:, width:].astype(BF16), "p").astype(F32)
        return plane_gather(total.astype(BF16), rank).astype(F32)

    down_low = grad_w_down.astype(BF16).reshape(2, 4, GW // 2, D)
    out_w_down = reduce_pair(down_low[0], down_low[1]).reshape(2 * GW, D)
    up_low = grad_w_up.astype(BF16).reshape(4, D // 4, 4 * GW)
    out_w_up = reduce_pair(up_low[:, :, : 2 * GW], up_low[:, :, 2 * GW :]).reshape(D, 2 * GW)
    wo_near = tn(o_mine, dy).astype(BF16)
    wo_far = swap(tn(o_in, dy).astype(BF16), "q").astype(F32)
    wo_low = (wo_near.astype(F32) + wo_far).astype(BF16).reshape(2, 4, HD // 2, D)
    out_w_out = reduce_pair(wo_low[0], wo_low[1]).reshape(2 * HD, D)
    wide_low = (tn(h1_near, d_near) + tn(h1_far, d_far)).astype(BF16)
    narrow = [
        nt(wide_low[:, k * 6 * LANES : (k + 1) * 6 * LANES], spread)
        .astype(BF16)
        .reshape(4, D // 4, 6 * HD)
        for k in range(2)
    ]
    out_w_qkv = reduce_pair(narrow[0], narrow[1]).reshape(D, 6 * HD)

    grad_tokens = flat(
        grad_mixed + norm_back(grad_hidden_one * (1.0 + scale_one), normed_one, inverse_one)
    )

    def from_rows(values, dtype):
        mine = jnp.where(first, values[0], values[1])
        other = swap(jnp.where(first, values[1], values[0]).astype(BF16), "p").astype(dtype)
        return jnp.stack(
            [jnp.where(first, mine, other), jnp.where(first, other, mine)], axis=1
        ).astype(dtype)

    out_final = from_rows(flat(final.astype(BF16)), BF16)
    out_tokens = from_rows(grad_tokens, F32)

    group_sums = [
        jnp.sum(v, axis=2)
        for v in (
            grad_hidden_one,
            grad_hidden_one * normed_one,
            grad_gate_one,
            grad_hidden_two,
            grad_scale_two,
            grad_final * route_keep * branch,
        )
    ]
    part_mod = jnp.einsum(
        "sgc,sgm->cm", hot, jnp.concatenate(group_sums, axis=-1), precision=highest
    )[:CROPS]
    part_mod = jnp.transpose(part_mod.reshape(CROPS, 8, 6 * D // 8), (1, 0, 2))
    smalls = jnp.stack([part_b_out, part_b_down, part_route]).reshape(3, 8, D // 8)
    smalls = jnp.pad(jnp.transpose(smalls, (1, 0, 2)), ((0, 0), (0, 0), (0, 5 * D // 8)))
    d_ones = jnp.sum(d_near, axis=0, dtype=F32) + jnp.sum(d_far, axis=0, dtype=F32)
    d_ones = d_ones.reshape(2, 2, 3, LANES)[..., :HD]
    qv_sums = jnp.stack([d_ones[:, :, 0], d_ones[:, :, 2]], axis=2).reshape(2, 4 * HD)
    bias_sums = jnp.concatenate([grad_b_up.reshape(2, 2 * GW), qv_sums], axis=1)
    who = jnp.arange(8)[:, None]
    bias_rows = jnp.where(
        who == shard, bias_sums[0], jnp.where(who == partner, bias_sums[1], 0.0)
    )
    parcel = jnp.concatenate(
        [part_mod, smalls, bias_rows[:, None], jnp.zeros((8, 1, 6 * D // 8), F32)], axis=1
    )
    parcels = line_exchange(parcel, "slice", 2, "dmod_exchange")
    line_sum = jnp.sum(parcels.reshape(2, 4, 16, 6 * D // 8), axis=1)
    line_low = line_sum.astype(BF16)
    mod_low = line_low[:, :CROPS]
    act_all = plane_exchange(act_low, 3, "act_exchange")
    plane_low = plane_exchange(line_low, 4, "small_exchange")
    mod_all = plane_low[:, :, :CROPS]
    grad_ada_w = jnp.einsum(
        "rbcd,rbcm->dm", act_all[:, :, :CROPS], mod_all, preferred_element_type=F32
    )
    grad_ada_b = jnp.sum(mod_all, axis=(0, 1, 2), dtype=F32)
    rest = jnp.sum(plane_low[:, :, CROPS:], axis=(0, 1), dtype=F32)
    grad_b_out, grad_b_down, grad_w_route = (rest[k, : D // 8] for k in range(3))
    out_b_up = rest[3, : 2 * GW]
    out_b_qv = rest[3, 2 * GW :]
    part_activ = jnp.einsum("bcm,dm->bcd", mod_low, ada_w, preferred_element_type=F32)
    part_activ = jnp.pad(part_activ.astype(BF16), ((0, 0), (0, 5), (0, 0)))
    grad_activ = jnp.sum(
        line_exchange(part_activ, "all", 5, "cond_exchange").astype(F32), axis=0
    )[:, :CROPS]
    grad_cond = grad_activ * sig * (1.0 + cvec * (1.0 - sig))
    return (
        out_final, out_tokens, grad_cond, grad_ada_w, grad_ada_b, out_w_qkv, out_b_qv, out_w_out,
        grad_b_out, out_w_up, out_b_up, out_w_down, grad_b_down, grad_w_route,
    )


IN_SPECS = (
    ("heads", "rows", None), ("rows", None, None), ("rows", None), ("rows", None), ("rows", None),
    ("rows", None, None), ("rows", None, None), ("heads", "rows"), (None, "heads"), ("heads",),
    (None, "heads"), ("heads",), ("heads", None), (), (None, "heads"), ("heads",), ("heads", None),
    (), (), ("heads", "rows", None),
)
OUT_SPECS = (
    ("heads", "rows", None), ("heads", "rows", None), ("rows", None, None), (None, "heads"),
    ("heads",), (None, "heads"), ("heads",), ("heads", None), ("heads",), (None, "heads"),
    ("heads",), ("heads", None), ("heads",), ("heads",),
)


def solution(mesh):
    paired = mesh.shape["rows"] == 4 and mesh.shape["heads"] == 8
    if paired:
        mesh = Mesh(mesh.devices.reshape(2, 2, 2, 2, 2), ("y", "x", "p", "q", "c"))
        names = {"rows": ("y", "x"), "heads": ("p", "q", "c"), None: None}
    else:
        names = {"rows": "rows", "heads": "heads", None: None}

    def specs(items):
        return tuple(P(*(names[name] for name in item)) for item in items)

    return jax.shard_map(
        layer_device if paired else per_device,
        mesh=mesh,
        in_specs=specs(IN_SPECS),
        out_specs=specs(OUT_SPECS),
        check_vma=False,
    )
```

```python
import math

import jax
import jax.numpy as jnp
import numpy as np
from jax import lax
from jax.experimental import pallas as pl
from jax.experimental.pallas import tpu as pltpu
from jax.sharding import Mesh
from jax.sharding import PartitionSpec as P

D = 1152
H = 16
HD = 72
GW = 288
SEQ = 1408
CROPS = 11
UNIT = 64
LANES = 128
EPSILON = 1e-06
MASKED_SCORE = -1000000000.0
MESH = pl.DeviceIdType.MESH
SWAP = [(0, 1), (1, 0)]
F32 = jnp.float32
BF16 = jnp.bfloat16
SCALE = HD ** (-0.5)


def time_embed(timesteps):
    halves = D // 2
    frequency = jnp.exp(-math.log(10000.0) * jnp.arange(halves, dtype=jnp.float32) / halves)
    angles = timesteps.astype(jnp.float32)[..., None] * frequency
    return jnp.concatenate([jnp.cos(angles), jnp.sin(angles)], axis=-1)


def gelu_tanh(values):
    return (
        0.5
        * values
        * (1.0 + jnp.tanh(0.7978845608028654 * (values + 0.044715 * values * values * values)))
    )


def norm_rows(values):
    average = jnp.mean(values, axis=-1, keepdims=True)
    centred = values - average
    inverse_dev = lax.rsqrt(jnp.mean(centred * centred, axis=-1, keepdims=True) + EPSILON)
    return (centred * inverse_dev, inverse_dev)


def norm_back(grad_normed, normed, inverse_dev):
    first_mean = jnp.mean(grad_normed, axis=-1, keepdims=True)
    second_mean = jnp.mean(grad_normed * normed, axis=-1, keepdims=True)
    return inverse_dev * (grad_normed - first_mean - normed * second_mean)


def crop_layout(lengths, pads, offset, amount):
    crop_ends = jnp.cumsum(lengths, axis=1)
    starts = crop_ends - lengths
    places = offset + jnp.arange(amount, dtype=jnp.int32)
    inside = (places[:, None, None] >= starts[None]) & (places[:, None, None] < crop_ends[None])
    live_part = places[:, None, None] < (crop_ends - pads)[None]
    one_hot = inside.astype(jnp.float32)
    item_ids = jnp.sum(
        inside.astype(jnp.int32) * jnp.arange(lengths.shape[1], dtype=jnp.int32), axis=2
    )
    valid = jnp.sum((inside & live_part).astype(jnp.float32), axis=2)
    return (one_hot, item_ids, valid)


def masked_scores(queries, key_rows, item_row, key_live, score_scale):
    raw = jnp.einsum("shd,thd->hst", queries, key_rows, preferred_element_type=jnp.float32)
    allowed = (item_row[:, None] == item_row[None, :]) & key_live[None, :]
    return jnp.where(allowed[None], raw * score_scale, MASKED_SCORE)


def attend_row(triple_row, item_row, key_live, score_scale):
    queries = triple_row[:, :, 0]
    key_rows = triple_row[:, :, 1]
    values = triple_row[:, :, 2]
    scores = masked_scores(queries, key_rows, item_row, key_live, score_scale)
    row_top = jnp.max(scores, axis=-1, keepdims=True)
    log_total = row_top + jnp.log(jnp.sum(jnp.exp(scores - row_top), axis=-1, keepdims=True))
    probability = jnp.exp(scores - log_total).astype(jnp.bfloat16)
    attended = jnp.einsum("hst,thd->shd", probability, values, preferred_element_type=jnp.float32)
    return (attended, log_total)


def attend_back(triple_row, grad_row, total_row, item_row, key_live, score_scale):
    queries = triple_row[:, :, 0]
    key_rows = triple_row[:, :, 1]
    values = triple_row[:, :, 2]
    scores = masked_scores(queries, key_rows, item_row, key_live, score_scale)
    probability = jnp.exp(scores - total_row)
    grad_prob = jnp.einsum("shd,thd->hst", grad_row, values, preferred_element_type=jnp.float32)
    grad_values = jnp.einsum(
        "hst,shd->thd",
        probability.astype(jnp.bfloat16),
        grad_row,
        preferred_element_type=jnp.float32,
    )
    inner = jnp.sum(probability * grad_prob, axis=-1, keepdims=True)
    grad_raw = (probability * (grad_prob - inner) * score_scale).astype(jnp.bfloat16)
    grad_queries = jnp.einsum(
        "hst,thd->shd", grad_raw, key_rows, preferred_element_type=jnp.float32
    )
    grad_keys = jnp.einsum("hst,shd->thd", grad_raw, queries, preferred_element_type=jnp.float32)
    return jnp.stack([grad_queries, grad_keys, grad_values], axis=2).astype(jnp.bfloat16)


def project_rows(source, weight):
    return jnp.einsum("sbk,kd->sbd", source, weight, preferred_element_type=jnp.float32)


def back_rows(source, weight):
    return jnp.einsum("sbk,dk->sbd", source, weight, preferred_element_type=jnp.float32)


def per_device(
    tokens,
    cond,
    lengths,
    pads,
    timesteps,
    head_mask,
    group_mask,
    keep,
    ada_w,
    ada_b,
    w_qkv,
    b_qv,
    w_out,
    b_out,
    w_up,
    b_up,
    w_down,
    b_down,
    w_route,
    grad_out,
):
    highest = lax.Precision.HIGHEST
    groups = lax.axis_size("heads")
    head_rank = lax.axis_index("heads")
    shard_len = tokens.shape[0]
    batch_local = tokens.shape[1]
    local_heads = H // groups
    score_scale = HD ** (-0.5)
    local_hot, local_items, local_valid = crop_layout(
        lengths, pads, head_rank * shard_len, shard_len
    )
    full_hot, full_items, full_valid = crop_layout(lengths, pads, 0, SEQ)
    cond_all = cond.astype(jnp.float32) + time_embed(timesteps)
    sigmoid_cond = lax.logistic(cond_all)
    silu_low = (cond_all * sigmoid_cond).astype(jnp.bfloat16)
    modulation_part = jnp.einsum(
        "bcd,dm->bcm", silu_low, ada_w, preferred_element_type=jnp.float32
    ) + ada_b.astype(jnp.float32)
    modulation = lax.all_gather(modulation_part, "heads", axis=2, tiled=True)
    token_mod = jnp.einsum("sbc,bcm->sbm", local_hot, modulation, precision=highest)
    shift_one, scale_one, gate_one, shift_two, scale_two, gate_two = jnp.split(
        token_mod, 6, axis=-1
    )
    token_values = tokens.astype(jnp.float32)
    normed_one, inverse_one = norm_rows(token_values)
    hidden_one = (normed_one * (1.0 + scale_one) + shift_one).astype(jnp.bfloat16)
    hidden_all = lax.all_gather(hidden_one, "heads", axis=0, tiled=True)
    bias_pairs = b_qv.astype(jnp.float32).reshape(local_heads, 2, HD)
    bias_triple = jnp.stack(
        [bias_pairs[:, 0], jnp.zeros_like(bias_pairs[:, 0]), bias_pairs[:, 1]], axis=1
    ).reshape(-1)
    triple_all = (
        jnp.einsum("sbd,dm->sbm", hidden_all, w_qkv, preferred_element_type=jnp.float32)
        + bias_triple
    ).astype(jnp.bfloat16)
    triple_rows = jnp.moveaxis(triple_all.reshape(SEQ, batch_local, local_heads, 3, HD), 1, 0)
    item_rows = jnp.transpose(full_items)
    live_rows = jnp.transpose(full_valid > 0.5)
    attended, totals = lax.map(
        lambda packed: attend_row(packed[0], packed[1], packed[2], score_scale),
        (triple_rows, item_rows, live_rows),
    )
    head_table = lax.dynamic_slice_in_dim(
        head_mask, head_rank * local_heads, local_heads, 2
    ).astype(jnp.float32)
    head_full = jnp.einsum("sbc,bch->sbh", full_hot, head_table, precision=highest)
    out_mask = head_full * full_valid[..., None]
    attn_low = (
        (jnp.moveaxis(attended, 0, 1) * out_mask[..., None])
        .reshape(SEQ, batch_local, local_heads * HD)
        .astype(jnp.bfloat16)
    )
    projected = lax.psum_scatter(
        project_rows(attn_low, w_out), "heads", scatter_dimension=0, tiled=True
    )
    b_out_values = b_out.astype(jnp.float32)
    mixed = token_values + gate_one * (projected + b_out_values)
    normed_two, inverse_two = norm_rows(mixed)
    hidden_two = normed_two * (1.0 + scale_two) + shift_two
    hidden_two_low = hidden_two.astype(jnp.bfloat16)
    route_values = w_route.astype(jnp.float32)
    route = lax.logistic(jnp.einsum("sbd,d->sb", hidden_two, route_values, precision=highest))
    keep_values = keep.astype(jnp.float32)
    route_keep = keep_values * route
    group_table = lax.dynamic_slice_in_dim(
        group_mask, head_rank * local_heads, local_heads, 2
    ).astype(jnp.float32)
    hidden_two_all = lax.all_gather(hidden_two_low, "heads", axis=0, tiled=True)
    group_tok = jnp.einsum("sbc,bch->sbh", full_hot, group_table, precision=highest)
    upper = jnp.einsum(
        "sbd,dk->sbk", hidden_two_all, w_up, preferred_element_type=jnp.float32
    ) + b_up.astype(jnp.float32)
    active, gelu_back = jax.vjp(gelu_tanh, upper)
    group_wide = jnp.repeat(group_tok, GW, axis=-1)
    active_low = (active * group_wide).astype(jnp.bfloat16)
    lowered = lax.psum_scatter(
        project_rows(active_low, w_down), "heads", scatter_dimension=0, tiled=True
    )
    branch = lowered + b_down.astype(jnp.float32)
    final = mixed + gate_two * route_keep[..., None] * branch
    grad_final = grad_out.astype(jnp.float32)
    grad_branch = grad_final * gate_two * route_keep[..., None]
    grad_gate_two = grad_final * route_keep[..., None] * branch
    grad_route = jnp.sum(grad_final * gate_two * branch, axis=-1) * keep_values
    grad_logit = grad_route * route * (1.0 - route)
    part_route = jnp.einsum("sb,sbd->d", grad_logit, hidden_two, precision=highest)
    part_b_down = jnp.sum(grad_branch, axis=(0, 1))
    grad_low = grad_branch.astype(jnp.bfloat16)
    grad_all = lax.all_gather(grad_low, "heads", axis=0, tiled=True)
    grad_active = jnp.einsum("sbd,kd->sbk", grad_all, w_down, preferred_element_type=jnp.float32)
    (grad_upper,) = gelu_back(grad_active * group_wide)
    upper_low = grad_upper.astype(jnp.bfloat16)
    grad_w_up = jnp.einsum(
        "sbd,sbk->dk", hidden_two_all, upper_low, preferred_element_type=jnp.float32
    )
    grad_b_up = jnp.sum(upper_low, axis=(0, 1), dtype=jnp.float32)
    grad_w_down = jnp.einsum(
        "sbk,sbd->kd", active_low, grad_all, preferred_element_type=jnp.float32
    )
    grad_hidden_two = lax.psum_scatter(
        back_rows(upper_low, w_up), "heads", scatter_dimension=0, tiled=True
    )
    grad_hidden_two = grad_hidden_two + grad_logit[..., None] * route_values
    grad_scale_two = grad_hidden_two * normed_two
    grad_mixed = grad_final + norm_back(
        grad_hidden_two * (1.0 + scale_two), normed_two, inverse_two
    )
    grad_gate_one = grad_mixed * (projected + b_out_values)
    grad_projected = grad_mixed * gate_one
    part_b_out = jnp.sum(grad_projected, axis=(0, 1))
    projected_low = grad_projected.astype(jnp.bfloat16)
    grad_proj_all = lax.all_gather(projected_low, "heads", axis=0, tiled=True)
    grad_attn = jnp.einsum(
        "sbd,kd->sbk", grad_proj_all, w_out, preferred_element_type=jnp.float32
    ).astype(jnp.bfloat16)
    grad_w_out = jnp.einsum(
        "sbk,sbd->kd", attn_low, grad_proj_all, preferred_element_type=jnp.float32
    )
    grad_masked = grad_attn.reshape(SEQ, batch_local, local_heads, HD) * out_mask[..., None].astype(
        jnp.bfloat16
    )
    grad_rows = jnp.moveaxis(grad_masked, 1, 0)
    grad_triple_rows = lax.map(
        lambda packed: attend_back(
            packed[0], packed[1], packed[2], packed[3], packed[4], score_scale
        ),
        (triple_rows, grad_rows, totals, item_rows, live_rows),
    )
    grad_triple = jnp.moveaxis(grad_triple_rows, 0, 1).reshape(
        SEQ, batch_local, local_heads * 3 * HD
    )
    grad_w_qkv = jnp.einsum(
        "sbd,sbm->dm", hidden_all, grad_triple, preferred_element_type=jnp.float32
    )
    bias_sums = jnp.sum(grad_triple, axis=(0, 1), dtype=jnp.float32).reshape(local_heads, 3, HD)
    grad_b_qv = jnp.stack([bias_sums[:, 0], bias_sums[:, 2]], axis=1).reshape(-1)
    grad_hidden_one = lax.psum_scatter(
        back_rows(grad_triple, w_qkv), "heads", scatter_dimension=0, tiled=True
    )
    grad_tokens = grad_mixed + norm_back(
        grad_hidden_one * (1.0 + scale_one), normed_one, inverse_one
    )
    grad_token_mod = jnp.concatenate(
        [
            grad_hidden_one,
            grad_hidden_one * normed_one,
            grad_gate_one,
            grad_hidden_two,
            grad_scale_two,
            grad_gate_two,
        ],
        axis=-1,
    )
    part_mod = jnp.einsum("sbc,sbm->bcm", local_hot, grad_token_mod, precision=highest)
    grad_mod, share_b_out, share_b_down, share_route = (
        lax.psum_scatter(part_mod, "heads", scatter_dimension=2, tiled=True),
        lax.psum_scatter(part_b_out, "heads", scatter_dimension=0, tiled=True),
        lax.psum_scatter(part_b_down, "heads", scatter_dimension=0, tiled=True),
        lax.psum_scatter(part_route, "heads", scatter_dimension=0, tiled=True),
    )
    mod_low = grad_mod.astype(jnp.bfloat16)
    grad_ada_w = jnp.einsum("bcd,bcm->dm", silu_low, mod_low, preferred_element_type=jnp.float32)
    grad_ada_b = jnp.sum(mod_low, axis=(0, 1), dtype=jnp.float32)
    part_activ = jnp.einsum("bcm,dm->bcd", mod_low, ada_w, preferred_element_type=jnp.float32)
    grad_activ = lax.psum(part_activ.astype(jnp.bfloat16), "heads").astype(jnp.float32)
    grad_cond = grad_activ * sigmoid_cond * (1.0 + cond_all * (1.0 - sigmoid_cond))
    summed = (
        lax.psum(grad_ada_w.astype(jnp.bfloat16), "rows").astype(jnp.float32),
        lax.psum(grad_ada_b.astype(jnp.bfloat16), "rows").astype(jnp.float32),
        lax.psum(grad_w_qkv.astype(jnp.bfloat16), "rows").astype(jnp.float32),
        lax.psum(grad_b_qv.astype(jnp.bfloat16), "rows").astype(jnp.float32),
        lax.psum(grad_w_out.astype(jnp.bfloat16), "rows").astype(jnp.float32),
        lax.psum(share_b_out.astype(jnp.bfloat16), "rows").astype(jnp.float32),
        lax.psum(grad_w_up.astype(jnp.bfloat16), "rows").astype(jnp.float32),
        lax.psum(grad_b_up.astype(jnp.bfloat16), "rows").astype(jnp.float32),
        lax.psum(grad_w_down.astype(jnp.bfloat16), "rows").astype(jnp.float32),
        lax.psum(share_b_down.astype(jnp.bfloat16), "rows").astype(jnp.float32),
        lax.psum(share_route.astype(jnp.bfloat16), "rows").astype(jnp.float32),
    )
    return (
        final.astype(jnp.bfloat16),
        grad_tokens,
        grad_cond,
        summed[0],
        summed[1],
        summed[2],
        summed[3],
        summed[4],
        summed[5],
        summed[6],
        summed[7],
        summed[8],
        summed[9],
        summed[10],
    )


BLK = 176
NH = 4
HALF = SEQ // 2


def each_crop(scal, body):
    def step(item, carry):
        units = scal[CROPS + item]
        for count in range(2, 9):

            @pl.when(units == count)
            def _():
                body(item, pl.multiple_of(scal[item], UNIT), count * UNIT)

        return carry

    lax.fori_loop(0, CROPS, step, 0)


def nt(a, b):
    return lax.dot_general(a, b, (((1,), (1,)), ((), ())), preferred_element_type=F32)


def tn(a, b):
    return lax.dot_general(a, b, (((0,), (0,)), ((), ())), preferred_element_type=F32)


def attn_fwd_kernel(scal, buf, pack, obuf, lse):
    lane = lax.broadcasted_iota(jnp.int32, (1, LANES), 1)

    def body(item, start, size):
        live = scal[2 * CROPS + item]
        keys_live = lax.broadcasted_iota(jnp.int32, (1, size), 1) < live
        rows_live = (lax.broadcasted_iota(jnp.int32, (size, 1), 0) < live).astype(F32)
        window = pl.ds(start, size)
        packed = jnp.zeros((size, NH * HD), F32)
        totals = jnp.zeros((size, LANES), F32)
        for head in range(NH):
            at = head * 3 * LANES
            queries = buf[window, at : at + LANES]
            keys = buf[window, at + LANES : at + 2 * LANES]
            values = buf[window, at + 2 * LANES : at + 3 * LANES]
            scores = jnp.where(keys_live, nt(queries, keys) * SCALE, MASKED_SCORE)
            top = jnp.max(scores, axis=1, keepdims=True)
            expo = jnp.exp(scores - top)
            total = jnp.sum(expo, axis=1, keepdims=True)
            prob = (expo * (1.0 / total)).astype(BF16)
            mixed = jnp.dot(prob, values, preferred_element_type=F32)
            mask = scal[3 * CROPS + item * NH + head].astype(F32)
            mixed = (mixed * (rows_live * mask)).astype(BF16)
            packed += jnp.dot(
                mixed, pack[head * LANES : (head + 1) * LANES, :], preferred_element_type=F32
            )
            totals = jnp.where(lane == head, top + jnp.log(total), totals)
        obuf[window, :] = packed.astype(BF16)
        lse[window, :] = totals

    each_crop(scal, body)


def attn_bwd_kernel(scal, buf, gbuf, lse, pack, dbuf):
    def body(item, start, size):
        live = scal[2 * CROPS + item]
        keys_live = lax.broadcasted_iota(jnp.int32, (1, size), 1) < live
        rows_live = lax.broadcasted_iota(jnp.int32, (size, 1), 0) < live
        window = pl.ds(start, size)
        grads = gbuf[window, :]
        grads = jnp.where(rows_live, grads.astype(F32), 0.0).astype(BF16)
        for head in range(NH):
            at = head * 3 * LANES
            queries = buf[window, at : at + LANES]
            keys = buf[window, at + LANES : at + 2 * LANES]
            values = buf[window, at + 2 * LANES : at + 3 * LANES]
            mask = scal[3 * CROPS + item * NH + head].astype(F32)
            grad = (nt(grads, pack[head * LANES : (head + 1) * LANES, :]) * mask).astype(BF16)
            scores = jnp.where(keys_live, nt(queries, keys) * SCALE, MASKED_SCORE)
            prob = jnp.exp(scores - lse[window, head : head + 1])
            grad_prob = nt(grad, values)
            grad_values = tn(prob.astype(BF16), grad)
            inner = jnp.sum(prob * grad_prob, axis=1, keepdims=True)
            grad_raw = (prob * (grad_prob - inner) * SCALE).astype(BF16)
            dbuf[window, at : at + LANES] = jnp.dot(
                grad_raw, keys, preferred_element_type=F32
            ).astype(BF16)
            dbuf[window, at + LANES : at + 2 * LANES] = tn(grad_raw, queries).astype(BF16)
            dbuf[window, at + 2 * LANES : at + 3 * LANES] = grad_values.astype(BF16)

    each_crop(scal, body)


WIDE = NH * 3 * LANES
SMEM_SPEC = pl.BlockSpec(memory_space=pltpu.SMEM)
VMEM_SPEC = pl.BlockSpec(memory_space=pltpu.VMEM)
ANY_SPEC = pl.BlockSpec(memory_space=pl.ANY)


def attn_fwd(scal, triple, pack):
    return pl.pallas_call(
        attn_fwd_kernel,
        out_shape=(
            jax.ShapeDtypeStruct((SEQ, NH * HD), BF16),
            jax.ShapeDtypeStruct((SEQ, LANES), F32),
        ),
        in_specs=[SMEM_SPEC, VMEM_SPEC, VMEM_SPEC],
        out_specs=(VMEM_SPEC, VMEM_SPEC),
        compiler_params=pltpu.CompilerParams(vmem_limit_bytes=48 * 2**20),
        name="attn_fwd",
    )(scal, triple, pack)


def attn_bwd(scal, triple, grads, lse, pack):
    return pl.pallas_call(
        attn_bwd_kernel,
        out_shape=jax.ShapeDtypeStruct((SEQ, WIDE), BF16),
        in_specs=[SMEM_SPEC] + [VMEM_SPEC] * 4,
        out_specs=VMEM_SPEC,
        compiler_params=pltpu.CompilerParams(vmem_limit_bytes=48 * 2**20),
        name="attn_bwd",
    )(scal, triple, grads, lse, pack)


def line_kernel(pick, src, out, send_sem, recv_sem, loc_sem):
    p, q, c = lax.axis_index("p"), lax.axis_index("q"), lax.axis_index("c")
    me = p * 4 + q * 2 + c
    peers = []
    for k in range(1, 8):
        pp, qq, cc = lax.rem(p + k // 4, 2), lax.rem(q + (k // 2) % 2, 2), lax.rem(c + k % 2, 2)
        peers.append((pp, qq, cc))
    barrier = pltpu.get_barrier_semaphore()
    for pp, qq, cc in peers:
        pl.semaphore_signal(
            barrier, inc=1, device_id={"p": pp, "q": qq, "c": cc}, device_id_type=MESH
        )
    pl.semaphore_wait(barrier, 7)

    def source(pp, qq, cc):
        if pick == "row":
            return src.at[pp]
        if pick == "all":
            return src
        return src.at[pp * 4 + qq * 2 + cc]

    copies = []
    for k, (pp, qq, cc) in enumerate(peers):
        copy = pltpu.make_async_remote_copy(
            src_ref=source(pp, qq, cc),
            dst_ref=out.at[me],
            send_sem=send_sem.at[k],
            recv_sem=recv_sem.at[k],
            device_id={"p": pp, "q": qq, "c": cc},
            device_id_type=MESH,
        )
        copy.start()
        copies.append(copy)
    own = pltpu.make_async_copy(source(p, q, c), out.at[me], loc_sem)
    own.start()
    own.wait()
    for copy in copies:
        copy.wait()


def line_exchange(src, pick, collective_id, name):
    shape = src.shape if pick == "all" else src.shape[1:]
    return pl.pallas_call(
        lambda *refs: line_kernel(pick, *refs),
        out_shape=jax.ShapeDtypeStruct((8,) + shape, src.dtype),
        in_specs=[VMEM_SPEC],
        out_specs=VMEM_SPEC,
        scratch_shapes=[
            pltpu.SemaphoreType.DMA((7,)),
            pltpu.SemaphoreType.DMA((7,)),
            pltpu.SemaphoreType.DMA,
        ],
        compiler_params=pltpu.CompilerParams(collective_id=collective_id, has_side_effects=True),
        name=name,
    )(src)


def plane_kernel(src, out, send_sem, recv_sem, loc_sem):
    y, x = lax.axis_index("y"), lax.axis_index("x")
    me = y * 2 + x
    peers = [(lax.rem(y + k // 2, 2), lax.rem(x + k % 2, 2)) for k in range(1, 4)]
    barrier = pltpu.get_barrier_semaphore()
    for yy, xx in peers:
        pl.semaphore_signal(barrier, inc=1, device_id={"y": yy, "x": xx}, device_id_type=MESH)
    pl.semaphore_wait(barrier, 3)
    copies = []
    for k, (yy, xx) in enumerate(peers):
        copy = pltpu.make_async_remote_copy(
            src_ref=src,
            dst_ref=out.at[me],
            send_sem=send_sem.at[k],
            recv_sem=recv_sem.at[k],
            device_id={"y": yy, "x": xx},
            device_id_type=MESH,
        )
        copy.start()
        copies.append(copy)
    own = pltpu.make_async_copy(src, out.at[me], loc_sem)
    own.start()
    own.wait()
    for copy in copies:
        copy.wait()


def plane_exchange(src, collective_id, name):
    return pl.pallas_call(
        plane_kernel,
        out_shape=jax.ShapeDtypeStruct((4,) + src.shape, src.dtype),
        in_specs=[VMEM_SPEC],
        out_specs=VMEM_SPEC,
        scratch_shapes=[
            pltpu.SemaphoreType.DMA((3,)),
            pltpu.SemaphoreType.DMA((3,)),
            pltpu.SemaphoreType.DMA,
        ],
        compiler_params=pltpu.CompilerParams(collective_id=collective_id, has_side_effects=True),
        name=name,
    )(src)


QTR = 144
WROWS = 576
BIAS = 1408
GROUPS = 24
UNIT_ROWS = 6 * HD
CUT = 80


def remote(src, dst, sems, k, **where):
    return pltpu.make_async_remote_copy(
        src_ref=src,
        dst_ref=dst,
        send_sem=sems[0].at[k],
        recv_sem=sems[1].at[k],
        device_id=where,
        device_id_type=MESH,
    )


def greet(peers):
    barrier = pltpu.get_barrier_semaphore()
    for where in peers:
        pl.semaphore_signal(barrier, inc=1, device_id=where, device_id_type=MESH)
    pl.semaphore_wait(barrier, len(peers))


def line_peers(p, q, c):
    out = []
    for k in range(1, 8):
        out.append(
            {
                "p": lax.rem(p + k // 4, 2),
                "q": lax.rem(q + (k // 2) % 2, 2),
                "c": lax.rem(c + k % 2, 2),
            }
        )
    return out


def rows_at(start, size):
    return pl.ds(pl.multiple_of(start, 16), size)


class PlaneGather:
    def __init__(self, src, dst, sems, k, y, x, p):
        self.dst, self.sems, self.k, self.y, self.x = dst, sems, k, y, x
        self.rank = y * 2 + x
        mine = rows_at(self.rank * QTR, QTR)
        self.over = remote(src.at[mine], dst.at[mine], sems, k, p=1 - p)
        self.to_x = remote(dst.at[mine], dst.at[mine], sems, k + 1, x=1 - x)
        self.to_y = remote(dst.at[mine], dst.at[mine], sems, k + 2, y=1 - y)
        from_x = rows_at((y * 2 + 1 - x) * QTR, CUT)
        from_y = rows_at(((1 - y) * 2 + x) * QTR + CUT, QTR - CUT)
        self.on_y = remote(dst.at[from_x], dst.at[from_x], sems, k + 3, y=1 - y)
        self.on_x = remote(dst.at[from_y], dst.at[from_y], sems, k + 4, x=1 - x)

    def start(self):
        self.over.start()

    def spread(self):
        self.over.wait_recv()
        self.to_x.start()
        self.to_y.start()

    def forward(self):
        self.to_x.wait_recv()
        self.on_y.start()
        self.to_y.wait_recv()
        self.on_x.start()

    def finish(self):
        self.on_y.wait_recv()
        self.on_x.wait_recv()

    def sent(self):
        for copy in (self.over, self.to_x, self.to_y, self.on_y, self.on_x):
            copy.wait_send()


def norm_tile(values):
    average = jnp.mean(values, axis=1, keepdims=True)
    centred = values - average
    inverse = lax.rsqrt(jnp.mean(centred * centred, axis=1, keepdims=True) + EPSILON)
    return centred * inverse, inverse


def front_kernel(
    part, x_pair, k_pair, act, bias_own, w_a, spread, hot,
    t_out, h_out, x_out, k_out, modg_out, wide_out, wo_out, bias_out, act_out,
    mods, modg, h, wide, other_a, own_a, tbuf, send, recv, loc,
):
    y, x, p, q, c = (lax.axis_index(name) for name in "yxpqc")
    sems = (send, recv)
    pair = [
        {"q": lax.rem(q + k // 2, 2), "c": lax.rem(c + k % 2, 2)} for k in range(1, 4)
    ]
    plane = [{"y": lax.rem(y + k // 2, 2), "x": lax.rem(x + k % 2, 2)} for k in range(1, 4)]
    greet(pair + plane + [{"p": 1 - p}])
    rank = y * 2 + x
    waits = []

    def keep_local(src, dst, k):
        copy = pltpu.make_async_copy(src, dst, loc.at[k])
        copy.start()
        return copy

    def spot(pp, qq, cc):
        return pp * 4 + qq * 2 + cc

    mod_over = remote(part.at[1 - p], mods.at[spot(p, q, c)], sems, 0, p=1 - p)
    mod_over.start()
    bias_copy = remote(bias_own, bias_out.at[1], sems, 7, p=1 - p)
    bias_copy.start()
    x_copy = remote(x_pair.at[1 - p], x_out.at[p], sems, 8, p=1 - p)
    x_copy.start()
    k_copy = remote(k_pair.at[1 - p], k_out.at[p], sems, 9, p=1 - p)
    k_copy.start()
    take_a = PlaneGather(w_a, other_a, sems, 10, y, x, p)
    take_a.start()
    own_mod = keep_local(part.at[p], mods.at[spot(p, q, c)], 1)
    mod_own = []
    mod_far = []
    for k, where in enumerate(pair):
        mine = mods.at[spot(p, q, c)]
        copy = remote(part.at[p], mine, sems, 1 + k, **where)
        copy.start()
        mod_own.append(copy)
    load_a = keep_local(w_a, own_a, 0)
    waits.append(keep_local(x_pair.at[p], x_out.at[p], 2))
    waits.append(keep_local(k_pair.at[p], k_out.at[p], 3))
    waits.append(keep_local(bias_own, bias_out.at[0], 4))
    waits.append(keep_local(act, act_out.at[rank], 5))
    acts = []
    for k, where in enumerate(plane):
        copy = remote(act, act_out.at[rank], sems, 15 + k, **where)
        copy.start()
        acts.append(copy)
    mod_over.wait_recv()
    for k, where in enumerate(pair):
        far = mods.at[spot(1 - p, q, c)]
        copy = remote(far, far, sems, 4 + k, **where)
        copy.start()
        mod_far.append(copy)

    load_a.wait()
    wide[: 6 * LANES, :] = jnp.dot(
        spread[...], own_a[:UNIT_ROWS, :], preferred_element_type=F32
    ).astype(BF16)

    own_mod.wait()
    for copy in mod_own + mod_far:
        copy.wait_recv()
    full = jnp.concatenate([mods[k] for k in range(8)], axis=1)
    modg[...] = jnp.dot(
        hot[...], full, preferred_element_type=F32, precision=lax.Precision.HIGHEST
    )
    waits.append(keep_local(modg, modg_out, 6))

    def place(slot, chip, core):
        return slot * HALF + chip * (2 * BLK) + core * BLK

    def modulate(src, slot):
        base = place(slot, q, c)

        def group(g, carry):
            values = src[rows_at(g * 16, 16), :].astype(F32)
            normed, _ = norm_tile(values)
            row = slot * (BLK // 16) + g
            shift = modg[pl.ds(row, 1), 0:D]
            scale = modg[pl.ds(row, 1), D : 2 * D]
            h[rows_at(base + g * 16, 16), :] = (normed * (1.0 + scale) + shift).astype(BF16)
            return carry

        lax.fori_loop(0, BLK // 16, group, 0)

    def block(slot, chip, core):
        return h.at[rows_at(place(slot, chip, core), BLK)]

    hops = {}
    for i in range(2):
        slot = p if i == 0 else 1 - p
        mine = block(slot, q, c)
        other = block(slot, 1 - q, c)
        hops[i] = (
            remote(mine, mine, sems, 18 + 3 * i, q=1 - q),
            remote(mine, mine, sems, 19 + 3 * i, c=1 - c),
            remote(other, other, sems, 20 + 3 * i, c=1 - c),
        )

    modulate(x_pair.at[p], p)
    hops[0][0].start()
    hops[0][1].start()
    x_copy.wait_recv()
    modulate(x_out.at[1 - p], 1 - p)
    hops[1][0].start()
    hops[1][1].start()
    take_a.spread()
    bias_copy.wait_recv()
    for copy in waits[2:3]:
        copy.wait()
    hops[0][1].wait_recv()

    def project(slot, chip, half):
        rows = rows_at(place(slot, chip, 0), 2 * BLK)
        cols = slice(half * 6 * LANES, (half + 1) * 6 * LANES)
        line = bias_out[half, 0:1, : 6 * LANES]
        tbuf[rows, cols] = (nt(h[rows, :], wide[cols, :]) + line).astype(BF16)

    first, second = p, 1 - p
    project(first, q, 0)
    hops[0][0].wait_recv()
    hops[0][2].start()
    hops[1][1].wait_recv()
    project(second, q, 0)
    take_a.forward()
    hops[0][2].wait_recv()
    project(first, 1 - q, 0)
    hops[1][0].wait_recv()
    hops[1][2].start()
    take_a.finish()
    wide[6 * LANES :, :] = jnp.dot(
        spread[...], other_a[:UNIT_ROWS, :], preferred_element_type=F32
    ).astype(BF16)
    waits.append(keep_local(wide, wide_out, 7))
    tails = (own_a.at[UNIT_ROWS:], other_a.at[UNIT_ROWS:])
    outer = [remote(tails[k], wo_out.at[2 + k], sems, 24 + k, q=1 - q) for k in range(2)]
    for copy in outer:
        copy.start()
    for k in range(2):
        waits.append(keep_local(tails[k], wo_out.at[k], 8 + k))
    project(first, q, 1)
    project(second, q, 1)
    project(first, 1 - q, 1)
    hops[1][2].wait_recv()
    waits.append(keep_local(h, h_out, 10))
    project(second, 1 - q, 0)
    project(second, 1 - q, 1)
    waits.append(keep_local(tbuf, t_out, 11))
    for copy in outer + acts + [k_copy]:
        copy.wait_recv()
    for copy in [mod_over, bias_copy, x_copy, k_copy] + mod_own + mod_far + outer + acts:
        copy.wait_send()
    for i in range(2):
        for copy in hops[i]:
            copy.wait_send()
    take_a.sent()
    for k, copy in enumerate(waits):
        if k != 2:
            copy.wait()


def shape_of(*shape, dtype=BF16):
    return jax.ShapeDtypeStruct(shape, dtype)


def front(part, x_pair, k_pair, act, bias_own, w_a, spread, hot):
    return pl.pallas_call(
        front_kernel,
        out_shape=(
            shape_of(SEQ, WIDE), shape_of(SEQ, D), shape_of(2, BLK, D), shape_of(2, BLK, LANES),
            shape_of(GROUPS, 6 * D, dtype=F32), shape_of(WIDE, D), shape_of(4, QTR, D),
            shape_of(2, 8, BIAS, dtype=F32), shape_of(4, 2, 16, D),
        ),
        in_specs=[VMEM_SPEC] * 5 + [ANY_SPEC] + [VMEM_SPEC] * 2,
        out_specs=(
            ANY_SPEC, ANY_SPEC, VMEM_SPEC, VMEM_SPEC, ANY_SPEC, ANY_SPEC, ANY_SPEC, VMEM_SPEC,
            VMEM_SPEC,
        ),
        scratch_shapes=[
            pltpu.VMEM((8, 16, 6 * D // 8), F32),
            pltpu.VMEM((GROUPS, 6 * D), F32),
            pltpu.VMEM((SEQ, D), BF16),
            pltpu.VMEM((WIDE, D), BF16),
            pltpu.VMEM((WROWS, D), BF16),
            pltpu.VMEM((WROWS, D), BF16),
            pltpu.VMEM((SEQ, WIDE), BF16),
            pltpu.SemaphoreType.DMA((26,)),
            pltpu.SemaphoreType.DMA((26,)),
            pltpu.SemaphoreType.DMA((12,)),
        ],
        compiler_params=pltpu.CompilerParams(
            collective_id=6, has_side_effects=True, vmem_limit_bytes=56 * 2**20
        ),
        name="front",
    )(part, x_pair, k_pair, act, bias_own, w_a, spread, hot)


def gelu_both(u):
    cube = 0.044715 * u * u
    t = jnp.tanh(0.7978845608028654 * (u + cube * u))
    half = 0.5 * (1.0 + t)
    slope = half + 0.5 * u * (1.0 - t * t) * (0.7978845608028654 * (1.0 + 3.0 * cube))
    return u * half, slope


def middle_kernel(
    o, x2, k2, modg, g_pair, wo, w_up, w_down, bias, consts, gmask,
    final_out, dx_out, do_out, sums_out, small_out, up_out, down_out, gwo_out, bup_out,
    g2, o_in, ybig, ysend, yrecv, y1, mixed, h2, dz, act, du, wup, wdown,
    own, csend, crecv, qsend, qrecv, dy, dofar, wosend, worecv, send, recv, loc,
):
    y, x, p, q, c = (lax.axis_index(name) for name in "yxpqc")
    sems = (send, recv)
    greet([{"q": 1 - q}, {"c": 1 - c}, {"p": 1 - p}, {"x": 1 - x}, {"y": 1 - y}])
    waits = []

    def keep_local(src, dst, k):
        copy = pltpu.make_async_copy(src, dst, loc.at[k])
        copy.start()
        return copy

    def place(slot, chip, core):
        return slot * HALF + chip * (2 * BLK) + core * BLK

    o_copies = []
    for slot in range(2):
        copy = remote(
            o.at[rows_at(place(slot, 1 - q, 0), 2 * BLK)], o_in.at[slot], sems, slot, q=1 - q
        )
        copy.start()
        o_copies.append(copy)
    g_copy = remote(g_pair.at[1 - p], g2.at[pl.ds(p * BLK, BLK)], sems, 2, p=1 - p)
    g_copy.start()
    take_up = PlaneGather(w_up, wup.at[WROWS:], sems, 3, y, x, p)
    take_down = PlaneGather(w_down, wdown.at[WROWS:], sems, 8, y, x, p)
    take_up.start()
    take_down.start()
    own_g = keep_local(g_pair.at[p], g2.at[pl.ds(p * BLK, BLK)], 0)
    own_up = keep_local(w_up, wup.at[:WROWS], 1)
    own_down = keep_local(w_down, wdown.at[:WROWS], 2)

    y_copies = []
    for slot in range(2):
        rows = rows_at(place(slot, q, 0), 2 * BLK)
        o_copies[slot].wait_recv()
        ybig[...] = jnp.dot(o[rows, :], wo[0 : 2 * QTR, :], preferred_element_type=F32) + jnp.dot(
            o_in[slot], wo[2 * QTR : 4 * QTR, :], preferred_element_type=F32
        )
        ysend[slot] = ybig[rows_at((1 - c) * BLK, BLK), :].astype(BF16)
        y1[slot * BLK : (slot + 1) * BLK, :] = ybig[rows_at(c * BLK, BLK), :]
        copy = remote(ysend.at[slot], yrecv.at[slot], sems, 13 + slot, c=1 - c)
        copy.start()
        y_copies.append(copy)

    own_g.wait()
    g_copy.wait_recv()
    take_up.spread()
    b_out, b_down, w_route = consts[0:1, :], consts[1:2, :], consts[2:3, :]

    def routed(row):
        rows = rows_at(row * 16, 16)
        normed, inverse = norm_tile(mixed[rows, :])
        hidden = normed * (1.0 + modg[pl.ds(row, 1), 4 * D : 5 * D]) + modg[
            pl.ds(row, 1), 3 * D : 4 * D
        ]
        logit = jnp.sum(hidden * w_route, axis=1, keepdims=True)
        route = 1.0 / (1.0 + jnp.exp(-logit))
        kept = k2[rows, 0:1].astype(F32)
        return rows, normed, inverse, hidden, route, kept

    bufs = (h2, dz)

    def hop(array, slot, kind):
        mine = bufs[array].at[rows_at(place(slot, q, c), BLK)]
        far = bufs[array].at[rows_at(place(slot, 1 - q, c), BLK)]
        k = 15 + (slot * 2 + array) * 3 + kind
        if kind == 0:
            return remote(mine, mine, sems, k, q=1 - q)
        if kind == 1:
            return remote(mine, mine, sems, k, c=1 - c)
        return remote(far, far, sems, k, c=1 - c)

    for slot in range(2):
        y_copies[slot].wait_recv()

        def group(g, carry, slot=slot):
            row = slot * (BLK // 16) + g
            rows = rows_at(row * 16, 16)
            branch = y1[rows, :] + yrecv[slot, rows_at(g * 16, 16), :].astype(F32) + b_out
            y1[rows, :] = branch
            mixed[rows, :] = x2[rows, :].astype(F32) + modg[pl.ds(row, 1), 2 * D : 3 * D] * branch
            _, _, _, hidden, route, kept = routed(row)
            there = rows_at(place(slot, q, c) + g * 16, 16)
            h2[there, :] = hidden.astype(BF16)
            gate = modg[pl.ds(row, 1), 5 * D : 6 * D]
            dz[there, :] = (g2[rows, :].astype(F32) * gate * (kept * route)).astype(BF16)
            return carry

        lax.fori_loop(0, BLK // 16, group, 0)
        for array in range(2):
            hop(array, slot, 0).start()
            hop(array, slot, 1).start()

    take_up.forward()
    take_down.spread()
    own_up.wait()
    own_down.wait()
    take_up.finish()
    take_down.forward()
    take_down.finish()

    def core_copy(array, side, slot):
        k = 27 + (array * 2 + side) * 2 + slot
        return remote(csend.at[array, side, slot], crecv.at[array, side, slot], sems, k, c=1 - c)

    def chip_copy(array, slot):
        return remote(qsend.at[array, slot], qrecv.at[array, slot], sems, 35 + array * 2 + slot, q=1 - q)

    def far_out(slot):
        for array in range(2):
            core_copy(array, 1, slot).wait_recv()
            qsend[array, slot] = (
                own[array, 1, slot] + crecv[array, 1, slot].astype(F32)
            ).astype(BF16)
            chip_copy(array, slot).start()

    def feed(step, carry):
        side, slot = step // 2, lax.rem(step, 2)
        chip = lax.rem(q + side, 2)
        start = place(slot, chip, 0)

        @pl.when(step == 0)
        def _():
            for array in range(2):
                hop(array, 0, 1).wait_recv()

        @pl.when(step == 1)
        def _():
            for array in range(2):
                hop(array, 1, 1).wait_recv()

        @pl.when(step == 2)
        def _():
            for array in range(2):
                hop(array, 0, 0).wait_recv()
                hop(array, 0, 2).start()
            for array in range(2):
                hop(array, 0, 2).wait_recv()

        @pl.when(step == 3)
        def _():
            for array in range(2):
                hop(array, 1, 0).wait_recv()
                hop(array, 1, 2).start()
            far_out(0)
            for array in range(2):
                hop(array, 1, 2).wait_recv()

        def tile(part, carry):
            rows = rows_at(start + part * BLK, BLK)
            u = nt(h2[rows, :], wup[...]) + bias[0:1, :]
            value, slope = gelu_both(u)
            row0 = start // 16 + part * (BLK // 16)
            mask = jnp.concatenate(
                [
                    jnp.broadcast_to(gmask[pl.ds(row0 + k, 1), :], (16, D))
                    for k in range(BLK // 16)
                ],
                axis=0,
            )
            act[rows, :] = (value * mask).astype(BF16)
            da = nt(dz[rows, :], wdown[...])
            du[rows, :] = (slope * mask * da).astype(BF16)
            z_part = jnp.dot(act[rows, :], wdown[...], preferred_element_type=F32)
            h_part = jnp.dot(du[rows, :], wup[...], preferred_element_type=F32)

            @pl.when(part == c)
            def _():
                own[0, side, slot] = z_part
                own[1, side, slot] = h_part

            @pl.when(part != c)
            def _():
                csend[0, side, slot] = z_part.astype(BF16)
                csend[1, side, slot] = h_part.astype(BF16)

            return carry

        lax.fori_loop(0, 2, tile, 0)
        for array in range(2):
            core_copy(array, side, slot).start()
        return carry

    lax.fori_loop(0, 4, feed, 0)
    far_out(1)

    for copy in (take_up, take_down):
        copy.sent()

    def weight_chunk(j, carry):
        cols = pl.ds(pl.multiple_of(j * 384, LANES), 384)
        rows = rows_at(j * 384, 384)
        wup[rows, :] = tn(du[:, cols], h2[...]).astype(BF16)
        wdown[rows, :] = tn(act[:, cols], dz[...]).astype(BF16)
        return carry

    lax.fori_loop(0, 3, weight_chunk, 0)
    waits.append(keep_local(wup, up_out, 3))
    waits.append(keep_local(wdown, down_out, 4))
    bup_out[...] = jnp.dot(jnp.ones((8, SEQ), BF16), du[...], preferred_element_type=F32)

    small_out[...] = jnp.zeros_like(small_out)
    sums_out[22:24, :] = jnp.zeros((2, 4 * D), F32)
    dy_copies = []
    do_copies = []
    for slot in range(2):
        for array in range(2):
            core_copy(array, 0, slot).wait_recv()
            chip_copy(array, slot).wait_recv()

        def back(g, carry, slot=slot):
            row = slot * (BLK // 16) + g
            rows, normed, inverse, hidden, route, kept = routed(row)
            here = rows_at(g * 16, 16)

            def total(array):
                return (
                    own[array, 0, slot, here, :]
                    + crecv[array, 0, slot, here, :].astype(F32)
                    + qrecv[array, slot, here, :].astype(F32)
                )

            gate_one = modg[pl.ds(row, 1), 2 * D : 3 * D]
            gate_two = modg[pl.ds(row, 1), 5 * D : 6 * D]
            scale_two = modg[pl.ds(row, 1), 4 * D : 5 * D]
            grad = g2[rows, :].astype(F32)
            pass_on = kept * route
            branch = total(0) + b_down
            final_out[rows, :] = (mixed[rows, :] + gate_two * pass_on * branch).astype(BF16)
            grad_gate_two = grad * pass_on * branch
            gated = grad * gate_two
            logit = (
                jnp.sum(gated * branch, axis=1, keepdims=True) * kept * route * (1.0 - route)
            )
            dh = total(1) + logit * w_route
            e = dh * (1.0 + scale_two)
            dx = grad + inverse * (
                e
                - jnp.mean(e, axis=1, keepdims=True)
                - normed * jnp.mean(e * normed, axis=1, keepdims=True)
            )
            dx_out[rows, :] = dx
            dyb = dx * gate_one
            dy[slot, c, here, :] = dyb.astype(BF16)

            def down(v):
                return jnp.sum(v, axis=0, keepdims=True)

            small_out[0:1, :] += down(dyb)
            small_out[1:2, :] += down(gated * pass_on)
            small_out[2:3, :] += down(logit * hidden)
            at = pl.ds(row, 1)
            sums_out[at, 0:D] = down(dx * y1[rows, :])
            sums_out[at, D : 2 * D] = down(dh)
            sums_out[at, 2 * D : 3 * D] = down(dh * normed)
            sums_out[at, 3 * D : 4 * D] = down(grad_gate_two)
            return carry

        lax.fori_loop(0, BLK // 16, back, 0)
        copy = remote(dy.at[slot, c], dy.at[slot, c], sems, 39 + slot, c=1 - c)
        copy.start()
        dy_copies.append(copy)
    for slot in range(2):
        dy_copies[slot].wait_recv()
        rows = rows_at(place(slot, q, 0), 2 * BLK)
        grads = dy[slot].reshape(2 * BLK, D)
        dofar[slot] = nt(grads, wo[2 * QTR : 4 * QTR, :]).astype(BF16)
        copy = remote(dofar.at[slot], do_out.at[rows], sems, 41 + slot, q=1 - q)
        copy.start()
        do_copies.append(copy)
        do_out[rows, :] = nt(grads, wo[0 : 2 * QTR, :]).astype(BF16)

    def out_grad(left):
        return sum(tn(left(slot), dy[slot].reshape(2 * BLK, D)) for slot in range(2))

    wosend[...] = out_grad(lambda slot: o_in[slot]).astype(BF16)
    wo_copy = remote(wosend, worecv, sems, 43, q=1 - q)
    wo_copy.start()
    near = out_grad(lambda slot: o[rows_at(place(slot, q, 0), 2 * BLK), :])
    wo_copy.wait_recv()
    gwo_out[...] = (near + worecv[...].astype(F32)).astype(BF16)
    for copy in do_copies:
        copy.wait_recv()
    for copy in o_copies + [g_copy] + y_copies + dy_copies + do_copies + [wo_copy]:
        copy.wait_send()
    for slot in range(2):
        for array in range(2):
            for kind in range(3):
                hop(array, slot, kind).wait_send()
            for side in range(2):
                core_copy(array, side, slot).wait_send()
            chip_copy(array, slot).wait_send()
    for copy in waits:
        copy.wait()


def middle(o, x2, k2, modg, g_pair, wo, w_up, w_down, bias, consts, gmask):
    return pl.pallas_call(
        middle_kernel,
        out_shape=(
            shape_of(2 * BLK, D), shape_of(2 * BLK, D, dtype=F32), shape_of(SEQ, NH * HD),
            shape_of(GROUPS, 4 * D, dtype=F32), shape_of(8, D, dtype=F32), shape_of(D, D),
            shape_of(D, D), shape_of(NH * HD, D), shape_of(8, D, dtype=F32),
        ),
        in_specs=[VMEM_SPEC] * 6 + [ANY_SPEC] * 2 + [VMEM_SPEC] * 3,
        out_specs=(
            VMEM_SPEC, VMEM_SPEC, VMEM_SPEC, VMEM_SPEC, VMEM_SPEC, ANY_SPEC, ANY_SPEC, VMEM_SPEC,
            VMEM_SPEC,
        ),
        scratch_shapes=[
            pltpu.VMEM((2 * BLK, D), BF16),
            pltpu.VMEM((2, 2 * BLK, NH * HD), BF16),
            pltpu.VMEM((2 * BLK, D), F32),
            pltpu.VMEM((2, BLK, D), BF16),
            pltpu.VMEM((2, BLK, D), BF16),
            pltpu.VMEM((2 * BLK, D), F32),
            pltpu.VMEM((2 * BLK, D), F32),
            pltpu.VMEM((SEQ, D), BF16),
            pltpu.VMEM((SEQ, D), BF16),
            pltpu.VMEM((SEQ, D), BF16),
            pltpu.VMEM((SEQ, D), BF16),
            pltpu.VMEM((D, D), BF16),
            pltpu.VMEM((D, D), BF16),
            pltpu.VMEM((2, 2, 2, BLK, D), F32),
            pltpu.VMEM((2, 2, 2, BLK, D), BF16),
            pltpu.VMEM((2, 2, 2, BLK, D), BF16),
            pltpu.VMEM((2, 2, BLK, D), BF16),
            pltpu.VMEM((2, 2, BLK, D), BF16),
            pltpu.VMEM((2, 2, BLK, D), BF16),
            pltpu.VMEM((2, 2 * BLK, NH * HD), BF16),
            pltpu.VMEM((NH * HD, D), BF16),
            pltpu.VMEM((NH * HD, D), BF16),
            pltpu.SemaphoreType.DMA((44,)),
            pltpu.SemaphoreType.DMA((44,)),
            pltpu.SemaphoreType.DMA((5,)),
        ],
        compiler_params=pltpu.CompilerParams(
            collective_id=7, has_side_effects=True, vmem_limit_bytes=63 * 2**20
        ),
        name="middle",
    )(o, x2, k2, modg, g_pair, wo, w_up, w_down, bias, consts, gmask)


def swap(values, axis):
    return lax.ppermute(values, axis, SWAP)


def at_index(stacked, index):
    return lax.dynamic_index_in_dim(stacked, index, 0, keepdims=False)


def plane_gather(part, rank):
    half = 80
    by_x = swap(part, "x")
    by_y = swap(part, "y")
    far = jnp.concatenate([swap(by_x[:half], "y"), swap(by_y[half:], "x")], axis=0)
    out = jnp.zeros((4,) + part.shape, part.dtype)
    for k, block in enumerate((part, by_x, by_y, far)):
        out = lax.dynamic_update_index_in_dim(out, block, rank ^ k, 0)
    return out


def plane_scatter(parts, rank):
    half = 80
    rel = [at_index(parts, rank ^ k) for k in range(4)]
    low = [v[:, :half] for v in rel]
    high = [v[:, half:] for v in rel]
    in_x = swap(jnp.stack([low[1], low[3]]), "x").astype(F32)
    in_y = swap(jnp.stack([high[2], high[3]]), "y").astype(F32)
    low_own = low[0].astype(F32) + in_x[0]
    high_own = high[0].astype(F32) + in_y[0]
    low_rest = (low[2].astype(F32) + in_x[1]).astype(BF16)
    high_rest = (high[1].astype(F32) + in_y[1]).astype(BF16)
    low_own = low_own + swap(low_rest, "y").astype(F32)
    high_own = high_own + swap(high_rest, "x").astype(F32)
    return jnp.concatenate([low_own, high_own], axis=1)


def layer_device(
    tokens, cond, lengths, pads, timesteps, head_mask, group_mask, keep, ada_w, ada_b, w_qkv, b_qv,
    w_out, b_out, w_up, b_up, w_down, b_down, w_route, grad_out,
):
    highest = lax.Precision.HIGHEST
    y, x, p, q, c = (lax.axis_index(name) for name in "yxpqc")
    rank = y * 2 + x
    first = p == 0
    shard = p * 4 + q * 2 + c
    partner = shard ^ 4

    spread = np.zeros((6 * LANES, UNIT_ROWS), np.float32)
    for unit in range(6):
        spread[np.arange(HD) + unit * LANES, np.arange(HD) + unit * HD] = 1.0
    spread = jnp.asarray(spread, BF16)
    w_up_rows = jnp.transpose(w_up)
    w_a = jnp.concatenate([jnp.transpose(w_qkv), w_out])
    pairs = b_qv.reshape(2, 2, HD).astype(F32)
    bias_own = jnp.pad(
        jnp.stack([pairs[:, 0], jnp.zeros_like(pairs[:, 0]), pairs[:, 1]], axis=1),
        ((0, 0), (0, 0), (0, LANES - HD)),
    ).reshape(6 * LANES)
    bias_own = jnp.pad(jnp.concatenate([bias_own, b_up.astype(F32)]), (0, BIAS - 1344))
    bias_own = jnp.broadcast_to(bias_own, (8, BIAS))

    cvec = cond.astype(F32) + time_embed(timesteps)
    sig = lax.logistic(cvec)
    act_low = jnp.pad((cvec * sig).astype(BF16), ((0, 0), (0, 5), (0, 0)))
    mod_part = jnp.einsum("bcd,dm->bcm", act_low, ada_w, preferred_element_type=F32) + ada_b.astype(
        F32
    )
    def row_of(values):
        return jnp.where(first, values[0], values[1])

    row_len = row_of(lengths)
    row_pad = row_of(pads)
    ends = jnp.cumsum(row_len)
    starts = ends - row_len

    def group_hot(dq, dc):
        base = (q ^ dq) * (2 * BLK) + (c ^ dc) * BLK
        places = base + jnp.arange(2)[:, None] * HALF + jnp.arange(BLK // 16)[None, :] * 16
        inside = (places[..., None] >= starts) & (places[..., None] < ends)
        return jnp.pad(inside.astype(F32), ((0, 0), (0, 0), (0, 5)))

    hot = group_hot(0, 0)
    hot_rows = jnp.pad(hot.reshape(22, 16), ((0, 2), (0, 0)))

    def by_row(values):
        return jnp.transpose(values, (1, 0, 2))

    keep_wide = jnp.broadcast_to(keep.T.astype(BF16)[..., None], (2, BLK, LANES))
    triple, hidden_one, token_low, keep_low, mod_groups, w_wide, w_out_all, biases, act_all = front(
        mod_part, by_row(tokens), keep_wide, act_low, bias_own, w_a, spread, hot_rows
    )
    mod_rows = mod_groups[:22].reshape(2, BLK // 16, 6 * D)
    scale_one = mod_rows[:, :, None, D : 2 * D]

    def grouped(values):
        return values.reshape(2, BLK // 16, 16, -1)

    def flat(values):
        return values.reshape(2, BLK, -1)

    token_values = grouped(token_low.astype(F32))
    normed_one, inverse_one = norm_rows(token_values)

    def group_scatter(near_part, far_part):
        far_sum = (far_part[0].astype(F32) + swap(far_part[1], "c").astype(F32)).astype(BF16)
        far_in = swap(far_sum, "q")
        near_sum = near_part[0].astype(F32) + swap(near_part[1], "c").astype(F32)
        return near_sum + far_in.astype(F32)

    def split_chips(values):
        parts = values.reshape(2, 2, 2, BLK, -1)

        def chip(index):
            one = lax.dynamic_index_in_dim(parts, index, 1, keepdims=False)
            return jnp.stack(
                [
                    lax.dynamic_index_in_dim(one, c, 1, keepdims=False),
                    lax.dynamic_index_in_dim(one, 1 - c, 1, keepdims=False),
                ]
            )

        return chip(q), chip(1 - q)

    head_row = row_of(head_mask)
    heads_here = jnp.concatenate(
        [
            lax.dynamic_slice_in_dim(head_row, shard * 2, 2, 1),
            lax.dynamic_slice_in_dim(head_row, partner * 2, 2, 1),
        ],
        axis=1,
    )
    scal = jnp.concatenate(
        [
            starts,
            row_len // UNIT,
            row_len - row_pad,
            heads_here.reshape(-1),
        ]
    ).astype(jnp.int32)
    pack = np.zeros((NH * LANES, NH * HD), np.float32)
    for head in range(NH):
        pack[np.arange(HD) + head * LANES, np.arange(HD) + head * HD] = 1.0
    pack = jnp.asarray(pack, BF16)
    attended, lse = attn_fwd(scal, triple, pack)
    group_row = row_of(group_mask)
    groups_here = jnp.concatenate(
        [
            lax.dynamic_slice_in_dim(group_row, shard * 2, 2, 1),
            lax.dynamic_slice_in_dim(group_row, partner * 2, 2, 1),
        ],
        axis=1,
    ).astype(F32)
    all_places = jnp.arange(SEQ // 16)[:, None] * 16
    all_hot = ((all_places >= starts) & (all_places < ends)).astype(F32)
    group_wide = jnp.repeat(
        jnp.dot(all_hot, groups_here, precision=highest), GW, axis=1
    )
    consts = jnp.pad(jnp.stack([b_out, b_down, w_route]).astype(F32), ((0, 5), (0, 0)))
    b_up_two = jnp.concatenate([biases[0, :, 768:1344], biases[1, :, 768:1344]], axis=1)
    final, grad_mixed, grad_attended, sums_two, smalls, up_low, down_low, wo_low, b_up_sums = middle(
        attended, token_low.reshape(2 * BLK, D), keep_low.reshape(2 * BLK, LANES), mod_groups,
        by_row(grad_out), w_out_all.reshape(4 * QTR, D), w_up_rows, w_down, b_up_two, consts,
        group_wide,
    )
    grad_mixed = grouped(grad_mixed)
    d_all = attn_bwd(scal, triple, grad_attended, lse, pack)
    d_near, d_far = split_chips(jnp.dot(d_all, w_wide, preferred_element_type=F32).astype(BF16))
    dh1_near, dh1_far = d_near, d_far
    grad_hidden_one = grouped(group_scatter(dh1_near, dh1_far))

    def reduce_pair(mine, other):
        both = plane_scatter(jnp.stack([mine, other], axis=1), rank)
        total = both[0] + swap(both[1].astype(BF16), "p").astype(F32)
        return plane_gather(total.astype(BF16), rank).astype(F32)

    down_low = down_low.reshape(2, 4, QTR, D)
    up_low = up_low.reshape(2, 4, QTR, D)
    out_w_down = reduce_pair(down_low[0], down_low[1]).reshape(WROWS, D)
    out_w_up = jnp.transpose(reduce_pair(up_low[0], up_low[1]).reshape(WROWS, D))
    wide_low = tn(d_all, hidden_one).astype(BF16)
    a_low = [
        jnp.concatenate(
            [
                tn(spread, wide_low[k * 6 * LANES : (k + 1) * 6 * LANES]).astype(BF16),
                wo_low[k * 2 * HD : (k + 1) * 2 * HD],
            ]
        ).reshape(4, QTR, D)
        for k in range(2)
    ]
    out_a = reduce_pair(a_low[0], a_low[1]).reshape(WROWS, D)
    out_w_qkv = jnp.transpose(out_a[:UNIT_ROWS])
    out_w_out = out_a[UNIT_ROWS:]

    grad_tokens = flat(
        grad_mixed + norm_back(grad_hidden_one * (1.0 + scale_one), normed_one, inverse_one)
    )

    def from_rows(values, dtype):
        mine = jnp.where(first, values[0], values[1])
        other = swap(jnp.where(first, values[1], values[0]).astype(BF16), "p").astype(dtype)
        return jnp.stack(
            [jnp.where(first, mine, other), jnp.where(first, other, mine)], axis=1
        ).astype(dtype)

    out_final = from_rows(final.reshape(2, BLK, D), BF16)
    out_tokens = from_rows(grad_tokens, F32)

    group_sums = [jnp.sum(v, axis=2) for v in (grad_hidden_one, grad_hidden_one * normed_one)]
    group_sums.append(sums_two[:22].reshape(2, BLK // 16, 4 * D))
    part_mod = jnp.einsum(
        "sgc,sgm->cm", hot, jnp.concatenate(group_sums, axis=-1), precision=highest
    )[:CROPS]
    part_mod = jnp.transpose(part_mod.reshape(CROPS, 8, 6 * D // 8), (1, 0, 2))
    smalls = smalls[:3].reshape(3, 8, D // 8)
    smalls = jnp.pad(jnp.transpose(smalls, (1, 0, 2)), ((0, 0), (0, 0), (0, 5 * D // 8)))
    d_ones = jnp.sum(d_all, axis=0, dtype=F32)
    d_ones = d_ones.reshape(2, 2, 3, LANES)[..., :HD]
    qv_sums = jnp.stack([d_ones[:, :, 0], d_ones[:, :, 2]], axis=2).reshape(2, 4 * HD)
    bias_sums = jnp.concatenate([b_up_sums[0].reshape(2, 2 * GW), qv_sums], axis=1)
    who = jnp.arange(8)[:, None]
    bias_rows = jnp.where(
        who == shard, bias_sums[0], jnp.where(who == partner, bias_sums[1], 0.0)
    )
    parcel = jnp.concatenate(
        [part_mod, smalls, bias_rows[:, None], jnp.zeros((8, 1, 6 * D // 8), F32)], axis=1
    )
    parcels = line_exchange(parcel, "slice", 2, "dmod_exchange")
    line_sum = jnp.sum(parcels.reshape(2, 4, 16, 6 * D // 8), axis=1)
    line_low = line_sum.astype(BF16)
    mod_low = line_low[:, :CROPS]
    plane_low = plane_exchange(line_low, 4, "small_exchange")
    mod_all = plane_low[:, :, :CROPS]
    grad_ada_w = jnp.einsum(
        "rbcd,rbcm->dm", act_all[:, :, :CROPS], mod_all, preferred_element_type=F32
    )
    grad_ada_b = jnp.sum(mod_all, axis=(0, 1, 2), dtype=F32)
    rest = jnp.sum(plane_low[:, :, CROPS:], axis=(0, 1), dtype=F32)
    grad_b_out, grad_b_down, grad_w_route = (rest[k, : D // 8] for k in range(3))
    out_b_up = rest[3, : 2 * GW]
    out_b_qv = rest[3, 2 * GW :]
    part_activ = jnp.einsum("bcm,dm->bcd", mod_low, ada_w, preferred_element_type=F32)
    part_activ = jnp.pad(part_activ.astype(BF16), ((0, 0), (0, 5), (0, 0)))
    grad_activ = jnp.sum(
        line_exchange(part_activ, "all", 5, "cond_exchange").astype(F32), axis=0
    )[:, :CROPS]
    grad_cond = grad_activ * sig * (1.0 + cvec * (1.0 - sig))
    return (
        out_final, out_tokens, grad_cond, grad_ada_w, grad_ada_b, out_w_qkv, out_b_qv, out_w_out,
        grad_b_out, out_w_up, out_b_up, out_w_down, grad_b_down, grad_w_route,
    )


IN_SPECS = (
    ("heads", "rows", None), ("rows", None, None), ("rows", None), ("rows", None), ("rows", None),
    ("rows", None, None), ("rows", None, None), ("heads", "rows"), (None, "heads"), ("heads",),
    (None, "heads"), ("heads",), ("heads", None), (), (None, "heads"), ("heads",), ("heads", None),
    (), (), ("heads", "rows", None),
)
OUT_SPECS = (
    ("heads", "rows", None), ("heads", "rows", None), ("rows", None, None), (None, "heads"),
    ("heads",), (None, "heads"), ("heads",), ("heads", None), ("heads",), (None, "heads"),
    ("heads",), ("heads", None), ("heads",), ("heads",),
)


def solution(mesh):
    paired = mesh.shape["rows"] == 4 and mesh.shape["heads"] == 8
    if paired:
        mesh = Mesh(mesh.devices.reshape(2, 2, 2, 2, 2), ("y", "x", "p", "q", "c"))
        names = {"rows": ("y", "x"), "heads": ("p", "q", "c"), None: None}
    else:
        names = {"rows": "rows", "heads": "heads", None: None}

    def specs(items):
        return tuple(P(*(names[name] for name in item)) for item in items)

    return jax.shard_map(
        layer_device if paired else per_device,
        mesh=mesh,
        in_specs=specs(IN_SPECS),
        out_specs=specs(OUT_SPECS),
        check_vma=False,
    )
```

```python
import math

import jax
import jax.numpy as jnp
import numpy as np
from jax import lax
from jax.experimental import pallas as pl
from jax.experimental.pallas import tpu as pltpu
from jax.sharding import Mesh
from jax.sharding import PartitionSpec as P

D = 1152
H = 16
HD = 72
GW = 288
SEQ = 1408
CROPS = 11
UNIT = 64
LANES = 128
EPSILON = 1e-06
MASKED_SCORE = -1000000000.0
MESH = pl.DeviceIdType.MESH
SWAP = [(0, 1), (1, 0)]
F32 = jnp.float32
BF16 = jnp.bfloat16
SCALE = HD ** (-0.5)


def time_embed(timesteps):
    halves = D // 2
    frequency = jnp.exp(-math.log(10000.0) * jnp.arange(halves, dtype=jnp.float32) / halves)
    angles = timesteps.astype(jnp.float32)[..., None] * frequency
    return jnp.concatenate([jnp.cos(angles), jnp.sin(angles)], axis=-1)


def gelu_tanh(values):
    return (
        0.5
        * values
        * (1.0 + jnp.tanh(0.7978845608028654 * (values + 0.044715 * values * values * values)))
    )


def norm_rows(values):
    average = jnp.mean(values, axis=-1, keepdims=True)
    centred = values - average
    inverse_dev = lax.rsqrt(jnp.mean(centred * centred, axis=-1, keepdims=True) + EPSILON)
    return (centred * inverse_dev, inverse_dev)


def norm_back(grad_normed, normed, inverse_dev):
    first_mean = jnp.mean(grad_normed, axis=-1, keepdims=True)
    second_mean = jnp.mean(grad_normed * normed, axis=-1, keepdims=True)
    return inverse_dev * (grad_normed - first_mean - normed * second_mean)


def crop_layout(lengths, pads, offset, amount):
    crop_ends = jnp.cumsum(lengths, axis=1)
    starts = crop_ends - lengths
    places = offset + jnp.arange(amount, dtype=jnp.int32)
    inside = (places[:, None, None] >= starts[None]) & (places[:, None, None] < crop_ends[None])
    live_part = places[:, None, None] < (crop_ends - pads)[None]
    one_hot = inside.astype(jnp.float32)
    item_ids = jnp.sum(
        inside.astype(jnp.int32) * jnp.arange(lengths.shape[1], dtype=jnp.int32), axis=2
    )
    valid = jnp.sum((inside & live_part).astype(jnp.float32), axis=2)
    return (one_hot, item_ids, valid)


def masked_scores(queries, key_rows, item_row, key_live, score_scale):
    raw = jnp.einsum("shd,thd->hst", queries, key_rows, preferred_element_type=jnp.float32)
    allowed = (item_row[:, None] == item_row[None, :]) & key_live[None, :]
    return jnp.where(allowed[None], raw * score_scale, MASKED_SCORE)


def attend_row(triple_row, item_row, key_live, score_scale):
    queries = triple_row[:, :, 0]
    key_rows = triple_row[:, :, 1]
    values = triple_row[:, :, 2]
    scores = masked_scores(queries, key_rows, item_row, key_live, score_scale)
    row_top = jnp.max(scores, axis=-1, keepdims=True)
    log_total = row_top + jnp.log(jnp.sum(jnp.exp(scores - row_top), axis=-1, keepdims=True))
    probability = jnp.exp(scores - log_total).astype(jnp.bfloat16)
    attended = jnp.einsum("hst,thd->shd", probability, values, preferred_element_type=jnp.float32)
    return (attended, log_total)


def attend_back(triple_row, grad_row, total_row, item_row, key_live, score_scale):
    queries = triple_row[:, :, 0]
    key_rows = triple_row[:, :, 1]
    values = triple_row[:, :, 2]
    scores = masked_scores(queries, key_rows, item_row, key_live, score_scale)
    probability = jnp.exp(scores - total_row)
    grad_prob = jnp.einsum("shd,thd->hst", grad_row, values, preferred_element_type=jnp.float32)
    grad_values = jnp.einsum(
        "hst,shd->thd",
        probability.astype(jnp.bfloat16),
        grad_row,
        preferred_element_type=jnp.float32,
    )
    inner = jnp.sum(probability * grad_prob, axis=-1, keepdims=True)
    grad_raw = (probability * (grad_prob - inner) * score_scale).astype(jnp.bfloat16)
    grad_queries = jnp.einsum(
        "hst,thd->shd", grad_raw, key_rows, preferred_element_type=jnp.float32
    )
    grad_keys = jnp.einsum("hst,shd->thd", grad_raw, queries, preferred_element_type=jnp.float32)
    return jnp.stack([grad_queries, grad_keys, grad_values], axis=2).astype(jnp.bfloat16)


def project_rows(source, weight):
    return jnp.einsum("sbk,kd->sbd", source, weight, preferred_element_type=jnp.float32)


def back_rows(source, weight):
    return jnp.einsum("sbk,dk->sbd", source, weight, preferred_element_type=jnp.float32)


def per_device(
    tokens,
    cond,
    lengths,
    pads,
    timesteps,
    head_mask,
    group_mask,
    keep,
    ada_w,
    ada_b,
    w_qkv,
    b_qv,
    w_out,
    b_out,
    w_up,
    b_up,
    w_down,
    b_down,
    w_route,
    grad_out,
):
    highest = lax.Precision.HIGHEST
    groups = lax.axis_size("heads")
    head_rank = lax.axis_index("heads")
    shard_len = tokens.shape[0]
    batch_local = tokens.shape[1]
    local_heads = H // groups
    score_scale = HD ** (-0.5)
    local_hot, local_items, local_valid = crop_layout(
        lengths, pads, head_rank * shard_len, shard_len
    )
    full_hot, full_items, full_valid = crop_layout(lengths, pads, 0, SEQ)
    cond_all = cond.astype(jnp.float32) + time_embed(timesteps)
    sigmoid_cond = lax.logistic(cond_all)
    silu_low = (cond_all * sigmoid_cond).astype(jnp.bfloat16)
    modulation_part = jnp.einsum(
        "bcd,dm->bcm", silu_low, ada_w, preferred_element_type=jnp.float32
    ) + ada_b.astype(jnp.float32)
    modulation = lax.all_gather(modulation_part, "heads", axis=2, tiled=True)
    token_mod = jnp.einsum("sbc,bcm->sbm", local_hot, modulation, precision=highest)
    shift_one, scale_one, gate_one, shift_two, scale_two, gate_two = jnp.split(
        token_mod, 6, axis=-1
    )
    token_values = tokens.astype(jnp.float32)
    normed_one, inverse_one = norm_rows(token_values)
    hidden_one = (normed_one * (1.0 + scale_one) + shift_one).astype(jnp.bfloat16)
    hidden_all = lax.all_gather(hidden_one, "heads", axis=0, tiled=True)
    bias_pairs = b_qv.astype(jnp.float32).reshape(local_heads, 2, HD)
    bias_triple = jnp.stack(
        [bias_pairs[:, 0], jnp.zeros_like(bias_pairs[:, 0]), bias_pairs[:, 1]], axis=1
    ).reshape(-1)
    triple_all = (
        jnp.einsum("sbd,dm->sbm", hidden_all, w_qkv, preferred_element_type=jnp.float32)
        + bias_triple
    ).astype(jnp.bfloat16)
    triple_rows = jnp.moveaxis(triple_all.reshape(SEQ, batch_local, local_heads, 3, HD), 1, 0)
    item_rows = jnp.transpose(full_items)
    live_rows = jnp.transpose(full_valid > 0.5)
    attended, totals = lax.map(
        lambda packed: attend_row(packed[0], packed[1], packed[2], score_scale),
        (triple_rows, item_rows, live_rows),
    )
    head_table = lax.dynamic_slice_in_dim(
        head_mask, head_rank * local_heads, local_heads, 2
    ).astype(jnp.float32)
    head_full = jnp.einsum("sbc,bch->sbh", full_hot, head_table, precision=highest)
    out_mask = head_full * full_valid[..., None]
    attn_low = (
        (jnp.moveaxis(attended, 0, 1) * out_mask[..., None])
        .reshape(SEQ, batch_local, local_heads * HD)
        .astype(jnp.bfloat16)
    )
    projected = lax.psum_scatter(
        project_rows(attn_low, w_out), "heads", scatter_dimension=0, tiled=True
    )
    b_out_values = b_out.astype(jnp.float32)
    mixed = token_values + gate_one * (projected + b_out_values)
    normed_two, inverse_two = norm_rows(mixed)
    hidden_two = normed_two * (1.0 + scale_two) + shift_two
    hidden_two_low = hidden_two.astype(jnp.bfloat16)
    route_values = w_route.astype(jnp.float32)
    route = lax.logistic(jnp.einsum("sbd,d->sb", hidden_two, route_values, precision=highest))
    keep_values = keep.astype(jnp.float32)
    route_keep = keep_values * route
    group_table = lax.dynamic_slice_in_dim(
        group_mask, head_rank * local_heads, local_heads, 2
    ).astype(jnp.float32)
    hidden_two_all = lax.all_gather(hidden_two_low, "heads", axis=0, tiled=True)
    group_tok = jnp.einsum("sbc,bch->sbh", full_hot, group_table, precision=highest)
    upper = jnp.einsum(
        "sbd,dk->sbk", hidden_two_all, w_up, preferred_element_type=jnp.float32
    ) + b_up.astype(jnp.float32)
    active, gelu_back = jax.vjp(gelu_tanh, upper)
    group_wide = jnp.repeat(group_tok, GW, axis=-1)
    active_low = (active * group_wide).astype(jnp.bfloat16)
    lowered = lax.psum_scatter(
        project_rows(active_low, w_down), "heads", scatter_dimension=0, tiled=True
    )
    branch = lowered + b_down.astype(jnp.float32)
    final = mixed + gate_two * route_keep[..., None] * branch
    grad_final = grad_out.astype(jnp.float32)
    grad_branch = grad_final * gate_two * route_keep[..., None]
    grad_gate_two = grad_final * route_keep[..., None] * branch
    grad_route = jnp.sum(grad_final * gate_two * branch, axis=-1) * keep_values
    grad_logit = grad_route * route * (1.0 - route)
    part_route = jnp.einsum("sb,sbd->d", grad_logit, hidden_two, precision=highest)
    part_b_down = jnp.sum(grad_branch, axis=(0, 1))
    grad_low = grad_branch.astype(jnp.bfloat16)
    grad_all = lax.all_gather(grad_low, "heads", axis=0, tiled=True)
    grad_active = jnp.einsum("sbd,kd->sbk", grad_all, w_down, preferred_element_type=jnp.float32)
    (grad_upper,) = gelu_back(grad_active * group_wide)
    upper_low = grad_upper.astype(jnp.bfloat16)
    grad_w_up = jnp.einsum(
        "sbd,sbk->dk", hidden_two_all, upper_low, preferred_element_type=jnp.float32
    )
    grad_b_up = jnp.sum(upper_low, axis=(0, 1), dtype=jnp.float32)
    grad_w_down = jnp.einsum(
        "sbk,sbd->kd", active_low, grad_all, preferred_element_type=jnp.float32
    )
    grad_hidden_two = lax.psum_scatter(
        back_rows(upper_low, w_up), "heads", scatter_dimension=0, tiled=True
    )
    grad_hidden_two = grad_hidden_two + grad_logit[..., None] * route_values
    grad_scale_two = grad_hidden_two * normed_two
    grad_mixed = grad_final + norm_back(
        grad_hidden_two * (1.0 + scale_two), normed_two, inverse_two
    )
    grad_gate_one = grad_mixed * (projected + b_out_values)
    grad_projected = grad_mixed * gate_one
    part_b_out = jnp.sum(grad_projected, axis=(0, 1))
    projected_low = grad_projected.astype(jnp.bfloat16)
    grad_proj_all = lax.all_gather(projected_low, "heads", axis=0, tiled=True)
    grad_attn = jnp.einsum(
        "sbd,kd->sbk", grad_proj_all, w_out, preferred_element_type=jnp.float32
    ).astype(jnp.bfloat16)
    grad_w_out = jnp.einsum(
        "sbk,sbd->kd", attn_low, grad_proj_all, preferred_element_type=jnp.float32
    )
    grad_masked = grad_attn.reshape(SEQ, batch_local, local_heads, HD) * out_mask[..., None].astype(
        jnp.bfloat16
    )
    grad_rows = jnp.moveaxis(grad_masked, 1, 0)
    grad_triple_rows = lax.map(
        lambda packed: attend_back(
            packed[0], packed[1], packed[2], packed[3], packed[4], score_scale
        ),
        (triple_rows, grad_rows, totals, item_rows, live_rows),
    )
    grad_triple = jnp.moveaxis(grad_triple_rows, 0, 1).reshape(
        SEQ, batch_local, local_heads * 3 * HD
    )
    grad_w_qkv = jnp.einsum(
        "sbd,sbm->dm", hidden_all, grad_triple, preferred_element_type=jnp.float32
    )
    bias_sums = jnp.sum(grad_triple, axis=(0, 1), dtype=jnp.float32).reshape(local_heads, 3, HD)
    grad_b_qv = jnp.stack([bias_sums[:, 0], bias_sums[:, 2]], axis=1).reshape(-1)
    grad_hidden_one = lax.psum_scatter(
        back_rows(grad_triple, w_qkv), "heads", scatter_dimension=0, tiled=True
    )
    grad_tokens = grad_mixed + norm_back(
        grad_hidden_one * (1.0 + scale_one), normed_one, inverse_one
    )
    grad_token_mod = jnp.concatenate(
        [
            grad_hidden_one,
            grad_hidden_one * normed_one,
            grad_gate_one,
            grad_hidden_two,
            grad_scale_two,
            grad_gate_two,
        ],
        axis=-1,
    )
    part_mod = jnp.einsum("sbc,sbm->bcm", local_hot, grad_token_mod, precision=highest)
    grad_mod, share_b_out, share_b_down, share_route = (
        lax.psum_scatter(part_mod, "heads", scatter_dimension=2, tiled=True),
        lax.psum_scatter(part_b_out, "heads", scatter_dimension=0, tiled=True),
        lax.psum_scatter(part_b_down, "heads", scatter_dimension=0, tiled=True),
        lax.psum_scatter(part_route, "heads", scatter_dimension=0, tiled=True),
    )
    mod_low = grad_mod.astype(jnp.bfloat16)
    grad_ada_w = jnp.einsum("bcd,bcm->dm", silu_low, mod_low, preferred_element_type=jnp.float32)
    grad_ada_b = jnp.sum(mod_low, axis=(0, 1), dtype=jnp.float32)
    part_activ = jnp.einsum("bcm,dm->bcd", mod_low, ada_w, preferred_element_type=jnp.float32)
    grad_activ = lax.psum(part_activ.astype(jnp.bfloat16), "heads").astype(jnp.float32)
    grad_cond = grad_activ * sigmoid_cond * (1.0 + cond_all * (1.0 - sigmoid_cond))
    summed = (
        lax.psum(grad_ada_w.astype(jnp.bfloat16), "rows").astype(jnp.float32),
        lax.psum(grad_ada_b.astype(jnp.bfloat16), "rows").astype(jnp.float32),
        lax.psum(grad_w_qkv.astype(jnp.bfloat16), "rows").astype(jnp.float32),
        lax.psum(grad_b_qv.astype(jnp.bfloat16), "rows").astype(jnp.float32),
        lax.psum(grad_w_out.astype(jnp.bfloat16), "rows").astype(jnp.float32),
        lax.psum(share_b_out.astype(jnp.bfloat16), "rows").astype(jnp.float32),
        lax.psum(grad_w_up.astype(jnp.bfloat16), "rows").astype(jnp.float32),
        lax.psum(grad_b_up.astype(jnp.bfloat16), "rows").astype(jnp.float32),
        lax.psum(grad_w_down.astype(jnp.bfloat16), "rows").astype(jnp.float32),
        lax.psum(share_b_down.astype(jnp.bfloat16), "rows").astype(jnp.float32),
        lax.psum(share_route.astype(jnp.bfloat16), "rows").astype(jnp.float32),
    )
    return (
        final.astype(jnp.bfloat16),
        grad_tokens,
        grad_cond,
        summed[0],
        summed[1],
        summed[2],
        summed[3],
        summed[4],
        summed[5],
        summed[6],
        summed[7],
        summed[8],
        summed[9],
        summed[10],
    )


BLK = 176
NH = 4
HALF = SEQ // 2


def each_crop(scal, body):
    def step(item, carry):
        units = scal[CROPS + item]
        for count in range(2, 9):

            @pl.when(units == count)
            def _():
                body(item, pl.multiple_of(scal[item], UNIT), count * UNIT)

        return carry

    lax.fori_loop(0, CROPS, step, 0)


def nt(a, b):
    return lax.dot_general(a, b, (((1,), (1,)), ((), ())), preferred_element_type=F32)


def tn(a, b):
    return lax.dot_general(a, b, (((0,), (0,)), ((), ())), preferred_element_type=F32)


def attn_fwd_kernel(scal, buf, pack, obuf, lse):
    lane = lax.broadcasted_iota(jnp.int32, (1, LANES), 1)

    def body(item, start, size):
        live = scal[2 * CROPS + item]
        keys_live = lax.broadcasted_iota(jnp.int32, (1, size), 1) < live
        rows_live = (lax.broadcasted_iota(jnp.int32, (size, 1), 0) < live).astype(F32)
        window = pl.ds(start, size)
        packed = jnp.zeros((size, NH * HD), F32)
        totals = jnp.zeros((size, LANES), F32)
        for head in range(NH):
            at = head * 3 * LANES
            queries = buf[window, at : at + LANES]
            keys = buf[window, at + LANES : at + 2 * LANES]
            values = buf[window, at + 2 * LANES : at + 3 * LANES]
            scores = jnp.where(keys_live, nt(queries, keys) * SCALE, MASKED_SCORE)
            top = jnp.max(scores, axis=1, keepdims=True)
            expo = jnp.exp(scores - top)
            total = jnp.sum(expo, axis=1, keepdims=True)
            prob = (expo * (1.0 / total)).astype(BF16)
            mixed = jnp.dot(prob, values, preferred_element_type=F32)
            mask = scal[3 * CROPS + item * NH + head].astype(F32)
            mixed = (mixed * (rows_live * mask)).astype(BF16)
            packed += jnp.dot(
                mixed, pack[head * LANES : (head + 1) * LANES, :], preferred_element_type=F32
            )
            totals = jnp.where(lane == head, top + jnp.log(total), totals)
        obuf[window, :] = packed.astype(BF16)
        lse[window, :] = totals

    each_crop(scal, body)


def attn_bwd_kernel(scal, buf, gbuf, lse, pack, dbuf):
    def body(item, start, size):
        live = scal[2 * CROPS + item]
        keys_live = lax.broadcasted_iota(jnp.int32, (1, size), 1) < live
        rows_live = lax.broadcasted_iota(jnp.int32, (size, 1), 0) < live
        window = pl.ds(start, size)
        grads = gbuf[window, :]
        grads = jnp.where(rows_live, grads.astype(F32), 0.0).astype(BF16)
        for head in range(NH):
            at = head * 3 * LANES
            queries = buf[window, at : at + LANES]
            keys = buf[window, at + LANES : at + 2 * LANES]
            values = buf[window, at + 2 * LANES : at + 3 * LANES]
            mask = scal[3 * CROPS + item * NH + head].astype(F32)
            grad = (nt(grads, pack[head * LANES : (head + 1) * LANES, :]) * mask).astype(BF16)
            scores = jnp.where(keys_live, nt(queries, keys) * SCALE, MASKED_SCORE)
            prob = jnp.exp(scores - lse[window, head : head + 1])
            grad_prob = nt(grad, values)
            grad_values = tn(prob.astype(BF16), grad)
            inner = jnp.sum(prob * grad_prob, axis=1, keepdims=True)
            grad_raw = (prob * (grad_prob - inner) * SCALE).astype(BF16)
            dbuf[window, at : at + LANES] = jnp.dot(
                grad_raw, keys, preferred_element_type=F32
            ).astype(BF16)
            dbuf[window, at + LANES : at + 2 * LANES] = tn(grad_raw, queries).astype(BF16)
            dbuf[window, at + 2 * LANES : at + 3 * LANES] = grad_values.astype(BF16)

    each_crop(scal, body)


WIDE = NH * 3 * LANES
SMEM_SPEC = pl.BlockSpec(memory_space=pltpu.SMEM)
VMEM_SPEC = pl.BlockSpec(memory_space=pltpu.VMEM)
ANY_SPEC = pl.BlockSpec(memory_space=pl.ANY)


def attn_fwd(scal, triple, pack):
    return pl.pallas_call(
        attn_fwd_kernel,
        out_shape=(
            jax.ShapeDtypeStruct((SEQ, NH * HD), BF16),
            jax.ShapeDtypeStruct((SEQ, LANES), F32),
        ),
        in_specs=[SMEM_SPEC, VMEM_SPEC, VMEM_SPEC],
        out_specs=(VMEM_SPEC, VMEM_SPEC),
        compiler_params=pltpu.CompilerParams(vmem_limit_bytes=48 * 2**20),
        name="attn_fwd",
    )(scal, triple, pack)


def attn_bwd(scal, triple, grads, lse, pack):
    return pl.pallas_call(
        attn_bwd_kernel,
        out_shape=jax.ShapeDtypeStruct((SEQ, WIDE), BF16),
        in_specs=[SMEM_SPEC] + [VMEM_SPEC] * 4,
        out_specs=VMEM_SPEC,
        compiler_params=pltpu.CompilerParams(vmem_limit_bytes=48 * 2**20),
        name="attn_bwd",
    )(scal, triple, grads, lse, pack)


QTR = 144
WROWS = 576
BIAS = 1408
GROUPS = 24
UNIT_ROWS = 6 * HD
MODS = 6 * D // 8
CUT = 80


def remote(src, dst, sems, k, **where):
    return pltpu.make_async_remote_copy(
        src_ref=src,
        dst_ref=dst,
        send_sem=sems[0].at[k],
        recv_sem=sems[1].at[k],
        device_id=where,
        device_id_type=MESH,
    )


def greet(peers):
    barrier = pltpu.get_barrier_semaphore()
    for where in peers:
        pl.semaphore_signal(barrier, inc=1, device_id=where, device_id_type=MESH)
    pl.semaphore_wait(barrier, len(peers))


def line_peers(p, q, c):
    out = []
    for k in range(1, 8):
        out.append(
            {
                "p": lax.rem(p + k // 4, 2),
                "q": lax.rem(q + (k // 2) % 2, 2),
                "c": lax.rem(c + k % 2, 2),
            }
        )
    return out


def rows_at(start, size):
    return pl.ds(pl.multiple_of(start, 16), size)


class PlaneGather:
    def __init__(self, src, dst, sems, k, y, x, p):
        self.dst, self.sems, self.k, self.y, self.x = dst, sems, k, y, x
        self.rank = y * 2 + x
        mine = rows_at(self.rank * QTR, QTR)
        self.over = remote(src.at[mine], dst.at[mine], sems, k, p=1 - p)
        self.to_x = remote(dst.at[mine], dst.at[mine], sems, k + 1, x=1 - x)
        self.to_y = remote(dst.at[mine], dst.at[mine], sems, k + 2, y=1 - y)
        from_x = rows_at((y * 2 + 1 - x) * QTR, CUT)
        from_y = rows_at(((1 - y) * 2 + x) * QTR + CUT, QTR - CUT)
        self.on_y = remote(dst.at[from_x], dst.at[from_x], sems, k + 3, y=1 - y)
        self.on_x = remote(dst.at[from_y], dst.at[from_y], sems, k + 4, x=1 - x)

    def start(self):
        self.over.start()

    def spread(self):
        self.over.wait_recv()
        self.to_x.start()
        self.to_y.start()

    def forward(self):
        self.to_x.wait_recv()
        self.on_y.start()
        self.to_y.wait_recv()
        self.on_x.start()

    def finish(self):
        self.on_y.wait_recv()
        self.on_x.wait_recv()

    def sent(self):
        for copy in (self.over, self.to_x, self.to_y, self.on_y, self.on_x):
            copy.wait_send()


def norm_tile(values):
    average = jnp.mean(values, axis=1, keepdims=True)
    centred = values - average
    inverse = lax.rsqrt(jnp.mean(centred * centred, axis=1, keepdims=True) + EPSILON)
    return centred * inverse, inverse


def front_kernel(
    part, x_pair, k_pair, act, bias_own, w_a, spread, hot,
    t_out, h_out, x_out, k_out, modg_out, wide_out, wo_out, bias_out, act_out,
    mods, modg, h, wide, other_a, own_a, tbuf, send, recv, loc,
):
    y, x, p, q, c = (lax.axis_index(name) for name in "yxpqc")
    sems = (send, recv)
    pair = [
        {"q": lax.rem(q + k // 2, 2), "c": lax.rem(c + k % 2, 2)} for k in range(1, 4)
    ]
    plane = [{"y": lax.rem(y + k // 2, 2), "x": lax.rem(x + k % 2, 2)} for k in range(1, 4)]
    greet(pair + plane + [{"p": 1 - p}])
    rank = y * 2 + x
    waits = []

    def keep_local(src, dst, k):
        copy = pltpu.make_async_copy(src, dst, loc.at[k])
        copy.start()
        return copy

    def spot(pp, qq, cc):
        return pp * 4 + qq * 2 + cc

    mod_over = remote(part.at[1 - p], mods.at[spot(p, q, c)], sems, 0, p=1 - p)
    mod_over.start()
    bias_copy = remote(bias_own, bias_out.at[1], sems, 7, p=1 - p)
    bias_copy.start()
    x_copy = remote(x_pair.at[1 - p], x_out.at[p], sems, 8, p=1 - p)
    x_copy.start()
    k_copy = remote(k_pair.at[1 - p], k_out.at[p], sems, 9, p=1 - p)
    k_copy.start()
    take_a = PlaneGather(w_a, other_a, sems, 10, y, x, p)
    take_a.start()
    own_mod = keep_local(part.at[p], mods.at[spot(p, q, c)], 1)
    mod_own = []
    mod_far = []
    for k, where in enumerate(pair):
        mine = mods.at[spot(p, q, c)]
        copy = remote(part.at[p], mine, sems, 1 + k, **where)
        copy.start()
        mod_own.append(copy)
    load_a = keep_local(w_a, own_a, 0)
    waits.append(keep_local(x_pair.at[p], x_out.at[p], 2))
    waits.append(keep_local(k_pair.at[p], k_out.at[p], 3))
    waits.append(keep_local(bias_own, bias_out.at[0], 4))
    waits.append(keep_local(act, act_out.at[rank], 5))
    acts = []
    for k, where in enumerate(plane):
        copy = remote(act, act_out.at[rank], sems, 15 + k, **where)
        copy.start()
        acts.append(copy)
    mod_over.wait_recv()
    for k, where in enumerate(pair):
        far = mods.at[spot(1 - p, q, c)]
        copy = remote(far, far, sems, 4 + k, **where)
        copy.start()
        mod_far.append(copy)

    load_a.wait()
    wide[: 6 * LANES, :] = jnp.dot(
        spread[...], own_a[:UNIT_ROWS, :], preferred_element_type=F32
    ).astype(BF16)

    own_mod.wait()
    for copy in mod_own + mod_far:
        copy.wait_recv()
    full = jnp.concatenate([mods[k] for k in range(8)], axis=1)
    modg[...] = jnp.dot(
        hot[...], full, preferred_element_type=F32, precision=lax.Precision.HIGHEST
    )
    waits.append(keep_local(modg, modg_out, 6))

    def place(slot, chip, core):
        return slot * HALF + chip * (2 * BLK) + core * BLK

    def modulate(src, slot):
        base = place(slot, q, c)

        def group(g, carry):
            values = src[rows_at(g * 16, 16), :].astype(F32)
            normed, _ = norm_tile(values)
            row = slot * (BLK // 16) + g
            shift = modg[pl.ds(row, 1), 0:D]
            scale = modg[pl.ds(row, 1), D : 2 * D]
            h[rows_at(base + g * 16, 16), :] = (normed * (1.0 + scale) + shift).astype(BF16)
            return carry

        lax.fori_loop(0, BLK // 16, group, 0)

    def block(slot, chip, core):
        return h.at[rows_at(place(slot, chip, core), BLK)]

    hops = {}
    for i in range(2):
        slot = p if i == 0 else 1 - p
        mine = block(slot, q, c)
        other = block(slot, 1 - q, c)
        hops[i] = (
            remote(mine, mine, sems, 18 + 3 * i, q=1 - q),
            remote(mine, mine, sems, 19 + 3 * i, c=1 - c),
            remote(other, other, sems, 20 + 3 * i, c=1 - c),
        )

    modulate(x_pair.at[p], p)
    hops[0][0].start()
    hops[0][1].start()
    x_copy.wait_recv()
    modulate(x_out.at[1 - p], 1 - p)
    hops[1][0].start()
    hops[1][1].start()
    take_a.spread()
    bias_copy.wait_recv()
    for copy in waits[2:3]:
        copy.wait()
    hops[0][1].wait_recv()

    def project(slot, chip, half):
        rows = rows_at(place(slot, chip, 0), 2 * BLK)
        cols = slice(half * 6 * LANES, (half + 1) * 6 * LANES)
        line = bias_out[half, 0:1, : 6 * LANES]
        tbuf[rows, cols] = (nt(h[rows, :], wide[cols, :]) + line).astype(BF16)

    first, second = p, 1 - p
    project(first, q, 0)
    hops[0][0].wait_recv()
    hops[0][2].start()
    hops[1][1].wait_recv()
    project(second, q, 0)
    take_a.forward()
    hops[0][2].wait_recv()
    project(first, 1 - q, 0)
    hops[1][0].wait_recv()
    hops[1][2].start()
    take_a.finish()
    wide[6 * LANES :, :] = jnp.dot(
        spread[...], other_a[:UNIT_ROWS, :], preferred_element_type=F32
    ).astype(BF16)
    waits.append(keep_local(wide, wide_out, 7))
    tails = (own_a.at[UNIT_ROWS:], other_a.at[UNIT_ROWS:])
    outer = [remote(tails[k], wo_out.at[2 + k], sems, 24 + k, q=1 - q) for k in range(2)]
    for copy in outer:
        copy.start()
    for k in range(2):
        waits.append(keep_local(tails[k], wo_out.at[k], 8 + k))
    project(first, q, 1)
    project(second, q, 1)
    project(first, 1 - q, 1)
    hops[1][2].wait_recv()
    waits.append(keep_local(h, h_out, 10))
    project(second, 1 - q, 0)
    project(second, 1 - q, 1)
    waits.append(keep_local(tbuf, t_out, 11))
    for copy in outer + acts + [k_copy]:
        copy.wait_recv()
    for copy in [mod_over, bias_copy, x_copy, k_copy] + mod_own + mod_far + outer + acts:
        copy.wait_send()
    for i in range(2):
        for copy in hops[i]:
            copy.wait_send()
    take_a.sent()
    for k, copy in enumerate(waits):
        if k != 2:
            copy.wait()


def shape_of(*shape, dtype=BF16):
    return jax.ShapeDtypeStruct(shape, dtype)


def front(part, x_pair, k_pair, act, bias_own, w_a, spread, hot):
    return pl.pallas_call(
        front_kernel,
        out_shape=(
            shape_of(SEQ, WIDE), shape_of(SEQ, D), shape_of(2, BLK, D), shape_of(2, BLK, LANES),
            shape_of(GROUPS, 6 * D, dtype=F32), shape_of(WIDE, D), shape_of(4, QTR, D),
            shape_of(2, 8, BIAS, dtype=F32), shape_of(4, 2, 16, D),
        ),
        in_specs=[VMEM_SPEC] * 5 + [ANY_SPEC] + [VMEM_SPEC] * 2,
        out_specs=(
            ANY_SPEC, ANY_SPEC, VMEM_SPEC, VMEM_SPEC, ANY_SPEC, ANY_SPEC, ANY_SPEC, VMEM_SPEC,
            VMEM_SPEC,
        ),
        scratch_shapes=[
            pltpu.VMEM((8, 16, 6 * D // 8), F32),
            pltpu.VMEM((GROUPS, 6 * D), F32),
            pltpu.VMEM((SEQ, D), BF16),
            pltpu.VMEM((WIDE, D), BF16),
            pltpu.VMEM((WROWS, D), BF16),
            pltpu.VMEM((WROWS, D), BF16),
            pltpu.VMEM((SEQ, WIDE), BF16),
            pltpu.SemaphoreType.DMA((26,)),
            pltpu.SemaphoreType.DMA((26,)),
            pltpu.SemaphoreType.DMA((12,)),
        ],
        compiler_params=pltpu.CompilerParams(
            collective_id=6, has_side_effects=True, vmem_limit_bytes=56 * 2**20
        ),
        name="front",
    )(part, x_pair, k_pair, act, bias_own, w_a, spread, hot)


def gelu_both(u):
    cube = 0.044715 * u * u
    t = jnp.tanh(0.7978845608028654 * (u + cube * u))
    half = 0.5 * (1.0 + t)
    slope = half + 0.5 * u * (1.0 - t * t) * (0.7978845608028654 * (1.0 + 3.0 * cube))
    return u * half, slope


def middle_kernel(
    o, x2, k2, modg, g_pair, wo, w_up, w_down, bias, consts, gmask,
    final_out, dx_out, do_out, sums_out, small_out, up_out, down_out, gwo_out, bup_out,
    g2, o_in, ybig, ysend, yrecv, y1, mixed, h2, dz, act, du, wup, wdown,
    own, csend, crecv, qsend, qrecv, dy, dofar, wosend, worecv, send, recv, loc,
):
    y, x, p, q, c = (lax.axis_index(name) for name in "yxpqc")
    sems = (send, recv)
    greet([{"q": 1 - q}, {"c": 1 - c}, {"p": 1 - p}, {"x": 1 - x}, {"y": 1 - y}])
    waits = []

    def keep_local(src, dst, k):
        copy = pltpu.make_async_copy(src, dst, loc.at[k])
        copy.start()
        return copy

    def place(slot, chip, core):
        return slot * HALF + chip * (2 * BLK) + core * BLK

    o_copies = []
    for slot in range(2):
        copy = remote(
            o.at[rows_at(place(slot, 1 - q, 0), 2 * BLK)], o_in.at[slot], sems, slot, q=1 - q
        )
        copy.start()
        o_copies.append(copy)
    g_copy = remote(g_pair.at[1 - p], g2.at[pl.ds(p * BLK, BLK)], sems, 2, p=1 - p)
    g_copy.start()
    take_up = PlaneGather(w_up, wup.at[WROWS:], sems, 3, y, x, p)
    take_down = PlaneGather(w_down, wdown.at[WROWS:], sems, 8, y, x, p)
    take_up.start()
    take_down.start()
    own_g = keep_local(g_pair.at[p], g2.at[pl.ds(p * BLK, BLK)], 0)
    own_up = keep_local(w_up, wup.at[:WROWS], 1)
    own_down = keep_local(w_down, wdown.at[:WROWS], 2)

    y_copies = []
    for slot in range(2):
        rows = rows_at(place(slot, q, 0), 2 * BLK)
        o_copies[slot].wait_recv()
        ybig[...] = jnp.dot(o[rows, :], wo[0 : 2 * QTR, :], preferred_element_type=F32) + jnp.dot(
            o_in[slot], wo[2 * QTR : 4 * QTR, :], preferred_element_type=F32
        )
        ysend[slot] = ybig[rows_at((1 - c) * BLK, BLK), :].astype(BF16)
        y1[slot * BLK : (slot + 1) * BLK, :] = ybig[rows_at(c * BLK, BLK), :]
        copy = remote(ysend.at[slot], yrecv.at[slot], sems, 13 + slot, c=1 - c)
        copy.start()
        y_copies.append(copy)

    own_g.wait()
    g_copy.wait_recv()
    take_up.spread()
    b_out, b_down, w_route = consts[0:1, :], consts[1:2, :], consts[2:3, :]

    def routed(row):
        rows = rows_at(row * 16, 16)
        normed, inverse = norm_tile(mixed[rows, :])
        hidden = normed * (1.0 + modg[pl.ds(row, 1), 4 * D : 5 * D]) + modg[
            pl.ds(row, 1), 3 * D : 4 * D
        ]
        logit = jnp.sum(hidden * w_route, axis=1, keepdims=True)
        route = 1.0 / (1.0 + jnp.exp(-logit))
        kept = k2[rows, 0:1].astype(F32)
        return rows, normed, inverse, hidden, route, kept

    bufs = (h2, dz)

    def hop(array, slot, kind):
        mine = bufs[array].at[rows_at(place(slot, q, c), BLK)]
        far = bufs[array].at[rows_at(place(slot, 1 - q, c), BLK)]
        k = 15 + (slot * 2 + array) * 3 + kind
        if kind == 0:
            return remote(mine, mine, sems, k, q=1 - q)
        if kind == 1:
            return remote(mine, mine, sems, k, c=1 - c)
        return remote(far, far, sems, k, c=1 - c)

    for slot in range(2):
        y_copies[slot].wait_recv()

        def group(g, carry, slot=slot):
            row = slot * (BLK // 16) + g
            rows = rows_at(row * 16, 16)
            branch = y1[rows, :] + yrecv[slot, rows_at(g * 16, 16), :].astype(F32) + b_out
            y1[rows, :] = branch
            mixed[rows, :] = x2[rows, :].astype(F32) + modg[pl.ds(row, 1), 2 * D : 3 * D] * branch
            _, _, _, hidden, route, kept = routed(row)
            there = rows_at(place(slot, q, c) + g * 16, 16)
            h2[there, :] = hidden.astype(BF16)
            gate = modg[pl.ds(row, 1), 5 * D : 6 * D]
            dz[there, :] = (g2[rows, :].astype(F32) * gate * (kept * route)).astype(BF16)
            return carry

        lax.fori_loop(0, BLK // 16, group, 0)
        for array in range(2):
            hop(array, slot, 0).start()
            hop(array, slot, 1).start()

    take_up.forward()
    take_down.spread()
    own_up.wait()
    own_down.wait()
    take_up.finish()
    take_down.forward()
    take_down.finish()

    def core_copy(array, side, slot):
        k = 27 + (array * 2 + side) * 2 + slot
        return remote(csend.at[array, side, slot], crecv.at[array, side, slot], sems, k, c=1 - c)

    def chip_copy(array, slot):
        return remote(qsend.at[array, slot], qrecv.at[array, slot], sems, 35 + array * 2 + slot, q=1 - q)

    def far_out(slot):
        for array in range(2):
            core_copy(array, 1, slot).wait_recv()
            qsend[array, slot] = (
                own[array, 1, slot] + crecv[array, 1, slot].astype(F32)
            ).astype(BF16)
            chip_copy(array, slot).start()

    def feed(step, carry):
        side, slot = step // 2, lax.rem(step, 2)
        chip = lax.rem(q + side, 2)
        start = place(slot, chip, 0)

        @pl.when(step == 0)
        def _():
            for array in range(2):
                hop(array, 0, 1).wait_recv()

        @pl.when(step == 1)
        def _():
            for array in range(2):
                hop(array, 1, 1).wait_recv()

        @pl.when(step == 2)
        def _():
            for array in range(2):
                hop(array, 0, 0).wait_recv()
                hop(array, 0, 2).start()
            for array in range(2):
                hop(array, 0, 2).wait_recv()

        @pl.when(step == 3)
        def _():
            for array in range(2):
                hop(array, 1, 0).wait_recv()
                hop(array, 1, 2).start()
            far_out(0)
            for array in range(2):
                hop(array, 1, 2).wait_recv()

        def tile(part, carry):
            rows = rows_at(start + part * BLK, BLK)
            u = nt(h2[rows, :], wup[...]) + bias[0:1, :]
            value, slope = gelu_both(u)
            row0 = start // 16 + part * (BLK // 16)
            mask = jnp.concatenate(
                [
                    jnp.broadcast_to(gmask[pl.ds(row0 + k, 1), :], (16, D))
                    for k in range(BLK // 16)
                ],
                axis=0,
            )
            act[rows, :] = (value * mask).astype(BF16)
            da = nt(dz[rows, :], wdown[...])
            du[rows, :] = (slope * mask * da).astype(BF16)
            z_part = jnp.dot(act[rows, :], wdown[...], preferred_element_type=F32)
            h_part = jnp.dot(du[rows, :], wup[...], preferred_element_type=F32)

            @pl.when(part == c)
            def _():
                own[0, side, slot] = z_part
                own[1, side, slot] = h_part

            @pl.when(part != c)
            def _():
                csend[0, side, slot] = z_part.astype(BF16)
                csend[1, side, slot] = h_part.astype(BF16)

            return carry

        lax.fori_loop(0, 2, tile, 0)
        for array in range(2):
            core_copy(array, side, slot).start()
        return carry

    lax.fori_loop(0, 4, feed, 0)
    far_out(1)

    for copy in (take_up, take_down):
        copy.sent()

    def weight_chunk(j, carry):
        cols = pl.ds(pl.multiple_of(j * 384, LANES), 384)
        rows = rows_at(j * 384, 384)
        wup[rows, :] = tn(du[:, cols], h2[...]).astype(BF16)
        wdown[rows, :] = tn(act[:, cols], dz[...]).astype(BF16)
        return carry

    lax.fori_loop(0, 3, weight_chunk, 0)
    waits.append(keep_local(wup, up_out, 3))
    waits.append(keep_local(wdown, down_out, 4))
    bup_out[...] = jnp.dot(jnp.ones((8, SEQ), BF16), du[...], preferred_element_type=F32)

    small_out[...] = jnp.zeros_like(small_out)
    sums_out[22:24, :] = jnp.zeros((2, 4 * D), F32)
    dy_copies = []
    do_copies = []
    for slot in range(2):
        for array in range(2):
            core_copy(array, 0, slot).wait_recv()
            chip_copy(array, slot).wait_recv()

        def back(g, carry, slot=slot):
            row = slot * (BLK // 16) + g
            rows, normed, inverse, hidden, route, kept = routed(row)
            here = rows_at(g * 16, 16)

            def total(array):
                return (
                    own[array, 0, slot, here, :]
                    + crecv[array, 0, slot, here, :].astype(F32)
                    + qrecv[array, slot, here, :].astype(F32)
                )

            gate_one = modg[pl.ds(row, 1), 2 * D : 3 * D]
            gate_two = modg[pl.ds(row, 1), 5 * D : 6 * D]
            scale_two = modg[pl.ds(row, 1), 4 * D : 5 * D]
            grad = g2[rows, :].astype(F32)
            pass_on = kept * route
            branch = total(0) + b_down
            final_out[rows, :] = (mixed[rows, :] + gate_two * pass_on * branch).astype(BF16)
            grad_gate_two = grad * pass_on * branch
            gated = grad * gate_two
            logit = (
                jnp.sum(gated * branch, axis=1, keepdims=True) * kept * route * (1.0 - route)
            )
            dh = total(1) + logit * w_route
            e = dh * (1.0 + scale_two)
            dx = grad + inverse * (
                e
                - jnp.mean(e, axis=1, keepdims=True)
                - normed * jnp.mean(e * normed, axis=1, keepdims=True)
            )
            dx_out[rows, :] = dx
            dyb = dx * gate_one
            dy[slot, c, here, :] = dyb.astype(BF16)

            def down(v):
                return jnp.sum(v, axis=0, keepdims=True)

            small_out[0:1, :] += down(dyb)
            small_out[1:2, :] += down(gated * pass_on)
            small_out[2:3, :] += down(logit * hidden)
            at = pl.ds(row, 1)
            sums_out[at, 0:D] = down(dx * y1[rows, :])
            sums_out[at, D : 2 * D] = down(dh)
            sums_out[at, 2 * D : 3 * D] = down(dh * normed)
            sums_out[at, 3 * D : 4 * D] = down(grad_gate_two)
            return carry

        lax.fori_loop(0, BLK // 16, back, 0)
        copy = remote(dy.at[slot, c], dy.at[slot, c], sems, 39 + slot, c=1 - c)
        copy.start()
        dy_copies.append(copy)
    for slot in range(2):
        dy_copies[slot].wait_recv()
        rows = rows_at(place(slot, q, 0), 2 * BLK)
        grads = dy[slot].reshape(2 * BLK, D)
        dofar[slot] = nt(grads, wo[2 * QTR : 4 * QTR, :]).astype(BF16)
        copy = remote(dofar.at[slot], do_out.at[rows], sems, 41 + slot, q=1 - q)
        copy.start()
        do_copies.append(copy)
        do_out[rows, :] = nt(grads, wo[0 : 2 * QTR, :]).astype(BF16)

    def out_grad(left):
        return sum(tn(left(slot), dy[slot].reshape(2 * BLK, D)) for slot in range(2))

    wosend[...] = out_grad(lambda slot: o_in[slot]).astype(BF16)
    wo_copy = remote(wosend, worecv, sems, 43, q=1 - q)
    wo_copy.start()
    near = out_grad(lambda slot: o[rows_at(place(slot, q, 0), 2 * BLK), :])
    wo_copy.wait_recv()
    gwo_out[...] = (near + worecv[...].astype(F32)).astype(BF16)
    for copy in do_copies:
        copy.wait_recv()
    for copy in o_copies + [g_copy] + y_copies + dy_copies + do_copies + [wo_copy]:
        copy.wait_send()
    for slot in range(2):
        for array in range(2):
            for kind in range(3):
                hop(array, slot, kind).wait_send()
            for side in range(2):
                core_copy(array, side, slot).wait_send()
            chip_copy(array, slot).wait_send()
    for copy in waits:
        copy.wait()


def middle(o, x2, k2, modg, g_pair, wo, w_up, w_down, bias, consts, gmask):
    return pl.pallas_call(
        middle_kernel,
        out_shape=(
            shape_of(2 * BLK, D), shape_of(2 * BLK, D, dtype=F32), shape_of(SEQ, NH * HD),
            shape_of(GROUPS, 4 * D, dtype=F32), shape_of(8, D, dtype=F32), shape_of(D, D),
            shape_of(D, D), shape_of(NH * HD, D), shape_of(8, D, dtype=F32),
        ),
        in_specs=[VMEM_SPEC] * 6 + [ANY_SPEC] * 2 + [VMEM_SPEC] * 3,
        out_specs=(
            VMEM_SPEC, VMEM_SPEC, VMEM_SPEC, VMEM_SPEC, VMEM_SPEC, ANY_SPEC, ANY_SPEC, VMEM_SPEC,
            VMEM_SPEC,
        ),
        scratch_shapes=[
            pltpu.VMEM((2 * BLK, D), BF16),
            pltpu.VMEM((2, 2 * BLK, NH * HD), BF16),
            pltpu.VMEM((2 * BLK, D), F32),
            pltpu.VMEM((2, BLK, D), BF16),
            pltpu.VMEM((2, BLK, D), BF16),
            pltpu.VMEM((2 * BLK, D), F32),
            pltpu.VMEM((2 * BLK, D), F32),
            pltpu.VMEM((SEQ, D), BF16),
            pltpu.VMEM((SEQ, D), BF16),
            pltpu.VMEM((SEQ, D), BF16),
            pltpu.VMEM((SEQ, D), BF16),
            pltpu.VMEM((D, D), BF16),
            pltpu.VMEM((D, D), BF16),
            pltpu.VMEM((2, 2, 2, BLK, D), F32),
            pltpu.VMEM((2, 2, 2, BLK, D), BF16),
            pltpu.VMEM((2, 2, 2, BLK, D), BF16),
            pltpu.VMEM((2, 2, BLK, D), BF16),
            pltpu.VMEM((2, 2, BLK, D), BF16),
            pltpu.VMEM((2, 2, BLK, D), BF16),
            pltpu.VMEM((2, 2 * BLK, NH * HD), BF16),
            pltpu.VMEM((NH * HD, D), BF16),
            pltpu.VMEM((NH * HD, D), BF16),
            pltpu.SemaphoreType.DMA((44,)),
            pltpu.SemaphoreType.DMA((44,)),
            pltpu.SemaphoreType.DMA((5,)),
        ],
        compiler_params=pltpu.CompilerParams(
            collective_id=7, has_side_effects=True, vmem_limit_bytes=63 * 2**20
        ),
        name="middle",
    )(o, x2, k2, modg, g_pair, wo, w_up, w_down, bias, consts, gmask)


class PlaneReduce:
    def __init__(self, grads, bufs, sems, k, y, x):
        self.grads, self.y, self.x = grads, y, x
        self.low_in, self.high_in, self.low_out, self.high_out, self.low_end, self.high_end = bufs
        self.first = [
            remote(grads.at[:, self.low(y, 1 - x)], self.low_in.at[0], sems, k, x=1 - x),
            remote(grads.at[:, self.low(1 - y, 1 - x)], self.low_in.at[1], sems, k + 1, x=1 - x),
            remote(grads.at[:, self.high(1 - y, x)], self.high_in.at[0], sems, k + 2, y=1 - y),
            remote(grads.at[:, self.high(1 - y, 1 - x)], self.high_in.at[1], sems, k + 3, y=1 - y),
        ]
        self.second = [
            remote(self.low_out, self.low_end, sems, k + 4, y=1 - y),
            remote(self.high_out, self.high_end, sems, k + 5, x=1 - x),
        ]

    def low(self, y, x):
        return rows_at((y * 2 + x) * QTR, CUT)

    def high(self, y, x):
        return rows_at((y * 2 + x) * QTR + CUT, QTR - CUT)

    def start(self):
        for copy in self.first:
            copy.start()

    def middle(self):
        y, x = self.y, self.x
        for copy in self.first:
            copy.wait_recv()
        for shard in range(2):
            self.low_out[shard] = (
                self.grads[shard, self.low(1 - y, x), :].astype(F32)
                + self.low_in[1, shard].astype(F32)
            ).astype(BF16)
            self.high_out[shard] = (
                self.grads[shard, self.high(y, 1 - x), :].astype(F32)
                + self.high_in[1, shard].astype(F32)
            ).astype(BF16)
        for copy in self.second:
            copy.start()

    def arrive(self):
        for copy in self.second:
            copy.wait_recv()

    def total(self, shard):
        low = (
            self.grads[shard, self.low(self.y, self.x), :].astype(F32)
            + self.low_in[0, shard].astype(F32)
            + self.low_end[shard].astype(F32)
        )
        high = (
            self.grads[shard, self.high(self.y, self.x), :].astype(F32)
            + self.high_in[0, shard].astype(F32)
            + self.high_end[shard].astype(F32)
        )
        return low, high

    def sent(self):
        for copy in self.first + self.second:
            copy.wait_send()


REDUCE_SCRATCH = [
    pltpu.VMEM((2, 2, CUT, D), BF16),
    pltpu.VMEM((2, 2, QTR - CUT, D), BF16),
    pltpu.VMEM((2, CUT, D), BF16),
    pltpu.VMEM((2, QTR - CUT, D), BF16),
    pltpu.VMEM((2, CUT, D), BF16),
    pltpu.VMEM((2, QTR - CUT, D), BF16),
]


class LineReduce:
    def __init__(self, reduce, half, out, sems, k, y, x, p):
        self.reduce, self.half, self.out = reduce, half, out
        self.mine = rows_at((y * 2 + x) * QTR, QTR)
        self.over = remote(half.at[0], half.at[1], sems, k, p=1 - p)
        mine = out.at[self.mine]
        self.to_x = remote(mine, mine, sems, k + 1, x=1 - x)
        self.to_y = remote(mine, mine, sems, k + 2, y=1 - y)
        from_x = out.at[rows_at((y * 2 + 1 - x) * QTR, CUT)]
        from_y = out.at[rows_at(((1 - y) * 2 + x) * QTR + CUT, QTR - CUT)]
        self.on_y = remote(from_x, from_x, sems, k + 3, y=1 - y)
        self.on_x = remote(from_y, from_y, sems, k + 4, x=1 - x)

    def start(self):
        self.reduce.arrive()
        low, high = self.reduce.total(1)
        self.half[0, :CUT] = low.astype(BF16)
        self.half[0, CUT:] = high.astype(BF16)
        self.over.start()

    def spread(self):
        low, high = self.reduce.total(0)
        self.over.wait_recv()
        start = (self.reduce.y * 2 + self.reduce.x) * QTR
        self.out[rows_at(start, CUT), :] = (low + self.half[1, :CUT].astype(F32)).astype(BF16)
        self.out[rows_at(start + CUT, QTR - CUT), :] = (
            high + self.half[1, CUT:].astype(F32)
        ).astype(BF16)
        self.to_x.start()
        self.to_y.start()

    def forward(self):
        self.to_x.wait_recv()
        self.on_y.start()
        self.to_y.wait_recv()
        self.on_x.start()

    def finish(self):
        self.on_y.wait_recv()
        self.on_x.wait_recv()

    def sent(self):
        for copy in (self.over, self.to_x, self.to_y, self.on_y, self.on_x):
            copy.wait_send()


def back_kernel(
    d, h1, wide, x2, dx, scale, sums_two, smalls, b_up, up_g, down_g, wo_g, hot, spread, final,
    ada, slope,
    final_out, tokens_out, a_out, up_out, down_out, mod_out, cond_out,
    own, csend, crecv, qsend, qrecv, wideg, grads, sums, parcel, parcels, modline, condbuf,
    tsend, halves, *rest,
):
    bufs = [rest[0:6], rest[6:12], rest[12:18]]
    send, recv, loc = rest[18:]
    y, x, p, q, c = (lax.axis_index(name) for name in "yxpqc")
    sems = (send, recv)
    line = line_peers(p, q, c)
    plane = [{"y": lax.rem(y + k // 2, 2), "x": lax.rem(x + k % 2, 2)} for k in range(1, 4)]
    greet(line + plane)
    rank = y * 2 + x
    me = p * 4 + q * 2 + c

    def keep_local(src, dst, k):
        copy = pltpu.make_async_copy(src, dst, loc.at[k])
        copy.start()
        return copy

    def place(slot, chip, core):
        return slot * HALF + chip * (2 * BLK) + core * BLK

    outs = (down_out, up_out, a_out)
    reduces = [PlaneReduce(grads.at[k], bufs[k], sems, 6 * k, y, x) for k in range(3)]
    lines = [
        LineReduce(reduces[k], halves.at[k], outs[k], sems, 18 + 5 * k, y, x, p) for k in range(3)
    ]
    loads = [keep_local(down_g, grads.at[0], 0), keep_local(up_g, grads.at[1], 1)]
    for k in range(2):
        loads[k].wait()
        reduces[k].start()
    final_copy = remote(
        final.at[pl.ds(pl.multiple_of((1 - p) * BLK, 16), BLK)], final_out.at[p], sems, 33, p=1 - p
    )
    own_final = keep_local(
        final.at[pl.ds(pl.multiple_of(p * BLK, 16), BLK)], final_out.at[p], 2
    )

    def core_copy(side, slot):
        return remote(
            csend.at[side, slot], crecv.at[side, slot], sems, 34 + side * 2 + slot, c=1 - c
        )

    def chip_copy(slot):
        return remote(qsend.at[slot], qrecv.at[slot], sems, 38 + slot, q=1 - q)

    def far_out(slot):
        core_copy(1, slot).wait_recv()
        qsend[slot] = (own[1, slot] + crecv[1, slot].astype(F32)).astype(BF16)
        chip_copy(slot).start()

    def through(step, carry):
        side, slot = 1 - step // 2, lax.rem(step, 2)
        start = place(slot, lax.rem(q + side, 2), 0)
        rows = rows_at(start, 2 * BLK)
        part = jnp.dot(d[rows, :], wide[...], preferred_element_type=F32)

        @pl.when(c == 0)
        def _():
            own[side, slot] = part[:BLK]
            csend[side, slot] = part[BLK:].astype(BF16)

        @pl.when(c == 1)
        def _():
            own[side, slot] = part[BLK:]
            csend[side, slot] = part[:BLK].astype(BF16)

        core_copy(side, slot).start()

        @pl.when(step == 1)
        def _():
            far_out(0)

        @pl.when(step == 2)
        def _():
            far_out(1)

        return carry

    lax.fori_loop(0, 4, through, 0)

    def weight_chunk(j, carry):
        cols = pl.ds(pl.multiple_of(j * 384, LANES), 384)
        wideg[rows_at(j * 384, 384), :] = tn(d[:, cols], h1[...]).astype(BF16)
        return carry

    lax.fori_loop(0, 4, weight_chunk, 0)
    for shard in range(2):
        grads[2, shard, :UNIT_ROWS, :] = tn(
            spread[...], wideg[shard * 6 * LANES : (shard + 1) * 6 * LANES, :]
        ).astype(BF16)
        grads[2, shard, UNIT_ROWS:, :] = wo_g[shard * QTR : (shard + 1) * QTR, :]
    reduces[2].start()
    ones = jnp.ones((8, SEQ), BF16)
    col_sums = jnp.dot(ones, d[...], preferred_element_type=F32)
    reduces[0].middle()
    final_copy.start()

    sums[...] = jnp.zeros_like(sums)
    for slot in range(2):
        core_copy(0, slot).wait_recv()
        chip_copy(slot).wait_recv()

        def group(g, carry, slot=slot):
            row = slot * (BLK // 16) + g
            rows = rows_at(row * 16, 16)
            here = rows_at(g * 16, 16)
            normed, inverse = norm_tile(x2[rows, :].astype(F32))
            dh = (
                own[0, slot, here, :]
                + crecv[0, slot, here, :].astype(F32)
                + qrecv[slot, here, :].astype(F32)
            )
            at = pl.ds(row, 1)
            e = dh * (1.0 + scale[at, :])
            out = dx[rows, :] + inverse * (
                e
                - jnp.mean(e, axis=1, keepdims=True)
                - normed * jnp.mean(e * normed, axis=1, keepdims=True)
            )
            tsend[slot, here, :] = out.astype(BF16)

            @pl.when(slot == p)
            def _():
                tokens_out[p, here, :] = out

            sums[at, 0:D] = jnp.sum(dh, axis=0, keepdims=True)
            sums[at, D : 2 * D] = jnp.sum(dh * normed, axis=0, keepdims=True)
            return carry

        lax.fori_loop(0, BLK // 16, group, 0)

    token_copy = remote(tsend.at[1 - p], tsend.at[2], sems, 40, p=1 - p)

    two = jnp.concatenate([sums[...], sums_two[...]], axis=1)
    full = lax.dot_general(
        hot[...], two, (((0,), (0,)), ((), ())), preferred_element_type=F32,
        precision=lax.Precision.HIGHEST,
    )
    for k in range(8):
        parcel[k] = full[:, k * MODS : (k + 1) * MODS]
        parcel[k, 11:14, : D // 8] = smalls[0:3, k * (D // 8) : (k + 1) * (D // 8)]
    for shard in range(2):
        heads = col_sums[0:1, shard * 6 * LANES : (shard + 1) * 6 * LANES]
        pieces = [b_up[0:1, shard * WROWS : (shard + 1) * WROWS]]
        for unit in (0, 2, 3, 5):
            pieces.append(heads[:, unit * LANES : unit * LANES + HD])
        owner = lax.rem(p + shard, 2) * 4 + q * 2 + c
        parcel[owner, 14:15, :] = jnp.concatenate(pieces, axis=1)
    copies = []
    for k, where in enumerate(line):
        copy = remote(
            parcel.at[where["p"] * 4 + where["q"] * 2 + where["c"]], parcels.at[me], sems, 41 + k,
            **where,
        )
        copy.start()
        copies.append(copy)
    own_parcel = keep_local(parcel.at[me], parcels.at[me], 3)
    token_copy.start()
    reduces[1].middle()
    lines[0].start()
    own_parcel.wait()
    for copy in copies:
        copy.wait_recv()
    for row in range(2):
        modline[row] = sum(parcels[row * 4 + k] for k in range(4)).astype(BF16)
    mods = []
    for k, where in enumerate(plane):
        copy = remote(modline, mod_out.at[rank], sems, 48 + k, **where)
        copy.start()
        mods.append(copy)
    own_mod = keep_local(modline, mod_out.at[rank], 4)

    condbuf[0] = jnp.dot(
        modline[...].reshape(32, MODS), ada[...], preferred_element_type=F32
    ).astype(BF16)
    conds = []
    for k, where in enumerate(({"c": 1 - c}, {"q": 1 - q}, {"p": 1 - p})):
        copy = remote(condbuf.at[2 * k], condbuf.at[2 * k + 1], sems, 51 + k, **where)
        copy.start()
        conds.append(copy)
        if k == 0:
            reduces[2].middle()
        if k == 1:
            lines[1].start()
        if k == 2:
            lines[0].spread()
        copy.wait_recv()
        total = condbuf[2 * k].astype(F32) + condbuf[2 * k + 1].astype(F32)
        if k < 2:
            condbuf[2 * k + 2] = total.astype(BF16)
    cond_out[...] = total * slope[...]

    lines[2].start()
    lines[0].forward()
    lines[1].spread()
    token_copy.wait_recv()
    tokens_out[1 - p] = tsend[2].astype(F32)
    lines[0].finish()
    lines[1].forward()
    lines[2].spread()
    lines[1].finish()
    lines[2].forward()
    lines[2].finish()
    final_copy.wait_recv()
    for copy in mods:
        copy.wait_recv()
    for copy in [final_copy, token_copy] + copies + mods + conds:
        copy.wait_send()
    for slot in range(2):
        for side in range(2):
            core_copy(side, slot).wait_send()
        chip_copy(slot).wait_send()
    for k in range(3):
        reduces[k].sent()
        lines[k].sent()
    own_final.wait()
    own_mod.wait()


def back(d, h1, wide, x2, dx, scale, sums_two, smalls, b_up, up_g, down_g, wo_g, hot, spread, final, ada, slope):
    return pl.pallas_call(
        back_kernel,
        out_shape=(
            shape_of(2, BLK, D), shape_of(2, BLK, D, dtype=F32), shape_of(WROWS, D),
            shape_of(WROWS, D), shape_of(WROWS, D), shape_of(4, 2, 16, MODS),
            shape_of(32, D, dtype=F32),
        ),
        in_specs=[VMEM_SPEC] * 9 + [ANY_SPEC] * 2 + [VMEM_SPEC] * 6,
        out_specs=(VMEM_SPEC,) * 7,
        scratch_shapes=[
            pltpu.VMEM((2, 2, BLK, D), F32),
            pltpu.VMEM((2, 2, BLK, D), BF16),
            pltpu.VMEM((2, 2, BLK, D), BF16),
            pltpu.VMEM((2, BLK, D), BF16),
            pltpu.VMEM((2, BLK, D), BF16),
            pltpu.VMEM((WIDE, D), BF16),
            pltpu.VMEM((3, 2, WROWS, D), BF16),
            pltpu.VMEM((GROUPS, 2 * D), F32),
            pltpu.VMEM((8, 16, MODS), F32),
            pltpu.VMEM((8, 16, MODS), F32),
            pltpu.VMEM((2, 16, MODS), BF16),
            pltpu.VMEM((6, 32, D), BF16),
            pltpu.VMEM((3, BLK, D), BF16),
            pltpu.VMEM((3, 2, QTR, D), BF16),
        ]
        + REDUCE_SCRATCH * 3
        + [
            pltpu.SemaphoreType.DMA((54,)),
            pltpu.SemaphoreType.DMA((54,)),
            pltpu.SemaphoreType.DMA((5,)),
        ],
        compiler_params=pltpu.CompilerParams(
            collective_id=8, has_side_effects=True, vmem_limit_bytes=63 * 2**20
        ),
        name="back",
    )(d, h1, wide, x2, dx, scale, sums_two, smalls, b_up, up_g, down_g, wo_g, hot, spread, final, ada, slope)


def layer_device(
    tokens, cond, lengths, pads, timesteps, head_mask, group_mask, keep, ada_w, ada_b, w_qkv, b_qv,
    w_out, b_out, w_up, b_up, w_down, b_down, w_route, grad_out,
):
    highest = lax.Precision.HIGHEST
    y, x, p, q, c = (lax.axis_index(name) for name in "yxpqc")
    rank = y * 2 + x
    first = p == 0
    shard = p * 4 + q * 2 + c
    partner = shard ^ 4

    spread = np.zeros((6 * LANES, UNIT_ROWS), np.float32)
    for unit in range(6):
        spread[np.arange(HD) + unit * LANES, np.arange(HD) + unit * HD] = 1.0
    spread = jnp.asarray(spread, BF16)
    w_up_rows = jnp.transpose(w_up)
    w_a = jnp.concatenate([jnp.transpose(w_qkv), w_out])
    pairs = b_qv.reshape(2, 2, HD).astype(F32)
    bias_own = jnp.pad(
        jnp.stack([pairs[:, 0], jnp.zeros_like(pairs[:, 0]), pairs[:, 1]], axis=1),
        ((0, 0), (0, 0), (0, LANES - HD)),
    ).reshape(6 * LANES)
    bias_own = jnp.pad(jnp.concatenate([bias_own, b_up.astype(F32)]), (0, BIAS - 1344))
    bias_own = jnp.broadcast_to(bias_own, (8, BIAS))

    cvec = cond.astype(F32) + time_embed(timesteps)
    sig = lax.logistic(cvec)
    act_low = jnp.pad((cvec * sig).astype(BF16), ((0, 0), (0, 5), (0, 0)))
    mod_part = jnp.einsum("bcd,dm->bcm", act_low, ada_w, preferred_element_type=F32) + ada_b.astype(
        F32
    )
    def row_of(values):
        return jnp.where(first, values[0], values[1])

    row_len = row_of(lengths)
    row_pad = row_of(pads)
    ends = jnp.cumsum(row_len)
    starts = ends - row_len

    def group_hot(dq, dc):
        base = (q ^ dq) * (2 * BLK) + (c ^ dc) * BLK
        places = base + jnp.arange(2)[:, None] * HALF + jnp.arange(BLK // 16)[None, :] * 16
        inside = (places[..., None] >= starts) & (places[..., None] < ends)
        return jnp.pad(inside.astype(F32), ((0, 0), (0, 0), (0, 5)))

    hot = group_hot(0, 0)
    hot_rows = jnp.pad(hot.reshape(22, 16), ((0, 2), (0, 0)))

    def by_row(values):
        return jnp.transpose(values, (1, 0, 2))

    keep_wide = jnp.broadcast_to(keep.T.astype(BF16)[..., None], (2, BLK, LANES))
    triple, hidden_one, token_low, keep_low, mod_groups, w_wide, w_out_all, biases, act_all = front(
        mod_part, by_row(tokens), keep_wide, act_low, bias_own, w_a, spread, hot_rows
    )
    head_row = row_of(head_mask)
    heads_here = jnp.concatenate(
        [
            lax.dynamic_slice_in_dim(head_row, shard * 2, 2, 1),
            lax.dynamic_slice_in_dim(head_row, partner * 2, 2, 1),
        ],
        axis=1,
    )
    scal = jnp.concatenate(
        [
            starts,
            row_len // UNIT,
            row_len - row_pad,
            heads_here.reshape(-1),
        ]
    ).astype(jnp.int32)
    pack = np.zeros((NH * LANES, NH * HD), np.float32)
    for head in range(NH):
        pack[np.arange(HD) + head * LANES, np.arange(HD) + head * HD] = 1.0
    pack = jnp.asarray(pack, BF16)
    attended, lse = attn_fwd(scal, triple, pack)
    group_row = row_of(group_mask)
    groups_here = jnp.concatenate(
        [
            lax.dynamic_slice_in_dim(group_row, shard * 2, 2, 1),
            lax.dynamic_slice_in_dim(group_row, partner * 2, 2, 1),
        ],
        axis=1,
    ).astype(F32)
    all_places = jnp.arange(SEQ // 16)[:, None] * 16
    all_hot = ((all_places >= starts) & (all_places < ends)).astype(F32)
    group_wide = jnp.repeat(
        jnp.dot(all_hot, groups_here, precision=highest), GW, axis=1
    )
    consts = jnp.pad(jnp.stack([b_out, b_down, w_route]).astype(F32), ((0, 5), (0, 0)))
    b_up_two = jnp.concatenate([biases[0, :, 768:1344], biases[1, :, 768:1344]], axis=1)
    final, grad_mixed, grad_attended, sums_two, smalls, up_low, down_low, wo_low, b_up_sums = middle(
        attended, token_low.reshape(2 * BLK, D), keep_low.reshape(2 * BLK, LANES), mod_groups,
        by_row(grad_out), w_out_all.reshape(4 * QTR, D), w_up_rows, w_down, b_up_two, consts,
        group_wide,
    )
    d_all = attn_bwd(scal, triple, grad_attended, lse, pack)
    slope = jnp.pad(sig * (1.0 + cvec * (1.0 - sig)), ((0, 0), (0, 5), (0, 0))).reshape(32, D)
    final_pair, token_pair, low_a, low_up, low_down, mod_all, grad_cond = back(
        d_all, hidden_one, w_wide, token_low.reshape(2 * BLK, D), grad_mixed,
        mod_groups[:, D : 2 * D], sums_two, smalls, b_up_sums, up_low.reshape(2, WROWS, D),
        down_low.reshape(2, WROWS, D), wo_low, hot_rows, spread, final, jnp.transpose(ada_w), slope,
    )
    out_a = low_a.astype(F32)
    mod_low = jnp.where(jnp.arange(16)[:, None] < CROPS, mod_all, 0)
    grad_ada_w = tn(mod_low.reshape(128, MODS), act_all.reshape(128, D))
    grad_ada_b = jnp.sum(mod_low, axis=(0, 1, 2), dtype=F32)
    rest = jnp.sum(mod_all[:, :, CROPS:], axis=(0, 1), dtype=F32)
    return (
        by_row(final_pair), by_row(token_pair), grad_cond.reshape(2, 16, D)[:, :CROPS],
        jnp.transpose(grad_ada_w), grad_ada_b, jnp.transpose(out_a[:UNIT_ROWS]), rest[3, 2 * GW :],
        out_a[UNIT_ROWS:], rest[0, : D // 8], jnp.transpose(low_up.astype(F32)), rest[3, : 2 * GW],
        low_down.astype(F32), rest[1, : D // 8], rest[2, : D // 8],
    )


IN_SPECS = (
    ("heads", "rows", None), ("rows", None, None), ("rows", None), ("rows", None), ("rows", None),
    ("rows", None, None), ("rows", None, None), ("heads", "rows"), (None, "heads"), ("heads",),
    (None, "heads"), ("heads",), ("heads", None), (), (None, "heads"), ("heads",), ("heads", None),
    (), (), ("heads", "rows", None),
)
OUT_SPECS = (
    ("heads", "rows", None), ("heads", "rows", None), ("rows", None, None), (None, "heads"),
    ("heads",), (None, "heads"), ("heads",), ("heads", None), ("heads",), (None, "heads"),
    ("heads",), ("heads", None), ("heads",), ("heads",),
)


def solution(mesh):
    paired = mesh.shape["rows"] == 4 and mesh.shape["heads"] == 8
    if paired:
        mesh = Mesh(mesh.devices.reshape(2, 2, 2, 2, 2), ("y", "x", "p", "q", "c"))
        names = {"rows": ("y", "x"), "heads": ("p", "q", "c"), None: None}
    else:
        names = {"rows": "rows", "heads": "heads", None: None}

    def specs(items):
        return tuple(P(*(names[name] for name in item)) for item in items)

    return jax.shard_map(
        layer_device if paired else per_device,
        mesh=mesh,
        in_specs=specs(IN_SPECS),
        out_specs=specs(OUT_SPECS),
        check_vma=False,
    )
```

```python
import math

import jax
import jax.numpy as jnp
import numpy as np
from jax import lax
from jax.experimental import pallas as pl
from jax.experimental.pallas import tpu as pltpu
from jax.sharding import Mesh
from jax.sharding import PartitionSpec as P

D = 1152
H = 16
HD = 72
GW = 288
SEQ = 1408
CROPS = 11
UNIT = 64
LANES = 128
EPSILON = 1e-06
MASKED_SCORE = -1000000000.0
MESH = pl.DeviceIdType.MESH
SWAP = [(0, 1), (1, 0)]
F32 = jnp.float32
BF16 = jnp.bfloat16
SCALE = HD ** (-0.5)


def time_embed(timesteps):
    halves = D // 2
    frequency = jnp.exp(-math.log(10000.0) * jnp.arange(halves, dtype=jnp.float32) / halves)
    angles = timesteps.astype(jnp.float32)[..., None] * frequency
    return jnp.concatenate([jnp.cos(angles), jnp.sin(angles)], axis=-1)


def gelu_tanh(values):
    return (
        0.5
        * values
        * (1.0 + jnp.tanh(0.7978845608028654 * (values + 0.044715 * values * values * values)))
    )


def norm_rows(values):
    average = jnp.mean(values, axis=-1, keepdims=True)
    centred = values - average
    inverse_dev = lax.rsqrt(jnp.mean(centred * centred, axis=-1, keepdims=True) + EPSILON)
    return (centred * inverse_dev, inverse_dev)


def norm_back(grad_normed, normed, inverse_dev):
    first_mean = jnp.mean(grad_normed, axis=-1, keepdims=True)
    second_mean = jnp.mean(grad_normed * normed, axis=-1, keepdims=True)
    return inverse_dev * (grad_normed - first_mean - normed * second_mean)


def crop_layout(lengths, pads, offset, amount):
    crop_ends = jnp.cumsum(lengths, axis=1)
    starts = crop_ends - lengths
    places = offset + jnp.arange(amount, dtype=jnp.int32)
    inside = (places[:, None, None] >= starts[None]) & (places[:, None, None] < crop_ends[None])
    live_part = places[:, None, None] < (crop_ends - pads)[None]
    one_hot = inside.astype(jnp.float32)
    item_ids = jnp.sum(
        inside.astype(jnp.int32) * jnp.arange(lengths.shape[1], dtype=jnp.int32), axis=2
    )
    valid = jnp.sum((inside & live_part).astype(jnp.float32), axis=2)
    return (one_hot, item_ids, valid)


def masked_scores(queries, key_rows, item_row, key_live, score_scale):
    raw = jnp.einsum("shd,thd->hst", queries, key_rows, preferred_element_type=jnp.float32)
    allowed = (item_row[:, None] == item_row[None, :]) & key_live[None, :]
    return jnp.where(allowed[None], raw * score_scale, MASKED_SCORE)


def attend_row(triple_row, item_row, key_live, score_scale):
    queries = triple_row[:, :, 0]
    key_rows = triple_row[:, :, 1]
    values = triple_row[:, :, 2]
    scores = masked_scores(queries, key_rows, item_row, key_live, score_scale)
    row_top = jnp.max(scores, axis=-1, keepdims=True)
    log_total = row_top + jnp.log(jnp.sum(jnp.exp(scores - row_top), axis=-1, keepdims=True))
    probability = jnp.exp(scores - log_total).astype(jnp.bfloat16)
    attended = jnp.einsum("hst,thd->shd", probability, values, preferred_element_type=jnp.float32)
    return (attended, log_total)


def attend_back(triple_row, grad_row, total_row, item_row, key_live, score_scale):
    queries = triple_row[:, :, 0]
    key_rows = triple_row[:, :, 1]
    values = triple_row[:, :, 2]
    scores = masked_scores(queries, key_rows, item_row, key_live, score_scale)
    probability = jnp.exp(scores - total_row)
    grad_prob = jnp.einsum("shd,thd->hst", grad_row, values, preferred_element_type=jnp.float32)
    grad_values = jnp.einsum(
        "hst,shd->thd",
        probability.astype(jnp.bfloat16),
        grad_row,
        preferred_element_type=jnp.float32,
    )
    inner = jnp.sum(probability * grad_prob, axis=-1, keepdims=True)
    grad_raw = (probability * (grad_prob - inner) * score_scale).astype(jnp.bfloat16)
    grad_queries = jnp.einsum(
        "hst,thd->shd", grad_raw, key_rows, preferred_element_type=jnp.float32
    )
    grad_keys = jnp.einsum("hst,shd->thd", grad_raw, queries, preferred_element_type=jnp.float32)
    return jnp.stack([grad_queries, grad_keys, grad_values], axis=2).astype(jnp.bfloat16)


def project_rows(source, weight):
    return jnp.einsum("sbk,kd->sbd", source, weight, preferred_element_type=jnp.float32)


def back_rows(source, weight):
    return jnp.einsum("sbk,dk->sbd", source, weight, preferred_element_type=jnp.float32)


def per_device(
    tokens,
    cond,
    lengths,
    pads,
    timesteps,
    head_mask,
    group_mask,
    keep,
    ada_w,
    ada_b,
    w_qkv,
    b_qv,
    w_out,
    b_out,
    w_up,
    b_up,
    w_down,
    b_down,
    w_route,
    grad_out,
):
    highest = lax.Precision.HIGHEST
    groups = lax.axis_size("heads")
    head_rank = lax.axis_index("heads")
    shard_len = tokens.shape[0]
    batch_local = tokens.shape[1]
    local_heads = H // groups
    score_scale = HD ** (-0.5)
    local_hot, local_items, local_valid = crop_layout(
        lengths, pads, head_rank * shard_len, shard_len
    )
    full_hot, full_items, full_valid = crop_layout(lengths, pads, 0, SEQ)
    cond_all = cond.astype(jnp.float32) + time_embed(timesteps)
    sigmoid_cond = lax.logistic(cond_all)
    silu_low = (cond_all * sigmoid_cond).astype(jnp.bfloat16)
    modulation_part = jnp.einsum(
        "bcd,dm->bcm", silu_low, ada_w, preferred_element_type=jnp.float32
    ) + ada_b.astype(jnp.float32)
    modulation = lax.all_gather(modulation_part, "heads", axis=2, tiled=True)
    token_mod = jnp.einsum("sbc,bcm->sbm", local_hot, modulation, precision=highest)
    shift_one, scale_one, gate_one, shift_two, scale_two, gate_two = jnp.split(
        token_mod, 6, axis=-1
    )
    token_values = tokens.astype(jnp.float32)
    normed_one, inverse_one = norm_rows(token_values)
    hidden_one = (normed_one * (1.0 + scale_one) + shift_one).astype(jnp.bfloat16)
    hidden_all = lax.all_gather(hidden_one, "heads", axis=0, tiled=True)
    bias_pairs = b_qv.astype(jnp.float32).reshape(local_heads, 2, HD)
    bias_triple = jnp.stack(
        [bias_pairs[:, 0], jnp.zeros_like(bias_pairs[:, 0]), bias_pairs[:, 1]], axis=1
    ).reshape(-1)
    triple_all = (
        jnp.einsum("sbd,dm->sbm", hidden_all, w_qkv, preferred_element_type=jnp.float32)
        + bias_triple
    ).astype(jnp.bfloat16)
    triple_rows = jnp.moveaxis(triple_all.reshape(SEQ, batch_local, local_heads, 3, HD), 1, 0)
    item_rows = jnp.transpose(full_items)
    live_rows = jnp.transpose(full_valid > 0.5)
    attended, totals = lax.map(
        lambda packed: attend_row(packed[0], packed[1], packed[2], score_scale),
        (triple_rows, item_rows, live_rows),
    )
    head_table = lax.dynamic_slice_in_dim(
        head_mask, head_rank * local_heads, local_heads, 2
    ).astype(jnp.float32)
    head_full = jnp.einsum("sbc,bch->sbh", full_hot, head_table, precision=highest)
    out_mask = head_full * full_valid[..., None]
    attn_low = (
        (jnp.moveaxis(attended, 0, 1) * out_mask[..., None])
        .reshape(SEQ, batch_local, local_heads * HD)
        .astype(jnp.bfloat16)
    )
    projected = lax.psum_scatter(
        project_rows(attn_low, w_out), "heads", scatter_dimension=0, tiled=True
    )
    b_out_values = b_out.astype(jnp.float32)
    mixed = token_values + gate_one * (projected + b_out_values)
    normed_two, inverse_two = norm_rows(mixed)
    hidden_two = normed_two * (1.0 + scale_two) + shift_two
    hidden_two_low = hidden_two.astype(jnp.bfloat16)
    route_values = w_route.astype(jnp.float32)
    route = lax.logistic(jnp.einsum("sbd,d->sb", hidden_two, route_values, precision=highest))
    keep_values = keep.astype(jnp.float32)
    route_keep = keep_values * route
    group_table = lax.dynamic_slice_in_dim(
        group_mask, head_rank * local_heads, local_heads, 2
    ).astype(jnp.float32)
    hidden_two_all = lax.all_gather(hidden_two_low, "heads", axis=0, tiled=True)
    group_tok = jnp.einsum("sbc,bch->sbh", full_hot, group_table, precision=highest)
    upper = jnp.einsum(
        "sbd,dk->sbk", hidden_two_all, w_up, preferred_element_type=jnp.float32
    ) + b_up.astype(jnp.float32)
    active, gelu_back = jax.vjp(gelu_tanh, upper)
    group_wide = jnp.repeat(group_tok, GW, axis=-1)
    active_low = (active * group_wide).astype(jnp.bfloat16)
    lowered = lax.psum_scatter(
        project_rows(active_low, w_down), "heads", scatter_dimension=0, tiled=True
    )
    branch = lowered + b_down.astype(jnp.float32)
    final = mixed + gate_two * route_keep[..., None] * branch
    grad_final = grad_out.astype(jnp.float32)
    grad_branch = grad_final * gate_two * route_keep[..., None]
    grad_gate_two = grad_final * route_keep[..., None] * branch
    grad_route = jnp.sum(grad_final * gate_two * branch, axis=-1) * keep_values
    grad_logit = grad_route * route * (1.0 - route)
    part_route = jnp.einsum("sb,sbd->d", grad_logit, hidden_two, precision=highest)
    part_b_down = jnp.sum(grad_branch, axis=(0, 1))
    grad_low = grad_branch.astype(jnp.bfloat16)
    grad_all = lax.all_gather(grad_low, "heads", axis=0, tiled=True)
    grad_active = jnp.einsum("sbd,kd->sbk", grad_all, w_down, preferred_element_type=jnp.float32)
    (grad_upper,) = gelu_back(grad_active * group_wide)
    upper_low = grad_upper.astype(jnp.bfloat16)
    grad_w_up = jnp.einsum(
        "sbd,sbk->dk", hidden_two_all, upper_low, preferred_element_type=jnp.float32
    )
    grad_b_up = jnp.sum(upper_low, axis=(0, 1), dtype=jnp.float32)
    grad_w_down = jnp.einsum(
        "sbk,sbd->kd", active_low, grad_all, preferred_element_type=jnp.float32
    )
    grad_hidden_two = lax.psum_scatter(
        back_rows(upper_low, w_up), "heads", scatter_dimension=0, tiled=True
    )
    grad_hidden_two = grad_hidden_two + grad_logit[..., None] * route_values
    grad_scale_two = grad_hidden_two * normed_two
    grad_mixed = grad_final + norm_back(
        grad_hidden_two * (1.0 + scale_two), normed_two, inverse_two
    )
    grad_gate_one = grad_mixed * (projected + b_out_values)
    grad_projected = grad_mixed * gate_one
    part_b_out = jnp.sum(grad_projected, axis=(0, 1))
    projected_low = grad_projected.astype(jnp.bfloat16)
    grad_proj_all = lax.all_gather(projected_low, "heads", axis=0, tiled=True)
    grad_attn = jnp.einsum(
        "sbd,kd->sbk", grad_proj_all, w_out, preferred_element_type=jnp.float32
    ).astype(jnp.bfloat16)
    grad_w_out = jnp.einsum(
        "sbk,sbd->kd", attn_low, grad_proj_all, preferred_element_type=jnp.float32
    )
    grad_masked = grad_attn.reshape(SEQ, batch_local, local_heads, HD) * out_mask[..., None].astype(
        jnp.bfloat16
    )
    grad_rows = jnp.moveaxis(grad_masked, 1, 0)
    grad_triple_rows = lax.map(
        lambda packed: attend_back(
            packed[0], packed[1], packed[2], packed[3], packed[4], score_scale
        ),
        (triple_rows, grad_rows, totals, item_rows, live_rows),
    )
    grad_triple = jnp.moveaxis(grad_triple_rows, 0, 1).reshape(
        SEQ, batch_local, local_heads * 3 * HD
    )
    grad_w_qkv = jnp.einsum(
        "sbd,sbm->dm", hidden_all, grad_triple, preferred_element_type=jnp.float32
    )
    bias_sums = jnp.sum(grad_triple, axis=(0, 1), dtype=jnp.float32).reshape(local_heads, 3, HD)
    grad_b_qv = jnp.stack([bias_sums[:, 0], bias_sums[:, 2]], axis=1).reshape(-1)
    grad_hidden_one = lax.psum_scatter(
        back_rows(grad_triple, w_qkv), "heads", scatter_dimension=0, tiled=True
    )
    grad_tokens = grad_mixed + norm_back(
        grad_hidden_one * (1.0 + scale_one), normed_one, inverse_one
    )
    grad_token_mod = jnp.concatenate(
        [
            grad_hidden_one,
            grad_hidden_one * normed_one,
            grad_gate_one,
            grad_hidden_two,
            grad_scale_two,
            grad_gate_two,
        ],
        axis=-1,
    )
    part_mod = jnp.einsum("sbc,sbm->bcm", local_hot, grad_token_mod, precision=highest)
    grad_mod, share_b_out, share_b_down, share_route = (
        lax.psum_scatter(part_mod, "heads", scatter_dimension=2, tiled=True),
        lax.psum_scatter(part_b_out, "heads", scatter_dimension=0, tiled=True),
        lax.psum_scatter(part_b_down, "heads", scatter_dimension=0, tiled=True),
        lax.psum_scatter(part_route, "heads", scatter_dimension=0, tiled=True),
    )
    mod_low = grad_mod.astype(jnp.bfloat16)
    grad_ada_w = jnp.einsum("bcd,bcm->dm", silu_low, mod_low, preferred_element_type=jnp.float32)
    grad_ada_b = jnp.sum(mod_low, axis=(0, 1), dtype=jnp.float32)
    part_activ = jnp.einsum("bcm,dm->bcd", mod_low, ada_w, preferred_element_type=jnp.float32)
    grad_activ = lax.psum(part_activ.astype(jnp.bfloat16), "heads").astype(jnp.float32)
    grad_cond = grad_activ * sigmoid_cond * (1.0 + cond_all * (1.0 - sigmoid_cond))
    summed = (
        lax.psum(grad_ada_w.astype(jnp.bfloat16), "rows").astype(jnp.float32),
        lax.psum(grad_ada_b.astype(jnp.bfloat16), "rows").astype(jnp.float32),
        lax.psum(grad_w_qkv.astype(jnp.bfloat16), "rows").astype(jnp.float32),
        lax.psum(grad_b_qv.astype(jnp.bfloat16), "rows").astype(jnp.float32),
        lax.psum(grad_w_out.astype(jnp.bfloat16), "rows").astype(jnp.float32),
        lax.psum(share_b_out.astype(jnp.bfloat16), "rows").astype(jnp.float32),
        lax.psum(grad_w_up.astype(jnp.bfloat16), "rows").astype(jnp.float32),
        lax.psum(grad_b_up.astype(jnp.bfloat16), "rows").astype(jnp.float32),
        lax.psum(grad_w_down.astype(jnp.bfloat16), "rows").astype(jnp.float32),
        lax.psum(share_b_down.astype(jnp.bfloat16), "rows").astype(jnp.float32),
        lax.psum(share_route.astype(jnp.bfloat16), "rows").astype(jnp.float32),
    )
    return (
        final.astype(jnp.bfloat16),
        grad_tokens,
        grad_cond,
        summed[0],
        summed[1],
        summed[2],
        summed[3],
        summed[4],
        summed[5],
        summed[6],
        summed[7],
        summed[8],
        summed[9],
        summed[10],
    )


BLK = 176
NH = 4
HALF = SEQ // 2


def each_crop(scal, body):
    def step(item, carry):
        units = scal[CROPS + item]
        for count in range(2, 9):

            @pl.when(units == count)
            def _():
                body(item, pl.multiple_of(scal[item], UNIT), count * UNIT)

        return carry

    lax.fori_loop(0, CROPS, step, 0)


def nt(a, b):
    return lax.dot_general(a, b, (((1,), (1,)), ((), ())), preferred_element_type=F32)


def tn(a, b):
    return lax.dot_general(a, b, (((0,), (0,)), ((), ())), preferred_element_type=F32)


def attn_fwd_kernel(scal, buf, pack, obuf, lse):
    lane = lax.broadcasted_iota(jnp.int32, (1, LANES), 1)

    def body(item, start, size):
        live = scal[2 * CROPS + item]
        keys_live = lax.broadcasted_iota(jnp.int32, (1, size), 1) < live
        rows_live = (lax.broadcasted_iota(jnp.int32, (size, 1), 0) < live).astype(F32)
        window = pl.ds(start, size)
        packed = jnp.zeros((size, NH * HD), F32)
        totals = jnp.zeros((size, LANES), F32)
        for head in range(NH):
            at = head * 3 * LANES
            queries = buf[window, at : at + LANES]
            keys = buf[window, at + LANES : at + 2 * LANES]
            values = buf[window, at + 2 * LANES : at + 3 * LANES]
            scores = jnp.where(keys_live, nt(queries, keys) * SCALE, MASKED_SCORE)
            top = jnp.max(scores, axis=1, keepdims=True)
            expo = jnp.exp(scores - top)
            total = jnp.sum(expo, axis=1, keepdims=True)
            prob = (expo * (1.0 / total)).astype(BF16)
            mixed = jnp.dot(prob, values, preferred_element_type=F32)
            mask = scal[3 * CROPS + item * NH + head].astype(F32)
            mixed = (mixed * (rows_live * mask)).astype(BF16)
            packed += jnp.dot(
                mixed, pack[head * LANES : (head + 1) * LANES, :], preferred_element_type=F32
            )
            totals = jnp.where(lane == head, top + jnp.log(total), totals)
        obuf[window, :] = packed.astype(BF16)
        lse[window, :] = totals

    each_crop(scal, body)


def attn_bwd_kernel(scal, buf, gbuf, lse, pack, dbuf):
    def body(item, start, size):
        live = scal[2 * CROPS + item]
        keys_live = lax.broadcasted_iota(jnp.int32, (1, size), 1) < live
        rows_live = lax.broadcasted_iota(jnp.int32, (size, 1), 0) < live
        window = pl.ds(start, size)
        grads = gbuf[window, :]
        grads = jnp.where(rows_live, grads.astype(F32), 0.0).astype(BF16)
        for head in range(NH):
            at = head * 3 * LANES
            queries = buf[window, at : at + LANES]
            keys = buf[window, at + LANES : at + 2 * LANES]
            values = buf[window, at + 2 * LANES : at + 3 * LANES]
            mask = scal[3 * CROPS + item * NH + head].astype(F32)
            grad = (nt(grads, pack[head * LANES : (head + 1) * LANES, :]) * mask).astype(BF16)
            scores = jnp.where(keys_live, nt(queries, keys) * SCALE, MASKED_SCORE)
            prob = jnp.exp(scores - lse[window, head : head + 1])
            grad_prob = nt(grad, values)
            grad_values = tn(prob.astype(BF16), grad)
            inner = jnp.sum(prob * grad_prob, axis=1, keepdims=True)
            grad_raw = (prob * (grad_prob - inner) * SCALE).astype(BF16)
            dbuf[window, at : at + LANES] = jnp.dot(
                grad_raw, keys, preferred_element_type=F32
            ).astype(BF16)
            dbuf[window, at + LANES : at + 2 * LANES] = tn(grad_raw, queries).astype(BF16)
            dbuf[window, at + 2 * LANES : at + 3 * LANES] = grad_values.astype(BF16)

    each_crop(scal, body)


WIDE = NH * 3 * LANES
SMEM_SPEC = pl.BlockSpec(memory_space=pltpu.SMEM)
VMEM_SPEC = pl.BlockSpec(memory_space=pltpu.VMEM)
ANY_SPEC = pl.BlockSpec(memory_space=pl.ANY)


def attn_fwd(scal, triple, pack):
    return pl.pallas_call(
        attn_fwd_kernel,
        out_shape=(
            jax.ShapeDtypeStruct((SEQ, NH * HD), BF16),
            jax.ShapeDtypeStruct((SEQ, LANES), F32),
        ),
        in_specs=[SMEM_SPEC, VMEM_SPEC, VMEM_SPEC],
        out_specs=(VMEM_SPEC, VMEM_SPEC),
        compiler_params=pltpu.CompilerParams(vmem_limit_bytes=48 * 2**20),
        name="attn_fwd",
    )(scal, triple, pack)


def attn_bwd(scal, triple, grads, lse, pack):
    return pl.pallas_call(
        attn_bwd_kernel,
        out_shape=jax.ShapeDtypeStruct((SEQ, WIDE), BF16),
        in_specs=[SMEM_SPEC] + [VMEM_SPEC] * 4,
        out_specs=VMEM_SPEC,
        compiler_params=pltpu.CompilerParams(vmem_limit_bytes=48 * 2**20),
        name="attn_bwd",
    )(scal, triple, grads, lse, pack)


QTR = 144
WROWS = 576
BIAS = 1408
GROUPS = 24
UNIT_ROWS = 6 * HD
MODS = 6 * D // 8
CUT = 80


def remote(src, dst, sems, k, **where):
    return pltpu.make_async_remote_copy(
        src_ref=src,
        dst_ref=dst,
        send_sem=sems[0].at[k],
        recv_sem=sems[1].at[k],
        device_id=where,
        device_id_type=MESH,
    )


def greet(peers):
    barrier = pltpu.get_barrier_semaphore()
    for where in peers:
        pl.semaphore_signal(barrier, inc=1, device_id=where, device_id_type=MESH)
    pl.semaphore_wait(barrier, len(peers))


def line_peers(p, q, c):
    out = []
    for k in range(1, 8):
        out.append(
            {
                "p": lax.rem(p + k // 4, 2),
                "q": lax.rem(q + (k // 2) % 2, 2),
                "c": lax.rem(c + k % 2, 2),
            }
        )
    return out


def rows_at(start, size):
    return pl.ds(pl.multiple_of(start, 16), size)


class PlaneGather:
    COPIES = 8

    def __init__(self, src, dst, sems, k, y, x, p, loaded=None):
        self.loaded = loaded
        self.over, self.to_x, self.to_y = [], [], []
        for i, (start, size) in enumerate(((0, CUT), (CUT, QTR - CUT))):
            rows = rows_at((y * 2 + x) * QTR + start, size)
            mine = dst.at[rows]
            if loaded is None:
                self.over.append(remote(src.at[rows], mine, sems, k + i, p=1 - p))
            else:
                self.over.append(
                    pltpu.make_async_copy(src.at[start : start + size], mine, loaded.at[i])
                )
            self.to_x.append(remote(mine, mine, sems, k + 2 + i, x=1 - x))
            self.to_y.append(remote(mine, mine, sems, k + 4 + i, y=1 - y))
        from_x = dst.at[rows_at((y * 2 + 1 - x) * QTR, CUT)]
        from_y = dst.at[rows_at(((1 - y) * 2 + x) * QTR + CUT, QTR - CUT)]
        self.on_y = remote(from_x, from_x, sems, k + 6, y=1 - y)
        self.on_x = remote(from_y, from_y, sems, k + 7, x=1 - x)

    def start(self):
        for copy in self.over:
            copy.start()

    def spread(self, i):
        if self.loaded is None:
            self.over[i].wait_recv()
        else:
            self.over[i].wait()
        self.to_x[i].start()
        self.to_y[i].start()

    def forward(self, i):
        if i == 0:
            self.to_x[0].wait_recv()
            self.on_y.start()
        else:
            self.to_y[1].wait_recv()
            self.on_x.start()

    def finish(self):
        for copy in (self.to_y[0], self.to_x[1], self.on_y, self.on_x):
            copy.wait_recv()

    def sent(self):
        copies = self.to_x + self.to_y + [self.on_y, self.on_x]
        for copy in copies if self.loaded is not None else self.over + copies:
            copy.wait_send()


def norm_tile(values):
    average = jnp.mean(values, axis=1, keepdims=True)
    centred = values - average
    inverse = lax.rsqrt(jnp.mean(centred * centred, axis=1, keepdims=True) + EPSILON)
    return centred * inverse, inverse


def front_kernel(
    cvec_ref, x_pair, k_pair, g_pair, bias_own, w_a, spread, hot, ada, ada_b,
    t_out, h_out, x_out, k_out, g_out, modg_out, wide_out, wo_out, bias_out, act_out, slope_out,
    part, mods, modg, h, wide, other_a, own_a, tbuf, send, recv, loc,
):
    y, x, p, q, c = (lax.axis_index(name) for name in "yxpqc")
    sems = (send, recv)
    pair = [
        {"q": lax.rem(q + k // 2, 2), "c": lax.rem(c + k % 2, 2)} for k in range(1, 4)
    ]
    plane = [{"y": lax.rem(y + k // 2, 2), "x": lax.rem(x + k % 2, 2)} for k in range(1, 4)]
    rank = y * 2 + x
    waits = []

    def keep_local(src, dst, k):
        copy = pltpu.make_async_copy(src, dst, loc.at[k])
        copy.start()
        return copy

    load_a = keep_local(w_a, own_a, 0)
    cvec = cvec_ref[...]
    sig = 1.0 / (1.0 + jnp.exp(-cvec))
    slope_out[...] = sig * (1.0 + cvec * (1.0 - sig))
    act = (cvec * sig).astype(BF16)
    act_mine = act_out.at[rank]
    act_mine[...] = act
    mod_all = nt(act, ada[...]) + ada_b[...]
    part[0] = mod_all[:16]
    part[1] = mod_all[16:]

    greet(pair + plane + [{"p": 1 - p}])

    def spot(pp, qq, cc):
        return pp * 4 + qq * 2 + cc

    mod_over = remote(part.at[1 - p], mods.at[spot(p, q, c)], sems, 0, p=1 - p)
    mod_over.start()
    own_mod = keep_local(part.at[p], mods.at[spot(p, q, c)], 1)
    mod_own = []
    mod_far = []
    for k, where in enumerate(pair):
        copy = remote(part.at[p], mods.at[spot(p, q, c)], sems, 1 + k, **where)
        copy.start()
        mod_own.append(copy)
    bias_copy = remote(bias_own, bias_out.at[1], sems, 17, p=1 - p)
    bias_copy.start()
    k_copy = remote(k_pair.at[1 - p], k_out.at[p], sems, 18, p=1 - p)
    k_copy.start()
    take_a = PlaneGather(w_a, other_a, sems, 7, y, x, p)
    take_a.start()
    pieces = ((0, 96), (96, 80))
    x_copies = []
    for i, (start, size) in enumerate(pieces):
        rows = slice(start, start + size)
        x_copies.append(remote(x_pair.at[1 - p, rows], x_out.at[p, rows], sems, 15 + i, p=1 - p))
    waits.append(keep_local(x_pair.at[p], x_out.at[p], 2))
    waits.append(keep_local(k_pair.at[p], k_out.at[p], 3))
    waits.append(keep_local(g_pair.at[p], g_out.at[p], 5))
    own_bias = keep_local(bias_own, bias_out.at[0], 4)
    load_a.wait()
    tails = (own_a.at[UNIT_ROWS:], other_a.at[UNIT_ROWS:])
    outer = [remote(tails[k], wo_out.at[2 + k], sems, 19 + k, q=1 - q) for k in range(2)]
    mod_over.wait_recv()
    for k, where in enumerate(pair):
        far = mods.at[spot(1 - p, q, c)]
        copy = remote(far, far, sems, 4 + k, **where)
        copy.start()
        mod_far.append(copy)
    acts = []
    for k, where in enumerate(plane):
        copy = remote(act_mine, act_mine, sems, 21 + k, **where)
        copy.start()
        acts.append(copy)

    wide[: 6 * LANES, :] = jnp.dot(
        spread[...], own_a[:UNIT_ROWS, :], preferred_element_type=F32
    ).astype(BF16)

    own_mod.wait()
    for copy in mod_own + mod_far:
        copy.wait_recv()
    full = jnp.concatenate([mods[k] for k in range(8)], axis=1)
    modg[...] = jnp.dot(
        hot[...], full, preferred_element_type=F32, precision=lax.Precision.HIGHEST
    )
    waits.append(keep_local(modg, modg_out, 6))

    def place(slot, chip, core):
        return slot * HALF + chip * (2 * BLK) + core * BLK

    def modulate(src, slot, start, size):
        base = place(slot, q, c)

        def group(g, carry):
            values = src[rows_at(g * 16, 16), :].astype(F32)
            normed, _ = norm_tile(values)
            row = slot * (BLK // 16) + g
            shift = modg[pl.ds(row, 1), 0:D]
            scale = modg[pl.ds(row, 1), D : 2 * D]
            h[rows_at(base + g * 16, 16), :] = (normed * (1.0 + scale) + shift).astype(BF16)
            return carry

        lax.fori_loop(start // 16, (start + size) // 16, group, 0)

    first, second = p, 1 - p
    spans = [(first, 0, BLK)] + [(second, start, size) for start, size in pieces]
    hops = []
    for i, (slot, start, size) in enumerate(spans):
        mine = h.at[rows_at(place(slot, q, c) + start, size)]
        other = h.at[rows_at(place(slot, 1 - q, c) + start, size)]
        hops.append(
            (
                remote(mine, mine, sems, 24 + 3 * i, q=1 - q),
                remote(mine, mine, sems, 25 + 3 * i, c=1 - c),
                remote(other, other, sems, 26 + 3 * i, c=1 - c),
            )
        )

    modulate(x_pair.at[p], first, 0, BLK)
    hops[0][0].start()
    hops[0][1].start()
    take_a.spread(0)
    own_bias.wait()
    bias_copy.wait_recv()
    take_a.spread(1)
    for copy in x_copies:
        copy.start()
    hops[0][1].wait_recv()

    def project(slot, chip, half):
        rows = rows_at(place(slot, chip, 0), 2 * BLK)
        cols = slice(half * 6 * LANES, (half + 1) * 6 * LANES)
        line = bias_out[half, 0:1, : 6 * LANES]
        tbuf[rows, cols] = (nt(h[rows, :], wide[cols, :]) + line).astype(BF16)

    def stored(slot, chip, k):
        rows = rows_at(place(slot, chip, 0), 2 * BLK)
        waits.append(keep_local(tbuf.at[rows], t_out.at[rows], k))
        waits.append(keep_local(h.at[rows], h_out.at[rows], k + 4))

    project(first, q, 0)
    take_a.forward(0)
    hops[0][0].wait_recv()
    hops[0][2].start()
    outer[0].start()
    take_a.forward(1)
    hops[0][2].wait_recv()
    project(first, 1 - q, 0)
    take_a.finish()
    outer[1].start()
    wide[6 * LANES :, :] = jnp.dot(
        spread[...], other_a[:UNIT_ROWS, :], preferred_element_type=F32
    ).astype(BF16)
    waits.append(keep_local(wide, wide_out, 7))
    for k in range(2):
        waits.append(keep_local(tails[k], wo_out.at[k], 8 + k))
    x_copies[0].wait_recv()
    modulate(x_out.at[second], second, *pieces[0])
    hops[1][0].start()
    hops[1][1].start()
    project(first, q, 1)
    stored(first, q, 10)
    x_copies[1].wait_recv()
    g_copy = remote(g_pair.at[1 - p], g_out.at[p], sems, 33, p=1 - p)
    g_copy.start()
    modulate(x_out.at[second], second, *pieces[1])
    hops[2][0].start()
    hops[2][1].start()
    hops[1][0].wait_recv()
    hops[1][2].start()
    project(first, 1 - q, 1)
    stored(first, 1 - q, 11)
    hops[1][1].wait_recv()
    hops[2][1].wait_recv()
    project(second, q, 0)
    hops[2][0].wait_recv()
    hops[2][2].start()
    project(second, q, 1)
    stored(second, q, 12)
    hops[1][2].wait_recv()
    hops[2][2].wait_recv()
    project(second, 1 - q, 0)
    project(second, 1 - q, 1)
    stored(second, 1 - q, 13)
    for copy in outer + acts + [k_copy, g_copy]:
        copy.wait_recv()
    for copy in [mod_over, bias_copy, k_copy, g_copy] + x_copies + mod_own + mod_far + outer + acts:
        copy.wait_send()
    for group in hops:
        for copy in group:
            copy.wait_send()
    take_a.sent()
    for copy in waits:
        copy.wait()


def shape_of(*shape, dtype=BF16):
    return jax.ShapeDtypeStruct(shape, dtype)


def front(*args):
    return pl.pallas_call(
        front_kernel,
        out_shape=(
            shape_of(SEQ, WIDE), shape_of(SEQ, D), shape_of(2, BLK, D), shape_of(2, BLK, LANES),
            shape_of(2, BLK, D), shape_of(GROUPS, 6 * D, dtype=F32), shape_of(WIDE, D),
            shape_of(4, QTR, D), shape_of(2, 8, BIAS, dtype=F32), shape_of(4, 32, D),
            shape_of(32, D, dtype=F32),
        ),
        in_specs=[VMEM_SPEC] * 3 + [ANY_SPEC, VMEM_SPEC, ANY_SPEC] + [VMEM_SPEC] * 4,
        out_specs=(
            ANY_SPEC, ANY_SPEC, VMEM_SPEC, VMEM_SPEC, ANY_SPEC, ANY_SPEC, ANY_SPEC, ANY_SPEC,
            VMEM_SPEC, VMEM_SPEC, VMEM_SPEC,
        ),
        scratch_shapes=[
            pltpu.VMEM((2, 16, MODS), F32),
            pltpu.VMEM((8, 16, MODS), F32),
            pltpu.VMEM((GROUPS, 6 * D), F32),
            pltpu.VMEM((SEQ, D), BF16),
            pltpu.VMEM((WIDE, D), BF16),
            pltpu.VMEM((WROWS, D), BF16),
            pltpu.VMEM((WROWS, D), BF16),
            pltpu.VMEM((SEQ, WIDE), BF16),
            pltpu.SemaphoreType.DMA((34,)),
            pltpu.SemaphoreType.DMA((34,)),
            pltpu.SemaphoreType.DMA((18,)),
        ],
        compiler_params=pltpu.CompilerParams(
            collective_id=6, has_side_effects=True, vmem_limit_bytes=56 * 2**20
        ),
        name="front",
    )(*args)


class PlaneReduce:
    def __init__(self, grads, bufs, sems, k, y, x, landed=False):
        self.grads, self.y, self.x = grads, y, x
        self.low_in, self.high_in, self.low_out, self.high_out, self.low_end, self.high_end = bufs
        self.first = [] if landed else [
            remote(grads.at[:, self.low(y, 1 - x)], self.low_in.at[0], sems, k, x=1 - x),
            remote(grads.at[:, self.low(1 - y, 1 - x)], self.low_in.at[1], sems, k + 1, x=1 - x),
            remote(grads.at[:, self.high(1 - y, x)], self.high_in.at[0], sems, k + 2, y=1 - y),
            remote(grads.at[:, self.high(1 - y, 1 - x)], self.high_in.at[1], sems, k + 3, y=1 - y),
        ]
        if self.low_out is None:
            return
        self.second = [
            remote(self.low_out, self.low_end, sems, k + 4, y=1 - y),
            remote(self.high_out, self.high_end, sems, k + 5, x=1 - x),
        ]

    def low(self, y, x):
        return rows_at((y * 2 + x) * QTR, CUT)

    def high(self, y, x):
        return rows_at((y * 2 + x) * QTR + CUT, QTR - CUT)

    def start(self):
        for copy in self.first:
            copy.start()

    def landed(self):
        for copy in self.first:
            copy.wait_recv()

    def middle(self):
        y, x = self.y, self.x
        for shard in range(2):
            self.low_out[shard] = (
                self.grads[shard, self.low(1 - y, x), :].astype(F32)
                + self.low_in[1, shard].astype(F32)
            ).astype(BF16)
            self.high_out[shard] = (
                self.grads[shard, self.high(y, 1 - x), :].astype(F32)
                + self.high_in[1, shard].astype(F32)
            ).astype(BF16)
        for copy in self.second:
            copy.start()

    def arrive(self):
        for copy in self.second:
            copy.wait_recv()

    def total(self, shard):
        low = (
            self.grads[shard, self.low(self.y, self.x), :].astype(F32)
            + self.low_in[0, shard].astype(F32)
            + self.low_end[shard].astype(F32)
        )
        high = (
            self.grads[shard, self.high(self.y, self.x), :].astype(F32)
            + self.high_in[0, shard].astype(F32)
            + self.high_end[shard].astype(F32)
        )
        return low, high

    def sent(self, second=True):
        for copy in self.first + (self.second if second else []):
            copy.wait_send()


REDUCE_SCRATCH = [
    pltpu.VMEM((2, 2, CUT, D), BF16),
    pltpu.VMEM((2, 2, QTR - CUT, D), BF16),
    pltpu.VMEM((2, CUT, D), BF16),
    pltpu.VMEM((2, QTR - CUT, D), BF16),
    pltpu.VMEM((2, CUT, D), BF16),
    pltpu.VMEM((2, QTR - CUT, D), BF16),
]


def gelu_both(u):
    cube = 0.044715 * u * u
    t = jnp.tanh(0.7978845608028654 * (u + cube * u))
    half = 0.5 * (1.0 + t)
    slope = half + 0.5 * u * (1.0 - t * t) * (0.7978845608028654 * (1.0 + 3.0 * cube))
    return u * half, slope


def middle_kernel(
    o, x2, k2, modg, g2, wo, w_up, up_quarter, w_down, bias, consts, gmask,
    fin_out, fin_send_out, dx_out, do_out, sums_out, small_out, up_out, down_out, gwo_out, gwo_far_out, bup_out, down_low, down_high, up_low, up_high,
    o_in, ybig, ysend, yrecv, y1, mixed, h2, dz, act, du, wup, wdown,
    own, csend, crecv, qsend, qrecv, dy, dofar, send, recv, loc,
):
    y, x, p, q, c = (lax.axis_index(name) for name in "yxpqc")
    sems = (send, recv)
    greet([{"q": 1 - q}, {"c": 1 - c}, {"p": 1 - p}, {"x": 1 - x}, {"y": 1 - y}])
    waits = []

    def keep_local(src, dst, k):
        copy = pltpu.make_async_copy(src, dst, loc.at[k])
        copy.start()
        return copy

    def place(slot, chip, core):
        return slot * HALF + chip * (2 * BLK) + core * BLK

    o_copies = []
    for slot in range(2):
        copy = remote(
            o.at[rows_at(place(slot, 1 - q, 0), 2 * BLK)], o_in.at[slot], sems, slot, q=1 - q
        )
        copy.start()
        o_copies.append(copy)
    take_up = PlaneGather(up_quarter, wup.at[1], sems, 43, y, x, p, loc.at[5:7])
    take_down = PlaneGather(w_down, wdown.at[1], sems, 51, y, x, p)
    take_up.start()
    take_down.start()
    take_up.spread(0)
    take_up.spread(1)
    own_up = keep_local(w_up, wup.at[0], 1)
    own_down = keep_local(w_down, wdown.at[0], 2)

    y_copies = []
    for slot in range(2):
        rows = rows_at(place(slot, q, 0), 2 * BLK)
        o_copies[slot].wait_recv()
        ybig[...] = jnp.dot(o[rows, :], wo[0 : 2 * QTR, :], preferred_element_type=F32) + jnp.dot(
            o_in[slot], wo[2 * QTR : 4 * QTR, :], preferred_element_type=F32
        )
        ysend[slot] = ybig[rows_at((1 - c) * BLK, BLK), :].astype(BF16)
        y1[slot * BLK : (slot + 1) * BLK, :] = ybig[rows_at(c * BLK, BLK), :]
        copy = remote(ysend.at[slot], yrecv.at[slot], sems, 13 + slot, c=1 - c)
        copy.start()
        y_copies.append(copy)

    take_up.forward(0)
    take_up.forward(1)
    take_down.spread(0)
    take_down.spread(1)
    b_out, b_down, w_route = consts[0:1, :], consts[1:2, :], consts[2:3, :]

    def routed(row):
        rows = rows_at(row * 16, 16)
        normed, inverse = norm_tile(mixed[rows, :])
        hidden = normed * (1.0 + modg[pl.ds(row, 1), 4 * D : 5 * D]) + modg[
            pl.ds(row, 1), 3 * D : 4 * D
        ]
        logit = jnp.sum(hidden * w_route, axis=1, keepdims=True)
        route = 1.0 / (1.0 + jnp.exp(-logit))
        kept = k2[rows, 0:1].astype(F32)
        return rows, normed, inverse, hidden, route, kept

    bufs = (h2, dz)

    def hop(array, slot, kind):
        mine = bufs[array].at[rows_at(place(slot, q, c), BLK)]
        far = bufs[array].at[rows_at(place(slot, 1 - q, c), BLK)]
        k = 15 + (slot * 2 + array) * 3 + kind
        if kind == 0:
            return remote(mine, mine, sems, k, q=1 - q)
        if kind == 1:
            return remote(mine, mine, sems, k, c=1 - c)
        return remote(far, far, sems, k, c=1 - c)

    for slot in range(2):
        y_copies[slot].wait_recv()

        def group(g, carry, slot=slot):
            row = slot * (BLK // 16) + g
            rows = rows_at(row * 16, 16)
            branch = y1[rows, :] + yrecv[slot, rows_at(g * 16, 16), :].astype(F32) + b_out
            y1[rows, :] = branch
            mixed[rows, :] = x2[rows, :].astype(F32) + modg[pl.ds(row, 1), 2 * D : 3 * D] * branch
            _, _, _, hidden, route, kept = routed(row)
            there = rows_at(place(slot, q, c) + g * 16, 16)
            h2[there, :] = hidden.astype(BF16)
            gate = modg[pl.ds(row, 1), 5 * D : 6 * D]
            dz[there, :] = (g2[rows, :].astype(F32) * gate * (kept * route)).astype(BF16)
            return carry

        lax.fori_loop(0, BLK // 16, group, 0)
        for array in range(2):
            if slot == 0:
                hop(array, slot, 0).start()
            hop(array, slot, 1).start()
        if slot == 0:
            take_down.forward(0)
            take_down.forward(1)

    own_up.wait()
    own_down.wait()
    take_up.finish()
    take_down.finish()

    def core_copy(array, side, slot):
        k = 27 + (array * 2 + side) * 2 + slot
        return remote(csend.at[array, side, slot], crecv.at[array, side, slot], sems, k, c=1 - c)

    def chip_copy(array, slot):
        return remote(qsend.at[array, slot], qrecv.at[array, slot], sems, 35 + array * 2 + slot, q=1 - q)

    def far_out(slot):
        for array in range(2):
            core_copy(array, 1, slot).wait_recv()
            qsend[array, slot] = (
                own[array, 1, slot] + crecv[array, 1, slot].astype(F32)
            ).astype(BF16)
            chip_copy(array, slot).start()

    def feed(step, carry):
        side, slot = step // 2, lax.rem(step, 2)
        chip = lax.rem(q + side, 2)
        start = place(slot, chip, 0)

        @pl.when(step == 0)
        def _():
            for array in range(2):
                hop(array, 0, 1).wait_recv()

        @pl.when(step == 1)
        def _():
            for array in range(2):
                hop(array, 1, 1).wait_recv()

        @pl.when(step == 2)
        def _():
            for array in range(2):
                hop(array, 0, 0).wait_recv()
                hop(array, 0, 2).start()
                hop(array, 1, 0).start()
            for array in range(2):
                hop(array, 0, 2).wait_recv()

        @pl.when(step == 3)
        def _():
            for array in range(2):
                hop(array, 1, 0).wait_recv()
                hop(array, 1, 2).start()
            far_out(0)
            for array in range(2):
                hop(array, 1, 2).wait_recv()

        def tile(part, carry):
            rows = rows_at(start + part * BLK, BLK)
            up_all = wup[...].reshape(D, D)
            down_all = wdown[...].reshape(D, D)
            u = nt(h2[rows, :], up_all) + bias[0:1, :]
            value, slope = gelu_both(u)
            row0 = start // 16 + part * (BLK // 16)
            mask = jnp.concatenate(
                [
                    jnp.broadcast_to(gmask[pl.ds(row0 + k, 1), :], (16, D))
                    for k in range(BLK // 16)
                ],
                axis=0,
            )
            act[rows, :] = (value * mask).astype(BF16)
            da = nt(dz[rows, :], down_all)
            du[rows, :] = (slope * mask * da).astype(BF16)
            z_part = jnp.dot(act[rows, :], down_all, preferred_element_type=F32)
            h_part = jnp.dot(du[rows, :], up_all, preferred_element_type=F32)

            @pl.when(part == c)
            def _():
                own[0, side, slot] = z_part
                own[1, side, slot] = h_part

            @pl.when(part != c)
            def _():
                csend[0, side, slot] = z_part.astype(BF16)
                csend[1, side, slot] = h_part.astype(BF16)

            return carry

        lax.fori_loop(0, 2, tile, 0)
        for array in range(2):
            core_copy(array, side, slot).start()
        return carry

    lax.fori_loop(0, 4, feed, 0)
    far_out(1)

    for copy in (take_up, take_down):
        copy.sent()

    def weight_grads(left, right, out):
        def chunk(j, carry):
            cols = pl.ds(pl.multiple_of(j * 384, LANES), 384)
            block = tn(left[:, cols], right[...]).astype(BF16)
            for k in range(2):
                at = j * 2 + k
                out[at // 3, rows_at(lax.rem(at, 3) * 192, 192), :] = block[k * 192 : (k + 1) * 192]
            return carry

        lax.fori_loop(0, 3, chunk, 0)

    down_sum = PlaneReduce(wdown, (down_low, down_high) + (None,) * 4, sems, 59, y, x)
    up_sum = PlaneReduce(wup, (up_low, up_high) + (None,) * 4, sems, 63, y, x)
    weight_grads(act, dz, wdown)
    down_sum.start()
    waits.append(keep_local(wdown, down_out, 4))
    weight_grads(du, h2, wup)
    up_sum.start()
    waits.append(keep_local(wup, up_out, 3))
    bup_out[...] = jnp.dot(jnp.ones((8, SEQ), BF16), du[...], preferred_element_type=F32)

    small_out[...] = jnp.zeros_like(small_out)
    sums_out[22:24, :] = jnp.zeros((2, 4 * D), F32)
    dy_copies = []
    do_copies = []
    for slot in range(2):
        for array in range(2):
            core_copy(array, 0, slot).wait_recv()
            chip_copy(array, slot).wait_recv()

        def back(g, carry, slot=slot):
            row = slot * (BLK // 16) + g
            rows, normed, inverse, hidden, route, kept = routed(row)
            here = rows_at(g * 16, 16)

            def total(array):
                return (
                    own[array, 0, slot, here, :]
                    + crecv[array, 0, slot, here, :].astype(F32)
                    + qrecv[array, slot, here, :].astype(F32)
                )

            gate_one = modg[pl.ds(row, 1), 2 * D : 3 * D]
            gate_two = modg[pl.ds(row, 1), 5 * D : 6 * D]
            scale_two = modg[pl.ds(row, 1), 4 * D : 5 * D]
            grad = g2[rows, :].astype(F32)
            pass_on = kept * route
            branch = total(0) + b_down
            low = (mixed[rows, :] + gate_two * pass_on * branch).astype(BF16)

            @pl.when(p == slot)
            def _():
                fin_out[here, :] = low

            @pl.when(p != slot)
            def _():
                fin_send_out[here, :] = low

            grad_gate_two = grad * pass_on * branch
            gated = grad * gate_two
            logit = (
                jnp.sum(gated * branch, axis=1, keepdims=True) * kept * route * (1.0 - route)
            )
            dh = total(1) + logit * w_route
            e = dh * (1.0 + scale_two)
            dx = grad + inverse * (
                e
                - jnp.mean(e, axis=1, keepdims=True)
                - normed * jnp.mean(e * normed, axis=1, keepdims=True)
            )
            dx_out[rows, :] = dx
            dyb = dx * gate_one
            dy[slot, c, here, :] = dyb.astype(BF16)

            def down(v):
                return jnp.sum(v, axis=0, keepdims=True)

            small_out[0:1, :] += down(dyb)
            small_out[1:2, :] += down(gated * pass_on)
            small_out[2:3, :] += down(logit * hidden)
            at = pl.ds(row, 1)
            sums_out[at, 0:D] = down(dx * y1[rows, :])
            sums_out[at, D : 2 * D] = down(dh)
            sums_out[at, 2 * D : 3 * D] = down(dh * normed)
            sums_out[at, 3 * D : 4 * D] = down(grad_gate_two)
            return carry

        lax.fori_loop(0, BLK // 16, back, 0)
        copy = remote(dy.at[slot, c], dy.at[slot, c], sems, 39 + slot, c=1 - c)
        copy.start()
        dy_copies.append(copy)
    for slot in range(2):
        dy_copies[slot].wait_recv()
        rows = rows_at(place(slot, q, 0), 2 * BLK)
        grads = dy[slot].reshape(2 * BLK, D)
        dofar[slot] = nt(grads, wo[2 * QTR : 4 * QTR, :]).astype(BF16)
        copy = remote(dofar.at[slot], do_out.at[rows], sems, 41 + slot, q=1 - q)
        copy.start()
        do_copies.append(copy)
        do_out[rows, :] = nt(grads, wo[0 : 2 * QTR, :]).astype(BF16)

    def out_grad(left):
        return sum(tn(left(slot), dy[slot].reshape(2 * BLK, D)) for slot in range(2))

    gwo_far_out[...] = out_grad(lambda slot: o_in[slot]).astype(BF16)
    gwo_out[...] = out_grad(lambda slot: o[rows_at(place(slot, q, 0), 2 * BLK), :]).astype(BF16)
    for copy in do_copies:
        copy.wait_recv()
    for copy in o_copies + y_copies + dy_copies + do_copies:
        copy.wait_send()
    for total in (down_sum, up_sum):
        total.landed()
        total.sent(second=False)
    for slot in range(2):
        for array in range(2):
            for kind in range(3):
                hop(array, slot, kind).wait_send()
            for side in range(2):
                core_copy(array, side, slot).wait_send()
            chip_copy(array, slot).wait_send()
    for copy in waits:
        copy.wait()


def middle(*args):
    return pl.pallas_call(
        middle_kernel,
        out_shape=(
            shape_of(BLK, D), shape_of(BLK, D), shape_of(2 * BLK, D, dtype=F32),
            shape_of(SEQ, NH * HD), shape_of(GROUPS, 4 * D, dtype=F32), shape_of(8, D, dtype=F32),
            shape_of(2, WROWS, D), shape_of(2, WROWS, D), shape_of(NH * HD, D),
            shape_of(NH * HD, D), shape_of(8, D, dtype=F32),
        )
        + (shape_of(2, 2, CUT, D), shape_of(2, 2, QTR - CUT, D)) * 2,
        in_specs=[VMEM_SPEC] * 6 + [ANY_SPEC] * 3 + [VMEM_SPEC] * 3,
        out_specs=(
            VMEM_SPEC, VMEM_SPEC, VMEM_SPEC, VMEM_SPEC, VMEM_SPEC, VMEM_SPEC, ANY_SPEC, ANY_SPEC,
            VMEM_SPEC, VMEM_SPEC, VMEM_SPEC, VMEM_SPEC, VMEM_SPEC, VMEM_SPEC, VMEM_SPEC,
        ),
        scratch_shapes=[
            pltpu.VMEM((2, 2 * BLK, NH * HD), BF16),
            pltpu.VMEM((2 * BLK, D), F32),
            pltpu.VMEM((2, BLK, D), BF16),
            pltpu.VMEM((2, BLK, D), BF16),
            pltpu.VMEM((2 * BLK, D), F32),
            pltpu.VMEM((2 * BLK, D), F32),
            pltpu.VMEM((SEQ, D), BF16),
            pltpu.VMEM((SEQ, D), BF16),
            pltpu.VMEM((SEQ, D), BF16),
            pltpu.VMEM((SEQ, D), BF16),
            pltpu.VMEM((2, WROWS, D), BF16),
            pltpu.VMEM((2, WROWS, D), BF16),
            pltpu.VMEM((2, 2, 2, BLK, D), F32),
            pltpu.VMEM((2, 2, 2, BLK, D), BF16),
            pltpu.VMEM((2, 2, 2, BLK, D), BF16),
            pltpu.VMEM((2, 2, BLK, D), BF16),
            pltpu.VMEM((2, 2, BLK, D), BF16),
            pltpu.VMEM((2, 2, BLK, D), BF16),
            pltpu.VMEM((2, 2 * BLK, NH * HD), BF16),
            pltpu.SemaphoreType.DMA((67,)),
            pltpu.SemaphoreType.DMA((67,)),
            pltpu.SemaphoreType.DMA((7,)),
        ],
        compiler_params=pltpu.CompilerParams(
            collective_id=7, has_side_effects=True, vmem_limit_bytes=63 * 2**20
        ),
        name="middle",
    )(*args)


class LineReduce:
    def __init__(self, reduce, half, out, sems, k, y, x, p):
        self.reduce, self.half, self.out = reduce, half, out
        self.mine = rows_at((y * 2 + x) * QTR, QTR)
        self.over = remote(half.at[0], half.at[1], sems, k, p=1 - p)
        mine = out.at[self.mine]
        self.to_x = remote(mine, mine, sems, k + 1, x=1 - x)
        self.to_y = remote(mine, mine, sems, k + 2, y=1 - y)
        from_x = out.at[rows_at((y * 2 + 1 - x) * QTR, CUT)]
        from_y = out.at[rows_at(((1 - y) * 2 + x) * QTR + CUT, QTR - CUT)]
        self.on_y = remote(from_x, from_x, sems, k + 3, y=1 - y)
        self.on_x = remote(from_y, from_y, sems, k + 4, x=1 - x)

    def start(self):
        self.reduce.arrive()
        low, high = self.reduce.total(1)
        self.half[0, :CUT] = low.astype(BF16)
        self.half[0, CUT:] = high.astype(BF16)
        self.over.start()

    def spread(self):
        low, high = self.reduce.total(0)
        self.over.wait_recv()
        start = (self.reduce.y * 2 + self.reduce.x) * QTR
        self.out[rows_at(start, CUT), :] = (low + self.half[1, :CUT].astype(F32)).astype(BF16)
        self.out[rows_at(start + CUT, QTR - CUT), :] = (
            high + self.half[1, CUT:].astype(F32)
        ).astype(BF16)
        self.to_x.start()
        self.to_y.start()

    def forward(self):
        self.to_x.wait_recv()
        self.on_y.start()
        self.to_y.wait_recv()
        self.on_x.start()

    def finish(self):
        self.on_y.wait_recv()
        self.on_x.wait_recv()

    def sent(self):
        for copy in (self.over, self.to_x, self.to_y, self.on_y, self.on_x):
            copy.wait_send()


def back_kernel(
    d, h1, wide, x2, dx, scale, sums_two, smalls, b_up, up_g, down_g, wo_g, wo_in, hot, spread,
    ada, slope, down_low, down_high, up_low, up_high,
    tokens_out, a_out, up_out, down_out, mod_out, cond_out,
    own, csend, crecv, qsend, qrecv, wideg, grads, sums, parcel, parcels, lsum, modline, condbuf,
    tsend, halves, *rest,
):
    bufs = [(down_low, down_high) + rest[0:4], (up_low, up_high) + rest[4:8], rest[8:14]]
    send, recv, loc = rest[14:]
    y, x, p, q, c = (lax.axis_index(name) for name in "yxpqc")
    sems = (send, recv)
    pair = [
        {"q": lax.rem(q + k // 2, 2), "c": lax.rem(c + k % 2, 2)} for k in range(1, 4)
    ]
    plane = [{"y": lax.rem(y + k // 2, 2), "x": lax.rem(x + k % 2, 2)} for k in range(1, 4)]
    greet(pair + plane + [{"p": 1 - p}])
    rank = y * 2 + x

    def keep_local(src, dst, k):
        copy = pltpu.make_async_copy(src, dst, loc.at[k])
        copy.start()
        return copy

    def place(slot, chip, core):
        return slot * HALF + chip * (2 * BLK) + core * BLK

    outs = (down_out, up_out, a_out)
    reduces = [PlaneReduce(grads.at[k], bufs[k], sems, 6 * k, y, x, landed=k < 2) for k in range(3)]
    lines = [
        LineReduce(reduces[k], halves.at[k], outs[k], sems, 18 + 5 * k, y, x, p)
        for k in range(3)
    ]
    loads = [keep_local(down_g, grads.at[0], 0), keep_local(up_g, grads.at[1], 1)]
    for k in range(2):
        loads[k].wait()
        reduces[k].middle()

    def weight_chunk(j, carry):
        cols = pl.ds(pl.multiple_of(j * 384, LANES), 384)
        wideg[rows_at(j * 384, 384), :] = tn(d[:, cols], h1[...]).astype(BF16)
        return carry

    lax.fori_loop(0, 4, weight_chunk, 0)
    for shard in range(2):
        grads[2, shard, :UNIT_ROWS, :] = tn(
            spread[...], wideg[shard * 6 * LANES : (shard + 1) * 6 * LANES, :]
        ).astype(BF16)
        rows = slice(shard * QTR, (shard + 1) * QTR)
        grads[2, shard, UNIT_ROWS:, :] = (
            wo_g[rows, :].astype(F32) + wo_in[rows, :].astype(F32)
        ).astype(BF16)
    reduces[2].start()
    lines[0].start()
    lines[1].start()

    def core_copy(side, slot):
        return remote(
            csend.at[side, slot], crecv.at[side, slot], sems, 34 + side * 2 + slot, c=1 - c
        )

    def chip_copy(slot):
        return remote(qsend.at[slot], qrecv.at[slot], sems, 38 + slot, q=1 - q)

    def far_out(slot):
        core_copy(1, slot).wait_recv()
        qsend[slot] = (own[1, slot] + crecv[1, slot].astype(F32)).astype(BF16)
        chip_copy(slot).start()

    def through(step, carry):
        side, slot = 1 - step // 2, lax.rem(step, 2)
        start = place(slot, lax.rem(q + side, 2), 0)
        rows = rows_at(start, 2 * BLK)
        part = jnp.dot(d[rows, :], wide[...], preferred_element_type=F32)

        @pl.when(c == 0)
        def _():
            own[side, slot] = part[:BLK]
            csend[side, slot] = part[BLK:].astype(BF16)

        @pl.when(c == 1)
        def _():
            own[side, slot] = part[BLK:]
            csend[side, slot] = part[:BLK].astype(BF16)

        core_copy(side, slot).start()

        @pl.when(step == 1)
        def _():
            far_out(0)

        @pl.when(step == 2)
        def _():
            far_out(1)

        return carry

    lax.fori_loop(0, 4, through, 0)

    ones = jnp.ones((8, SEQ), BF16)
    col_sums = jnp.dot(ones, d[...], preferred_element_type=F32)

    reduces[2].landed()
    reduces[2].middle()
    lines[0].spread()
    lines[2].start()
    lines[0].forward()

    sums[...] = jnp.zeros_like(sums)
    for slot in range(2):
        core_copy(0, slot).wait_recv()
        chip_copy(slot).wait_recv()

        def group(g, carry, slot=slot):
            row = slot * (BLK // 16) + g
            rows = rows_at(row * 16, 16)
            here = rows_at(g * 16, 16)
            normed, inverse = norm_tile(x2[rows, :].astype(F32))
            dh = (
                own[0, slot, here, :]
                + crecv[0, slot, here, :].astype(F32)
                + qrecv[slot, here, :].astype(F32)
            )
            at = pl.ds(row, 1)
            e = dh * (1.0 + scale[at, :])
            out = dx[rows, :] + inverse * (
                e
                - jnp.mean(e, axis=1, keepdims=True)
                - normed * jnp.mean(e * normed, axis=1, keepdims=True)
            )
            tsend[slot, here, :] = out.astype(BF16)

            @pl.when(slot == p)
            def _():
                tokens_out[p, here, :] = out

            sums[at, 0:D] = jnp.sum(dh, axis=0, keepdims=True)
            sums[at, D : 2 * D] = jnp.sum(dh * normed, axis=0, keepdims=True)
            return carry

        lax.fori_loop(0, BLK // 16, group, 0)

    token_copy = remote(tsend.at[1 - p], tsend.at[2], sems, 40, p=1 - p)
    two = jnp.concatenate([sums[...], sums_two[...]], axis=1)
    full = lax.dot_general(
        hot[...], two, (((0,), (0,)), ((), ())), preferred_element_type=F32,
        precision=lax.Precision.HIGHEST,
    )
    for k in range(8):
        there = parcel.at[k // 4, (k // 2) % 2, k % 2]
        there[...] = full[:, k * MODS : (k + 1) * MODS]
        there[11:14, : D // 8] = smalls[0:3, k * (D // 8) : (k + 1) * (D // 8)]
    for shard in range(2):
        heads = col_sums[0:1, shard * 6 * LANES : (shard + 1) * 6 * LANES]
        pieces = [b_up[0:1, shard * WROWS : (shard + 1) * WROWS]]
        for unit in (0, 2, 3, 5):
            pieces.append(heads[:, unit * LANES : unit * LANES + HD])
        parcel[lax.rem(p + shard, 2), q, c, 14:15, :] = jnp.concatenate(pieces, axis=1)
    here = q * 2 + c
    copies = []
    for k, where in enumerate(pair):
        copy = remote(
            parcel.at[:, where["q"], where["c"]], parcels.at[here], sems, 41 + k, **where
        )
        copy.start()
        copies.append(copy)
    own_parcel = keep_local(parcel.at[:, q, c], parcels.at[here], 3)
    own_parcel.wait()
    for copy in copies:
        copy.wait_recv()
    line_sum = sum(parcels[k] for k in range(4))
    lsum[0:2] = line_sum
    over = remote(lsum.at[1 - p], lsum.at[2], sems, 44, p=1 - p)
    over.start()
    copies.append(over)
    token_copy.start()
    lines[1].spread()
    over.wait_recv()
    modline[p] = lsum[p].astype(BF16)
    modline[1 - p] = lsum[2].astype(BF16)
    mods = []
    for k, where in enumerate(plane):
        copy = remote(modline, mod_out.at[rank], sems, 48 + k, **where)
        copy.start()
        mods.append(copy)
    own_mod = keep_local(modline, mod_out.at[rank], 4)

    condbuf[0] = jnp.dot(
        modline[...].reshape(32, MODS), ada[...], preferred_element_type=F32
    ).astype(BF16)
    conds = []
    for k, where in enumerate(({"c": 1 - c}, {"q": 1 - q}, {"p": 1 - p})):
        copy = remote(condbuf.at[2 * k], condbuf.at[2 * k + 1], sems, 51 + k, **where)
        copy.start()
        conds.append(copy)
        if k == 0:
            lines[1].forward()
        if k == 1:
            lines[2].spread()
        copy.wait_recv()
        total = condbuf[2 * k].astype(F32) + condbuf[2 * k + 1].astype(F32)
        if k < 2:
            condbuf[2 * k + 2] = total.astype(BF16)
    cond_out[...] = total * slope[...]

    lines[2].forward()
    token_copy.wait_recv()
    tokens_out[1 - p] = tsend[2].astype(F32)
    for k in range(3):
        lines[k].finish()
    for copy in mods:
        copy.wait_recv()
    for copy in [token_copy] + copies + mods + conds:
        copy.wait_send()
    for slot in range(2):
        for side in range(2):
            core_copy(side, slot).wait_send()
        chip_copy(slot).wait_send()
    for k in range(3):
        reduces[k].sent()
        lines[k].sent()
    own_mod.wait()


def back(*args):
    return pl.pallas_call(
        back_kernel,
        out_shape=(
            shape_of(2, BLK, D, dtype=F32), shape_of(WROWS, D), shape_of(WROWS, D),
            shape_of(WROWS, D), shape_of(4, 2, 16, MODS), shape_of(32, D, dtype=F32),
        ),
        in_specs=[VMEM_SPEC] * 9 + [ANY_SPEC] * 2 + [VMEM_SPEC] * 10,
        out_specs=(VMEM_SPEC,) * 6,
        scratch_shapes=[
            pltpu.VMEM((2, 2, BLK, D), F32),
            pltpu.VMEM((2, 2, BLK, D), BF16),
            pltpu.VMEM((2, 2, BLK, D), BF16),
            pltpu.VMEM((2, BLK, D), BF16),
            pltpu.VMEM((2, BLK, D), BF16),
            pltpu.VMEM((WIDE, D), BF16),
            pltpu.VMEM((3, 2, WROWS, D), BF16),
            pltpu.VMEM((GROUPS, 2 * D), F32),
            pltpu.VMEM((2, 2, 2, 16, MODS), F32),
            pltpu.VMEM((4, 2, 16, MODS), F32),
            pltpu.VMEM((3, 16, MODS), F32),
            pltpu.VMEM((2, 16, MODS), BF16),
            pltpu.VMEM((6, 32, D), BF16),
            pltpu.VMEM((3, BLK, D), BF16),
            pltpu.VMEM((3, 2, QTR, D), BF16),
        ]
        + REDUCE_SCRATCH[2:] * 2
        + REDUCE_SCRATCH
        + [
            pltpu.SemaphoreType.DMA((54,)),
            pltpu.SemaphoreType.DMA((54,)),
            pltpu.SemaphoreType.DMA((5,)),
        ],
        compiler_params=pltpu.CompilerParams(
            collective_id=8, has_side_effects=True, vmem_limit_bytes=63 * 2**20
        ),
        name="back",
    )(*args)


def swap(values, axis):
    return lax.ppermute(values, axis, SWAP)


def layer_device(
    tokens, cond, lengths, pads, timesteps, head_mask, group_mask, keep, ada_w, ada_b, w_qkv, b_qv,
    w_out, b_out, w_up, b_up, w_down, b_down, w_route, grad_out,
):
    highest = lax.Precision.HIGHEST
    y, x, p, q, c = (lax.axis_index(name) for name in "yxpqc")
    rank = y * 2 + x
    first = p == 0
    shard = p * 4 + q * 2 + c
    partner = shard ^ 4

    spread = np.zeros((6 * LANES, UNIT_ROWS), np.float32)
    for unit in range(6):
        spread[np.arange(HD) + unit * LANES, np.arange(HD) + unit * HD] = 1.0
    spread = jnp.asarray(spread, BF16)
    w_up_rows = jnp.transpose(w_up)
    w_a = jnp.concatenate([jnp.transpose(w_qkv), w_out])
    pairs = b_qv.reshape(2, 2, HD).astype(F32)
    bias_own = jnp.pad(
        jnp.stack([pairs[:, 0], jnp.zeros_like(pairs[:, 0]), pairs[:, 1]], axis=1),
        ((0, 0), (0, 0), (0, LANES - HD)),
    ).reshape(6 * LANES)
    bias_own = jnp.pad(jnp.concatenate([bias_own, b_up.astype(F32)]), (0, BIAS - 1344))
    bias_own = jnp.broadcast_to(bias_own, (8, BIAS))

    def row_of(values):
        return jnp.where(first, values[0], values[1])

    row_len = row_of(lengths)
    row_pad = row_of(pads)
    ends = jnp.cumsum(row_len)
    starts = ends - row_len

    def group_hot(dq, dc):
        base = (q ^ dq) * (2 * BLK) + (c ^ dc) * BLK
        places = base + jnp.arange(2)[:, None] * HALF + jnp.arange(BLK // 16)[None, :] * 16
        inside = (places[..., None] >= starts) & (places[..., None] < ends)
        return jnp.pad(inside.astype(F32), ((0, 0), (0, 0), (0, 5)))

    hot = group_hot(0, 0)
    hot_rows = jnp.pad(hot.reshape(22, 16), ((0, 2), (0, 0)))

    def by_row(values):
        return jnp.transpose(values, (1, 0, 2))

    def items(values):
        return jnp.pad(values, ((0, 0), (0, 5), (0, 0))).reshape(32, -1)

    keep_wide = jnp.broadcast_to(keep.T.astype(BF16)[..., None], (2, BLK, LANES))
    ada_rows = jnp.transpose(ada_w)
    (
        triple, hidden_one, token_low, keep_low, grad_low, mod_groups, w_wide, w_out_all, biases,
        act_all, slope,
    ) = front(
        items(cond.astype(F32) + time_embed(timesteps)), by_row(tokens), keep_wide, by_row(grad_out), bias_own, w_a, spread,
        hot_rows, ada_rows, ada_b.astype(F32)[None],
    )
    up_quarter, triple = lax.optimization_barrier(
        (lax.dynamic_slice_in_dim(w_up_rows, rank * QTR, QTR, 0), triple)
    )
    up_quarter = swap(up_quarter, "p")

    head_row = row_of(head_mask)
    heads_here = jnp.concatenate(
        [
            lax.dynamic_slice_in_dim(head_row, shard * 2, 2, 1),
            lax.dynamic_slice_in_dim(head_row, partner * 2, 2, 1),
        ],
        axis=1,
    )
    scal = jnp.concatenate(
        [
            starts,
            row_len // UNIT,
            row_len - row_pad,
            heads_here.reshape(-1),
        ]
    ).astype(jnp.int32)
    pack = np.zeros((NH * LANES, NH * HD), np.float32)
    for head in range(NH):
        pack[np.arange(HD) + head * LANES, np.arange(HD) + head * HD] = 1.0
    pack = jnp.asarray(pack, BF16)
    attended, lse = attn_fwd(scal, triple, pack)
    group_row = row_of(group_mask)
    groups_here = jnp.concatenate(
        [
            lax.dynamic_slice_in_dim(group_row, shard * 2, 2, 1),
            lax.dynamic_slice_in_dim(group_row, partner * 2, 2, 1),
        ],
        axis=1,
    ).astype(F32)
    all_places = jnp.arange(SEQ // 16)[:, None] * 16
    all_hot = ((all_places >= starts) & (all_places < ends)).astype(F32)
    group_wide = jnp.repeat(
        jnp.dot(all_hot, groups_here, precision=highest), GW, axis=1
    )
    consts = jnp.pad(jnp.stack([b_out, b_down, w_route]).astype(F32), ((0, 5), (0, 0)))
    b_up_two = jnp.concatenate([biases[0, :, 768:1344], biases[1, :, 768:1344]], axis=1)
    (
        final, final_send, grad_mixed, grad_attended, sums_two, smalls, up_low, down_low, wo_low, wo_far,
        b_up_sums, *landed,
    ) = middle(
        attended, token_low.reshape(2 * BLK, D), keep_low.reshape(2 * BLK, LANES), mod_groups,
        grad_low.reshape(2 * BLK, D), w_out_all.reshape(4 * QTR, D), w_up_rows, up_quarter, w_down,
        b_up_two, consts, group_wide,
    )
    wo_in = swap(wo_far, "q")
    final_in = swap(final_send, "p")
    final_pair = jnp.stack([jnp.where(first, final, final_in), jnp.where(first, final_in, final)])
    d_all = attn_bwd(scal, triple, grad_attended, lse, pack)
    token_pair, low_a, low_up, low_down, mod_all, grad_cond = back(
        d_all, hidden_one, w_wide, token_low.reshape(2 * BLK, D), grad_mixed,
        mod_groups[:, D : 2 * D], sums_two, smalls, b_up_sums, up_low, down_low, wo_low, wo_in,
        hot_rows, spread, ada_rows, slope, *landed,
    )
    out_a = low_a.astype(F32)
    mod_low = jnp.where(jnp.arange(16)[:, None] < CROPS, mod_all, 0)
    grad_ada_w = tn(mod_low.reshape(128, MODS), act_all.reshape(128, D))
    grad_ada_b = jnp.sum(mod_low, axis=(0, 1, 2), dtype=F32)
    rest = jnp.sum(mod_all[:, :, CROPS:], axis=(0, 1), dtype=F32)
    return (
        by_row(final_pair), by_row(token_pair), grad_cond.reshape(2, 16, D)[:, :CROPS],
        jnp.transpose(grad_ada_w), grad_ada_b, jnp.transpose(out_a[:UNIT_ROWS]), rest[3, 2 * GW :],
        out_a[UNIT_ROWS:], rest[0, : D // 8], jnp.transpose(low_up.astype(F32)), rest[3, : 2 * GW],
        low_down.astype(F32), rest[1, : D // 8], rest[2, : D // 8],
    )


IN_SPECS = (
    ("heads", "rows", None), ("rows", None, None), ("rows", None), ("rows", None), ("rows", None),
    ("rows", None, None), ("rows", None, None), ("heads", "rows"), (None, "heads"), ("heads",),
    (None, "heads"), ("heads",), ("heads", None), (), (None, "heads"), ("heads",), ("heads", None),
    (), (), ("heads", "rows", None),
)
OUT_SPECS = (
    ("heads", "rows", None), ("heads", "rows", None), ("rows", None, None), (None, "heads"),
    ("heads",), (None, "heads"), ("heads",), ("heads", None), ("heads",), (None, "heads"),
    ("heads",), ("heads", None), ("heads",), ("heads",),
)


def solution(mesh):
    paired = mesh.shape["rows"] == 4 and mesh.shape["heads"] == 8
    if paired:
        mesh = Mesh(mesh.devices.reshape(2, 2, 2, 2, 2), ("y", "x", "p", "q", "c"))
        names = {"rows": ("y", "x"), "heads": ("p", "q", "c"), None: None}
    else:
        names = {"rows": "rows", "heads": "heads", None: None}

    def specs(items):
        return tuple(P(*(names[name] for name in item)) for item in items)

    return jax.shard_map(
        layer_device if paired else per_device,
        mesh=mesh,
        in_specs=specs(IN_SPECS),
        out_specs=specs(OUT_SPECS),
        check_vma=False,
    )
```

```python
import math

import jax
import jax.numpy as jnp
import numpy as np
from jax import lax
from jax.experimental import pallas as pl
from jax.experimental.pallas import tpu as pltpu
from jax.sharding import Mesh
from jax.sharding import PartitionSpec as P

D = 1152
H = 16
HD = 72
GW = 288
SEQ = 1408
CROPS = 11
UNIT = 64
LANES = 128
EPSILON = 1e-06
MASKED_SCORE = -1000000000.0
MESH = pl.DeviceIdType.MESH
SWAP = [(0, 1), (1, 0)]
F32 = jnp.float32
BF16 = jnp.bfloat16
SCALE = HD ** (-0.5)


def time_embed(timesteps):
    halves = D // 2
    frequency = jnp.exp(-math.log(10000.0) * jnp.arange(halves, dtype=jnp.float32) / halves)
    angles = timesteps.astype(jnp.float32)[..., None] * frequency
    return jnp.concatenate([jnp.cos(angles), jnp.sin(angles)], axis=-1)


def gelu_tanh(values):
    return (
        0.5
        * values
        * (1.0 + jnp.tanh(0.7978845608028654 * (values + 0.044715 * values * values * values)))
    )


def norm_rows(values):
    average = jnp.mean(values, axis=-1, keepdims=True)
    centred = values - average
    inverse_dev = lax.rsqrt(jnp.mean(centred * centred, axis=-1, keepdims=True) + EPSILON)
    return (centred * inverse_dev, inverse_dev)


def norm_back(grad_normed, normed, inverse_dev):
    first_mean = jnp.mean(grad_normed, axis=-1, keepdims=True)
    second_mean = jnp.mean(grad_normed * normed, axis=-1, keepdims=True)
    return inverse_dev * (grad_normed - first_mean - normed * second_mean)


def crop_layout(lengths, pads, offset, amount):
    crop_ends = jnp.cumsum(lengths, axis=1)
    starts = crop_ends - lengths
    places = offset + jnp.arange(amount, dtype=jnp.int32)
    inside = (places[:, None, None] >= starts[None]) & (places[:, None, None] < crop_ends[None])
    live_part = places[:, None, None] < (crop_ends - pads)[None]
    one_hot = inside.astype(jnp.float32)
    item_ids = jnp.sum(
        inside.astype(jnp.int32) * jnp.arange(lengths.shape[1], dtype=jnp.int32), axis=2
    )
    valid = jnp.sum((inside & live_part).astype(jnp.float32), axis=2)
    return (one_hot, item_ids, valid)


def masked_scores(queries, key_rows, item_row, key_live, score_scale):
    raw = jnp.einsum("shd,thd->hst", queries, key_rows, preferred_element_type=jnp.float32)
    allowed = (item_row[:, None] == item_row[None, :]) & key_live[None, :]
    return jnp.where(allowed[None], raw * score_scale, MASKED_SCORE)


def attend_row(triple_row, item_row, key_live, score_scale):
    queries = triple_row[:, :, 0]
    key_rows = triple_row[:, :, 1]
    values = triple_row[:, :, 2]
    scores = masked_scores(queries, key_rows, item_row, key_live, score_scale)
    row_top = jnp.max(scores, axis=-1, keepdims=True)
    log_total = row_top + jnp.log(jnp.sum(jnp.exp(scores - row_top), axis=-1, keepdims=True))
    probability = jnp.exp(scores - log_total).astype(jnp.bfloat16)
    attended = jnp.einsum("hst,thd->shd", probability, values, preferred_element_type=jnp.float32)
    return (attended, log_total)


def attend_back(triple_row, grad_row, total_row, item_row, key_live, score_scale):
    queries = triple_row[:, :, 0]
    key_rows = triple_row[:, :, 1]
    values = triple_row[:, :, 2]
    scores = masked_scores(queries, key_rows, item_row, key_live, score_scale)
    probability = jnp.exp(scores - total_row)
    grad_prob = jnp.einsum("shd,thd->hst", grad_row, values, preferred_element_type=jnp.float32)
    grad_values = jnp.einsum(
        "hst,shd->thd",
        probability.astype(jnp.bfloat16),
        grad_row,
        preferred_element_type=jnp.float32,
    )
    inner = jnp.sum(probability * grad_prob, axis=-1, keepdims=True)
    grad_raw = (probability * (grad_prob - inner) * score_scale).astype(jnp.bfloat16)
    grad_queries = jnp.einsum(
        "hst,thd->shd", grad_raw, key_rows, preferred_element_type=jnp.float32
    )
    grad_keys = jnp.einsum("hst,shd->thd", grad_raw, queries, preferred_element_type=jnp.float32)
    return jnp.stack([grad_queries, grad_keys, grad_values], axis=2).astype(jnp.bfloat16)


def project_rows(source, weight):
    return jnp.einsum("sbk,kd->sbd", source, weight, preferred_element_type=jnp.float32)


def back_rows(source, weight):
    return jnp.einsum("sbk,dk->sbd", source, weight, preferred_element_type=jnp.float32)


def per_device(
    tokens,
    cond,
    lengths,
    pads,
    timesteps,
    head_mask,
    group_mask,
    keep,
    ada_w,
    ada_b,
    w_qkv,
    b_qv,
    w_out,
    b_out,
    w_up,
    b_up,
    w_down,
    b_down,
    w_route,
    grad_out,
):
    highest = lax.Precision.HIGHEST
    groups = lax.axis_size("heads")
    head_rank = lax.axis_index("heads")
    shard_len = tokens.shape[0]
    batch_local = tokens.shape[1]
    local_heads = H // groups
    score_scale = HD ** (-0.5)
    local_hot, local_items, local_valid = crop_layout(
        lengths, pads, head_rank * shard_len, shard_len
    )
    full_hot, full_items, full_valid = crop_layout(lengths, pads, 0, SEQ)
    cond_all = cond.astype(jnp.float32) + time_embed(timesteps)
    sigmoid_cond = lax.logistic(cond_all)
    silu_low = (cond_all * sigmoid_cond).astype(jnp.bfloat16)
    modulation_part = jnp.einsum(
        "bcd,dm->bcm", silu_low, ada_w, preferred_element_type=jnp.float32
    ) + ada_b.astype(jnp.float32)
    modulation = lax.all_gather(modulation_part, "heads", axis=2, tiled=True)
    token_mod = jnp.einsum("sbc,bcm->sbm", local_hot, modulation, precision=highest)
    shift_one, scale_one, gate_one, shift_two, scale_two, gate_two = jnp.split(
        token_mod, 6, axis=-1
    )
    token_values = tokens.astype(jnp.float32)
    normed_one, inverse_one = norm_rows(token_values)
    hidden_one = (normed_one * (1.0 + scale_one) + shift_one).astype(jnp.bfloat16)
    hidden_all = lax.all_gather(hidden_one, "heads", axis=0, tiled=True)
    bias_pairs = b_qv.astype(jnp.float32).reshape(local_heads, 2, HD)
    bias_triple = jnp.stack(
        [bias_pairs[:, 0], jnp.zeros_like(bias_pairs[:, 0]), bias_pairs[:, 1]], axis=1
    ).reshape(-1)
    triple_all = (
        jnp.einsum("sbd,dm->sbm", hidden_all, w_qkv, preferred_element_type=jnp.float32)
        + bias_triple
    ).astype(jnp.bfloat16)
    triple_rows = jnp.moveaxis(triple_all.reshape(SEQ, batch_local, local_heads, 3, HD), 1, 0)
    item_rows = jnp.transpose(full_items)
    live_rows = jnp.transpose(full_valid > 0.5)
    attended, totals = lax.map(
        lambda packed: attend_row(packed[0], packed[1], packed[2], score_scale),
        (triple_rows, item_rows, live_rows),
    )
    head_table = lax.dynamic_slice_in_dim(
        head_mask, head_rank * local_heads, local_heads, 2
    ).astype(jnp.float32)
    head_full = jnp.einsum("sbc,bch->sbh", full_hot, head_table, precision=highest)
    out_mask = head_full * full_valid[..., None]
    attn_low = (
        (jnp.moveaxis(attended, 0, 1) * out_mask[..., None])
        .reshape(SEQ, batch_local, local_heads * HD)
        .astype(jnp.bfloat16)
    )
    projected = lax.psum_scatter(
        project_rows(attn_low, w_out), "heads", scatter_dimension=0, tiled=True
    )
    b_out_values = b_out.astype(jnp.float32)
    mixed = token_values + gate_one * (projected + b_out_values)
    normed_two, inverse_two = norm_rows(mixed)
    hidden_two = normed_two * (1.0 + scale_two) + shift_two
    hidden_two_low = hidden_two.astype(jnp.bfloat16)
    route_values = w_route.astype(jnp.float32)
    route = lax.logistic(jnp.einsum("sbd,d->sb", hidden_two, route_values, precision=highest))
    keep_values = keep.astype(jnp.float32)
    route_keep = keep_values * route
    group_table = lax.dynamic_slice_in_dim(
        group_mask, head_rank * local_heads, local_heads, 2
    ).astype(jnp.float32)
    hidden_two_all = lax.all_gather(hidden_two_low, "heads", axis=0, tiled=True)
    group_tok = jnp.einsum("sbc,bch->sbh", full_hot, group_table, precision=highest)
    upper = jnp.einsum(
        "sbd,dk->sbk", hidden_two_all, w_up, preferred_element_type=jnp.float32
    ) + b_up.astype(jnp.float32)
    active, gelu_back = jax.vjp(gelu_tanh, upper)
    group_wide = jnp.repeat(group_tok, GW, axis=-1)
    active_low = (active * group_wide).astype(jnp.bfloat16)
    lowered = lax.psum_scatter(
        project_rows(active_low, w_down), "heads", scatter_dimension=0, tiled=True
    )
    branch = lowered + b_down.astype(jnp.float32)
    final = mixed + gate_two * route_keep[..., None] * branch
    grad_final = grad_out.astype(jnp.float32)
    grad_branch = grad_final * gate_two * route_keep[..., None]
    grad_gate_two = grad_final * route_keep[..., None] * branch
    grad_route = jnp.sum(grad_final * gate_two * branch, axis=-1) * keep_values
    grad_logit = grad_route * route * (1.0 - route)
    part_route = jnp.einsum("sb,sbd->d", grad_logit, hidden_two, precision=highest)
    part_b_down = jnp.sum(grad_branch, axis=(0, 1))
    grad_low = grad_branch.astype(jnp.bfloat16)
    grad_all = lax.all_gather(grad_low, "heads", axis=0, tiled=True)
    grad_active = jnp.einsum("sbd,kd->sbk", grad_all, w_down, preferred_element_type=jnp.float32)
    (grad_upper,) = gelu_back(grad_active * group_wide)
    upper_low = grad_upper.astype(jnp.bfloat16)
    grad_w_up = jnp.einsum(
        "sbd,sbk->dk", hidden_two_all, upper_low, preferred_element_type=jnp.float32
    )
    grad_b_up = jnp.sum(upper_low, axis=(0, 1), dtype=jnp.float32)
    grad_w_down = jnp.einsum(
        "sbk,sbd->kd", active_low, grad_all, preferred_element_type=jnp.float32
    )
    grad_hidden_two = lax.psum_scatter(
        back_rows(upper_low, w_up), "heads", scatter_dimension=0, tiled=True
    )
    grad_hidden_two = grad_hidden_two + grad_logit[..., None] * route_values
    grad_scale_two = grad_hidden_two * normed_two
    grad_mixed = grad_final + norm_back(
        grad_hidden_two * (1.0 + scale_two), normed_two, inverse_two
    )
    grad_gate_one = grad_mixed * (projected + b_out_values)
    grad_projected = grad_mixed * gate_one
    part_b_out = jnp.sum(grad_projected, axis=(0, 1))
    projected_low = grad_projected.astype(jnp.bfloat16)
    grad_proj_all = lax.all_gather(projected_low, "heads", axis=0, tiled=True)
    grad_attn = jnp.einsum(
        "sbd,kd->sbk", grad_proj_all, w_out, preferred_element_type=jnp.float32
    ).astype(jnp.bfloat16)
    grad_w_out = jnp.einsum(
        "sbk,sbd->kd", attn_low, grad_proj_all, preferred_element_type=jnp.float32
    )
    grad_masked = grad_attn.reshape(SEQ, batch_local, local_heads, HD) * out_mask[..., None].astype(
        jnp.bfloat16
    )
    grad_rows = jnp.moveaxis(grad_masked, 1, 0)
    grad_triple_rows = lax.map(
        lambda packed: attend_back(
            packed[0], packed[1], packed[2], packed[3], packed[4], score_scale
        ),
        (triple_rows, grad_rows, totals, item_rows, live_rows),
    )
    grad_triple = jnp.moveaxis(grad_triple_rows, 0, 1).reshape(
        SEQ, batch_local, local_heads * 3 * HD
    )
    grad_w_qkv = jnp.einsum(
        "sbd,sbm->dm", hidden_all, grad_triple, preferred_element_type=jnp.float32
    )
    bias_sums = jnp.sum(grad_triple, axis=(0, 1), dtype=jnp.float32).reshape(local_heads, 3, HD)
    grad_b_qv = jnp.stack([bias_sums[:, 0], bias_sums[:, 2]], axis=1).reshape(-1)
    grad_hidden_one = lax.psum_scatter(
        back_rows(grad_triple, w_qkv), "heads", scatter_dimension=0, tiled=True
    )
    grad_tokens = grad_mixed + norm_back(
        grad_hidden_one * (1.0 + scale_one), normed_one, inverse_one
    )
    grad_token_mod = jnp.concatenate(
        [
            grad_hidden_one,
            grad_hidden_one * normed_one,
            grad_gate_one,
            grad_hidden_two,
            grad_scale_two,
            grad_gate_two,
        ],
        axis=-1,
    )
    part_mod = jnp.einsum("sbc,sbm->bcm", local_hot, grad_token_mod, precision=highest)
    grad_mod, share_b_out, share_b_down, share_route = (
        lax.psum_scatter(part_mod, "heads", scatter_dimension=2, tiled=True),
        lax.psum_scatter(part_b_out, "heads", scatter_dimension=0, tiled=True),
        lax.psum_scatter(part_b_down, "heads", scatter_dimension=0, tiled=True),
        lax.psum_scatter(part_route, "heads", scatter_dimension=0, tiled=True),
    )
    mod_low = grad_mod.astype(jnp.bfloat16)
    grad_ada_w = jnp.einsum("bcd,bcm->dm", silu_low, mod_low, preferred_element_type=jnp.float32)
    grad_ada_b = jnp.sum(mod_low, axis=(0, 1), dtype=jnp.float32)
    part_activ = jnp.einsum("bcm,dm->bcd", mod_low, ada_w, preferred_element_type=jnp.float32)
    grad_activ = lax.psum(part_activ.astype(jnp.bfloat16), "heads").astype(jnp.float32)
    grad_cond = grad_activ * sigmoid_cond * (1.0 + cond_all * (1.0 - sigmoid_cond))
    summed = (
        lax.psum(grad_ada_w.astype(jnp.bfloat16), "rows").astype(jnp.float32),
        lax.psum(grad_ada_b.astype(jnp.bfloat16), "rows").astype(jnp.float32),
        lax.psum(grad_w_qkv.astype(jnp.bfloat16), "rows").astype(jnp.float32),
        lax.psum(grad_b_qv.astype(jnp.bfloat16), "rows").astype(jnp.float32),
        lax.psum(grad_w_out.astype(jnp.bfloat16), "rows").astype(jnp.float32),
        lax.psum(share_b_out.astype(jnp.bfloat16), "rows").astype(jnp.float32),
        lax.psum(grad_w_up.astype(jnp.bfloat16), "rows").astype(jnp.float32),
        lax.psum(grad_b_up.astype(jnp.bfloat16), "rows").astype(jnp.float32),
        lax.psum(grad_w_down.astype(jnp.bfloat16), "rows").astype(jnp.float32),
        lax.psum(share_b_down.astype(jnp.bfloat16), "rows").astype(jnp.float32),
        lax.psum(share_route.astype(jnp.bfloat16), "rows").astype(jnp.float32),
    )
    return (
        final.astype(jnp.bfloat16),
        grad_tokens,
        grad_cond,
        summed[0],
        summed[1],
        summed[2],
        summed[3],
        summed[4],
        summed[5],
        summed[6],
        summed[7],
        summed[8],
        summed[9],
        summed[10],
    )


BLK = 176
NH = 4
HALF = SEQ // 2


def each_crop(scal, body):
    def step(item, carry):
        units = scal[CROPS + item]
        for count in range(2, 9):

            @pl.when(units == count)
            def _():
                body(item, pl.multiple_of(scal[item], UNIT), count * UNIT)

        return carry

    lax.fori_loop(0, CROPS, step, 0)


def nt(a, b):
    return lax.dot_general(a, b, (((1,), (1,)), ((), ())), preferred_element_type=F32)


def tn(a, b):
    return lax.dot_general(a, b, (((0,), (0,)), ((), ())), preferred_element_type=F32)


def attn_fwd_kernel(scal, buf, pack, obuf, lse):
    lane = lax.broadcasted_iota(jnp.int32, (1, LANES), 1)

    def body(item, start, size):
        live = scal[2 * CROPS + item]
        keys_live = lax.broadcasted_iota(jnp.int32, (1, size), 1) < live
        rows_live = (lax.broadcasted_iota(jnp.int32, (size, 1), 0) < live).astype(F32)
        window = pl.ds(start, size)
        packed = jnp.zeros((size, NH * HD), F32)
        totals = jnp.zeros((size, LANES), F32)
        for head in range(NH):
            at = head * 3 * LANES
            queries = buf[window, at : at + LANES]
            keys = buf[window, at + LANES : at + 2 * LANES]
            values = buf[window, at + 2 * LANES : at + 3 * LANES]
            scores = jnp.where(keys_live, nt(queries, keys) * SCALE, MASKED_SCORE)
            top = jnp.max(scores, axis=1, keepdims=True)
            expo = jnp.exp(scores - top)
            total = jnp.sum(expo, axis=1, keepdims=True)
            prob = (expo * (1.0 / total)).astype(BF16)
            mixed = jnp.dot(prob, values, preferred_element_type=F32)
            mask = scal[3 * CROPS + item * NH + head].astype(F32)
            mixed = (mixed * (rows_live * mask)).astype(BF16)
            packed += jnp.dot(
                mixed, pack[head * LANES : (head + 1) * LANES, :], preferred_element_type=F32
            )
            totals = jnp.where(lane == head, top + jnp.log(total), totals)
        obuf[window, :] = packed.astype(BF16)
        lse[window, :] = totals

    each_crop(scal, body)


def attn_bwd_kernel(scal, buf, gbuf, lse, pack, dbuf):
    def body(item, start, size):
        live = scal[2 * CROPS + item]
        keys_live = lax.broadcasted_iota(jnp.int32, (1, size), 1) < live
        rows_live = lax.broadcasted_iota(jnp.int32, (size, 1), 0) < live
        window = pl.ds(start, size)
        grads = gbuf[window, :]
        grads = jnp.where(rows_live, grads.astype(F32), 0.0).astype(BF16)
        for head in range(NH):
            at = head * 3 * LANES
            queries = buf[window, at : at + LANES]
            keys = buf[window, at + LANES : at + 2 * LANES]
            values = buf[window, at + 2 * LANES : at + 3 * LANES]
            mask = scal[3 * CROPS + item * NH + head].astype(F32)
            grad = (nt(grads, pack[head * LANES : (head + 1) * LANES, :]) * mask).astype(BF16)
            scores = jnp.where(keys_live, nt(queries, keys) * SCALE, MASKED_SCORE)
            prob = jnp.exp(scores - lse[window, head : head + 1])
            grad_prob = nt(grad, values)
            grad_values = tn(prob.astype(BF16), grad)
            inner = jnp.sum(prob * grad_prob, axis=1, keepdims=True)
            grad_raw = (prob * (grad_prob - inner) * SCALE).astype(BF16)
            dbuf[window, at : at + LANES] = jnp.dot(
                grad_raw, keys, preferred_element_type=F32
            ).astype(BF16)
            dbuf[window, at + LANES : at + 2 * LANES] = tn(grad_raw, queries).astype(BF16)
            dbuf[window, at + 2 * LANES : at + 3 * LANES] = grad_values.astype(BF16)

    each_crop(scal, body)


WIDE = NH * 3 * LANES
SMEM_SPEC = pl.BlockSpec(memory_space=pltpu.SMEM)
VMEM_SPEC = pl.BlockSpec(memory_space=pltpu.VMEM)
ANY_SPEC = pl.BlockSpec(memory_space=pl.ANY)


def attn_fwd(scal, triple, pack):
    return pl.pallas_call(
        attn_fwd_kernel,
        out_shape=(
            jax.ShapeDtypeStruct((SEQ, NH * HD), BF16),
            jax.ShapeDtypeStruct((SEQ, LANES), F32),
        ),
        in_specs=[SMEM_SPEC, VMEM_SPEC, VMEM_SPEC],
        out_specs=(VMEM_SPEC, VMEM_SPEC),
        compiler_params=pltpu.CompilerParams(vmem_limit_bytes=48 * 2**20),
        name="attn_fwd",
    )(scal, triple, pack)


def attn_bwd(scal, triple, grads, lse, pack):
    return pl.pallas_call(
        attn_bwd_kernel,
        out_shape=jax.ShapeDtypeStruct((SEQ, WIDE), BF16),
        in_specs=[SMEM_SPEC] + [VMEM_SPEC] * 4,
        out_specs=VMEM_SPEC,
        compiler_params=pltpu.CompilerParams(vmem_limit_bytes=48 * 2**20),
        name="attn_bwd",
    )(scal, triple, grads, lse, pack)


QTR = 144
WROWS = 576
BIAS = 1408
GROUPS = 24
UNIT_ROWS = 6 * HD
MODS = 6 * D // 8
CUT = 80


def remote(src, dst, sems, k, **where):
    return pltpu.make_async_remote_copy(
        src_ref=src,
        dst_ref=dst,
        send_sem=sems[0].at[k],
        recv_sem=sems[1].at[k],
        device_id=where,
        device_id_type=MESH,
    )


def greet(peers):
    barrier = pltpu.get_barrier_semaphore()
    for where in peers:
        pl.semaphore_signal(barrier, inc=1, device_id=where, device_id_type=MESH)
    pl.semaphore_wait(barrier, len(peers))


def line_peers(p, q, c):
    out = []
    for k in range(1, 8):
        out.append(
            {
                "p": lax.rem(p + k // 4, 2),
                "q": lax.rem(q + (k // 2) % 2, 2),
                "c": lax.rem(c + k % 2, 2),
            }
        )
    return out


def rows_at(start, size):
    return pl.ds(pl.multiple_of(start, 16), size)


class PlaneGather:
    COPIES = 8

    def __init__(self, src, dst, sems, k, y, x, p, loaded=None):
        self.loaded = loaded
        self.over, self.to_x, self.to_y = [], [], []
        for i, (start, size) in enumerate(((0, CUT), (CUT, QTR - CUT))):
            rows = rows_at((y * 2 + x) * QTR + start, size)
            mine = dst.at[rows]
            if loaded is None:
                self.over.append(remote(src.at[rows], mine, sems, k + i, p=1 - p))
            else:
                self.over.append(
                    pltpu.make_async_copy(src.at[start : start + size], mine, loaded.at[i])
                )
            self.to_x.append(remote(mine, mine, sems, k + 2 + i, x=1 - x))
            self.to_y.append(remote(mine, mine, sems, k + 4 + i, y=1 - y))
        from_x = dst.at[rows_at((y * 2 + 1 - x) * QTR, CUT)]
        from_y = dst.at[rows_at(((1 - y) * 2 + x) * QTR + CUT, QTR - CUT)]
        self.on_y = remote(from_x, from_x, sems, k + 6, y=1 - y)
        self.on_x = remote(from_y, from_y, sems, k + 7, x=1 - x)

    def start(self):
        for copy in self.over:
            copy.start()

    def spread(self, i):
        if self.loaded is None:
            self.over[i].wait_recv()
        else:
            self.over[i].wait()
        self.to_x[i].start()
        self.to_y[i].start()

    def forward(self, i):
        if i == 0:
            self.to_x[0].wait_recv()
            self.on_y.start()
        else:
            self.to_y[1].wait_recv()
            self.on_x.start()

    def finish(self):
        for copy in (self.to_y[0], self.to_x[1], self.on_y, self.on_x):
            copy.wait_recv()

    def sent(self):
        copies = self.to_x + self.to_y + [self.on_y, self.on_x]
        for copy in copies if self.loaded is not None else self.over + copies:
            copy.wait_send()


def each_group(body, start=0, stop=BLK // 16, width=4):
    whole = (stop - start) // width

    def step(i, carry):
        for j in range(width):
            body(start + i * width + j)
        return carry

    lax.fori_loop(0, whole, step, 0)
    for g in range(start + whole * width, stop):
        body(g)


def norm_tile(values):
    average = jnp.mean(values, axis=1, keepdims=True)
    centred = values - average
    inverse = lax.rsqrt(jnp.mean(centred * centred, axis=1, keepdims=True) + EPSILON)
    return centred * inverse, inverse


def front_kernel(
    cvec_ref, x_pair, k_pair, g_pair, bias_own, w_a, c_quarter, spread, hot, ada, ada_b,
    t_out, h_out, x_out, k_out, g_out, modg_out, wide_out, wo_out, bias_out, act_out, slope_out, scale_out, c_out,
    part, mods, modg, h, wide, other_a, own_a, tbuf, send, recv, loc,
):
    y, x, p, q, c = (lax.axis_index(name) for name in "yxpqc")
    sems = (send, recv)
    pair = [
        {"q": lax.rem(q + k // 2, 2), "c": lax.rem(c + k % 2, 2)} for k in range(1, 4)
    ]
    plane = [{"y": lax.rem(y + k // 2, 2), "x": lax.rem(x + k % 2, 2)} for k in range(1, 4)]
    rank = y * 2 + x
    waits = []

    def keep_local(src, dst, k):
        copy = pltpu.make_async_copy(src, dst, loc.at[k])
        copy.start()
        return copy

    load_a = keep_local(w_a, own_a, 0)
    cvec = cvec_ref[...]
    sig = 1.0 / (1.0 + jnp.exp(-cvec))
    slope_out[...] = sig * (1.0 + cvec * (1.0 - sig))
    act = (cvec * sig).astype(BF16)
    act_mine = act_out.at[rank]
    act_mine[...] = act
    mod_all = nt(act, ada[...]) + ada_b[...]
    part[0] = mod_all[:16]
    part[1] = mod_all[16:]

    greet(pair + plane + [{"p": 1 - p}])

    def spot(pp, qq, cc):
        return pp * 4 + qq * 2 + cc

    mod_over = remote(part.at[1 - p], mods.at[spot(p, q, c)], sems, 0, p=1 - p)
    mod_over.start()
    own_mod = keep_local(part.at[p], mods.at[spot(p, q, c)], 1)
    mod_own = []
    mod_far = []
    for k, where in enumerate(pair):
        copy = remote(part.at[p], mods.at[spot(p, q, c)], sems, 1 + k, **where)
        copy.start()
        mod_own.append(copy)
    bias_copy = remote(bias_own, bias_out.at[1], sems, 17, p=1 - p)
    bias_copy.start()
    k_copy = remote(k_pair.at[1 - p], k_out.at[p], sems, 18, p=1 - p)
    k_copy.start()
    take_a = PlaneGather(w_a, other_a, sems, 7, y, x, p)
    take_a.start()
    take_c = PlaneGather(c_quarter, c_out, sems, 34, y, x, p, loc.at[18:20])
    take_c.start()
    pieces = ((0, 96), (96, 80))
    x_copies = []
    for i, (start, size) in enumerate(pieces):
        rows = slice(start, start + size)
        x_copies.append(remote(x_pair.at[1 - p, rows], x_out.at[p, rows], sems, 15 + i, p=1 - p))
    waits.append(keep_local(x_pair.at[p], x_out.at[p], 2))
    waits.append(keep_local(k_pair.at[p], k_out.at[p], 3))
    waits.append(keep_local(g_pair.at[p], g_out.at[p], 5))
    own_bias = keep_local(bias_own, bias_out.at[0], 4)
    load_a.wait()
    tails = (own_a.at[UNIT_ROWS:], other_a.at[UNIT_ROWS:])
    mod_over.wait_recv()
    for k, where in enumerate(pair):
        far = mods.at[spot(1 - p, q, c)]
        copy = remote(far, far, sems, 4 + k, **where)
        copy.start()
        mod_far.append(copy)
    acts = []
    for k, where in enumerate(plane):
        copy = remote(act_mine, act_mine, sems, 21 + k, **where)
        copy.start()
        acts.append(copy)

    wide[: 6 * LANES, :] = jnp.dot(
        spread[...], own_a[:UNIT_ROWS, :], preferred_element_type=F32
    ).astype(BF16)

    own_mod.wait()
    for copy in mod_own + mod_far:
        copy.wait_recv()
    full = jnp.concatenate([mods[k] for k in range(8)], axis=1)
    modg[...] = jnp.dot(
        hot[...], full, preferred_element_type=F32, precision=lax.Precision.HIGHEST
    )
    waits.append(keep_local(modg, modg_out, 6))
    scale_out[...] = modg[:, D : 2 * D]

    def place(slot, chip, core):
        return slot * HALF + chip * (2 * BLK) + core * BLK

    def modulate(src, slot, start, size):
        base = place(slot, q, c)

        def group(g):
            values = src[rows_at(g * 16, 16), :].astype(F32)
            normed, _ = norm_tile(values)
            row = slot * (BLK // 16) + g
            shift = modg[pl.ds(row, 1), 0:D]
            scale = modg[pl.ds(row, 1), D : 2 * D]
            h[rows_at(base + g * 16, 16), :] = (normed * (1.0 + scale) + shift).astype(BF16)

        each_group(group, start // 16, (start + size) // 16)

    first, second = p, 1 - p
    spans = [(first, 0, BLK)] + [(second, start, size) for start, size in pieces]
    hops = []
    for i, (slot, start, size) in enumerate(spans):
        mine = h.at[rows_at(place(slot, q, c) + start, size)]
        other = h.at[rows_at(place(slot, 1 - q, c) + start, size)]
        hops.append(
            (
                remote(mine, mine, sems, 24 + 3 * i, q=1 - q),
                remote(mine, mine, sems, 25 + 3 * i, c=1 - c),
                remote(other, other, sems, 26 + 3 * i, c=1 - c),
            )
        )

    modulate(x_pair.at[p], first, 0, BLK)
    hops[0][0].start()
    hops[0][1].start()
    take_c.spread(0)
    take_c.spread(1)
    take_a.spread(0)
    own_bias.wait()
    bias_copy.wait_recv()
    take_a.spread(1)
    for copy in x_copies:
        copy.start()
    hops[0][1].wait_recv()

    def project(slot, chip, half):
        rows = rows_at(place(slot, chip, 0), 2 * BLK)
        cols = slice(half * 6 * LANES, (half + 1) * 6 * LANES)
        line = bias_out[half, 0:1, : 6 * LANES]
        tbuf[rows, cols] = (nt(h[rows, :], wide[cols, :]) + line).astype(BF16)

    def stored(slot, chip, k):
        rows = rows_at(place(slot, chip, 0), 2 * BLK)
        waits.append(keep_local(tbuf.at[rows], t_out.at[rows], k))
        waits.append(keep_local(h.at[rows], h_out.at[rows], k + 4))

    project(first, q, 0)
    take_a.forward(0)
    hops[0][0].wait_recv()
    hops[0][2].start()
    take_a.forward(1)
    hops[0][2].wait_recv()
    take_c.forward(0)
    take_c.forward(1)
    project(first, 1 - q, 0)
    take_a.finish()
    wide[6 * LANES :, :] = jnp.dot(
        spread[...], other_a[:UNIT_ROWS, :], preferred_element_type=F32
    ).astype(BF16)
    waits.append(keep_local(wide, wide_out, 7))
    for k in range(2):
        waits.append(keep_local(tails[k], wo_out.at[k], 8 + k))
    x_copies[0].wait_recv()
    modulate(x_out.at[second], second, *pieces[0])
    hops[1][0].start()
    hops[1][1].start()
    project(first, q, 1)
    stored(first, q, 10)
    x_copies[1].wait_recv()
    g_copy = remote(g_pair.at[1 - p], g_out.at[p], sems, 33, p=1 - p)
    g_copy.start()
    modulate(x_out.at[second], second, *pieces[1])
    hops[2][0].start()
    hops[2][1].start()
    hops[1][0].wait_recv()
    hops[1][2].start()
    project(first, 1 - q, 1)
    stored(first, 1 - q, 11)
    hops[1][1].wait_recv()
    hops[2][1].wait_recv()
    project(second, q, 0)
    hops[2][0].wait_recv()
    hops[2][2].start()
    project(second, q, 1)
    stored(second, q, 12)
    hops[1][2].wait_recv()
    hops[2][2].wait_recv()
    project(second, 1 - q, 0)
    project(second, 1 - q, 1)
    stored(second, 1 - q, 13)
    for copy in acts + [k_copy, g_copy]:
        copy.wait_recv()
    for copy in [mod_over, bias_copy, k_copy, g_copy] + x_copies + mod_own + mod_far + acts:
        copy.wait_send()
    for group in hops:
        for copy in group:
            copy.wait_send()
    take_c.finish()
    for take in (take_a, take_c):
        take.sent()
    for copy in waits:
        copy.wait()


def shape_of(*shape, dtype=BF16):
    return jax.ShapeDtypeStruct(shape, dtype)


def front(*args):
    return pl.pallas_call(
        front_kernel,
        out_shape=(
            shape_of(SEQ, WIDE), shape_of(SEQ, D), shape_of(2, BLK, D), shape_of(2, BLK, LANES),
            shape_of(2, BLK, D), shape_of(GROUPS, 6 * D, dtype=F32), shape_of(WIDE, D),
            shape_of(2, QTR, D), shape_of(2, 8, BIAS, dtype=F32), shape_of(4, 32, D),
            shape_of(32, D, dtype=F32), shape_of(GROUPS, D, dtype=F32), shape_of(WROWS, D),
        ),
        in_specs=[VMEM_SPEC] * 3 + [ANY_SPEC, VMEM_SPEC, ANY_SPEC, ANY_SPEC] + [VMEM_SPEC] * 4,
        out_specs=(
            ANY_SPEC, ANY_SPEC, VMEM_SPEC, VMEM_SPEC, ANY_SPEC, ANY_SPEC, ANY_SPEC, ANY_SPEC,
            VMEM_SPEC, VMEM_SPEC, VMEM_SPEC, VMEM_SPEC, ANY_SPEC,
        ),
        scratch_shapes=[
            pltpu.VMEM((2, 16, MODS), F32),
            pltpu.VMEM((8, 16, MODS), F32),
            pltpu.VMEM((GROUPS, 6 * D), F32),
            pltpu.VMEM((SEQ, D), BF16),
            pltpu.VMEM((WIDE, D), BF16),
            pltpu.VMEM((WROWS, D), BF16),
            pltpu.VMEM((WROWS, D), BF16),
            pltpu.VMEM((SEQ, WIDE), BF16),
            pltpu.SemaphoreType.DMA((42,)),
            pltpu.SemaphoreType.DMA((42,)),
            pltpu.SemaphoreType.DMA((20,)),
        ],
        compiler_params=pltpu.CompilerParams(
            collective_id=6, has_side_effects=True, vmem_limit_bytes=56 * 2**20
        ),
        name="front",
    )(*args)


class PlaneReduce:
    def __init__(self, grads, bufs, sems, k, y, x):
        self.grads, self.y, self.x = grads, y, x
        self.low_in, self.high_in, self.low_out, self.high_out, self.low_end, self.high_end = bufs
        self.first = [
            remote(grads.at[:, self.low(y, 1 - x)], self.low_in.at[0], sems, k, x=1 - x),
            remote(grads.at[:, self.low(1 - y, 1 - x)], self.low_in.at[1], sems, k + 1, x=1 - x),
            remote(grads.at[:, self.high(1 - y, x)], self.high_in.at[0], sems, k + 2, y=1 - y),
            remote(grads.at[:, self.high(1 - y, 1 - x)], self.high_in.at[1], sems, k + 3, y=1 - y),
        ]
        self.second = [
            remote(self.low_out, self.low_end, sems, k + 4, y=1 - y),
            remote(self.high_out, self.high_end, sems, k + 5, x=1 - x),
        ]

    def low(self, y, x):
        return rows_at((y * 2 + x) * QTR, CUT)

    def high(self, y, x):
        return rows_at((y * 2 + x) * QTR + CUT, QTR - CUT)

    def start(self):
        for copy in self.first:
            copy.start()

    def landed(self):
        for copy in self.first:
            copy.wait_recv()

    def middle(self):
        y, x = self.y, self.x
        for shard in range(2):
            self.low_out[shard] = (
                self.grads[shard, self.low(1 - y, x), :].astype(F32)
                + self.low_in[1, shard].astype(F32)
            ).astype(BF16)
            self.high_out[shard] = (
                self.grads[shard, self.high(y, 1 - x), :].astype(F32)
                + self.high_in[1, shard].astype(F32)
            ).astype(BF16)
        for copy in self.second:
            copy.start()

    def arrive(self):
        for copy in self.second:
            copy.wait_recv()

    def total(self, shard):
        low = (
            self.grads[shard, self.low(self.y, self.x), :].astype(F32)
            + self.low_in[0, shard].astype(F32)
            + self.low_end[shard].astype(F32)
        )
        high = (
            self.grads[shard, self.high(self.y, self.x), :].astype(F32)
            + self.high_in[0, shard].astype(F32)
            + self.high_end[shard].astype(F32)
        )
        return low, high

    def settle(self, mine, other):
        self.arrive()
        for shard, ref in enumerate((mine, other)):
            low, high = self.total(shard)
            ref[:CUT, :] = low.astype(ref.dtype)
            ref[CUT:, :] = high.astype(ref.dtype)

    def sent(self):
        for copy in self.first + self.second:
            copy.wait_send()


REDUCE_SCRATCH = [
    pltpu.VMEM((2, 2, CUT, D), BF16),
    pltpu.VMEM((2, 2, QTR - CUT, D), BF16),
    pltpu.VMEM((2, CUT, D), BF16),
    pltpu.VMEM((2, QTR - CUT, D), BF16),
    pltpu.VMEM((2, CUT, D), BF16),
    pltpu.VMEM((2, QTR - CUT, D), BF16),
]


def gelu_both(u):
    cube = 0.044715 * u * u
    t = jnp.tanh(0.7978845608028654 * (u + cube * u))
    half = 0.5 * (1.0 + t)
    slope = half + 0.5 * u * (1.0 - t * t) * (0.7978845608028654 * (1.0 + 3.0 * cube))
    return u * half, slope


def middle_kernel(
    o, x2, k2, modg, g2, wo, wo_far, w_up, up_quarter, w_down, down_other, bias, consts, gmask,
    fin_out, fin_send_out, dx_out, do_out, sums_out, small_out, gwo_out, gwo_far_out, bup_out,
    mine_out, other_out,
    o_in, ysend, yrecv, y1, mixed, h2, dz, act, du, wup, wdown,
    own, csend, crecv, qsend, qrecv, dy, dofar, shared, *rest,
):
    send, recv, loc = rest[12:]
    y, x, p, q, c = (lax.axis_index(name) for name in "yxpqc")
    sems = (send, recv)
    greet([{"q": 1 - q}, {"c": 1 - c}, {"p": 1 - p}, {"x": 1 - x}, {"y": 1 - y}])
    waits = []

    def keep_local(src, dst, k):
        copy = pltpu.make_async_copy(src, dst, loc.at[k])
        copy.start()
        return copy

    def place(slot, chip, core):
        return slot * HALF + chip * (2 * BLK) + core * BLK

    o_copies = []
    for slot in range(2):
        copy = remote(
            o.at[rows_at(place(slot, 1 - q, 0), 2 * BLK)], o_in.at[slot], sems, slot, q=1 - q
        )
        o_copies.append(copy)
    o_copies[0].start()
    take_up = PlaneGather(up_quarter, wup.at[1], sems, 43, y, x, p, loc.at[5:7])
    take_up.start()
    for i in range(2):
        take_up.spread(i)
    own_up = keep_local(w_up, wup.at[0], 1)
    own_down = keep_local(w_down, wdown.at[0], 2)
    other_down = keep_local(down_other, wdown.at[1], 3)

    y_copies = []
    for slot in range(2):
        rows = rows_at(place(slot, q, 0), 2 * BLK)
        o_copies[slot].wait_recv()
        if slot == 0:
            o_copies[1].start()
        whole = jnp.dot(o[rows, :], wo[...], preferred_element_type=F32) + jnp.dot(
            o_in[slot], wo_far[...], preferred_element_type=F32
        )
        own[0, 0:2] = whole.reshape(2, BLK, D)
        ysend[slot] = own[0, 1 - c].astype(BF16)
        y1[slot * BLK : (slot + 1) * BLK, :] = own[0, c]
        copy = remote(ysend.at[slot], yrecv.at[slot], sems, 13 + slot, c=1 - c)
        copy.start()
        y_copies.append(copy)

    take_up.forward(0)
    take_up.forward(1)
    b_out, b_down, w_route = consts[0:1, :], consts[1:2, :], consts[2:3, :]

    def routed(row):
        rows = rows_at(row * 16, 16)
        normed, inverse = norm_tile(mixed[rows, :])
        hidden = normed * (1.0 + modg[pl.ds(row, 1), 4 * D : 5 * D]) + modg[
            pl.ds(row, 1), 3 * D : 4 * D
        ]
        logit = jnp.sum(hidden * w_route, axis=1, keepdims=True)
        route = 1.0 / (1.0 + jnp.exp(-logit))
        kept = k2[rows, 0:1].astype(F32)
        return rows, normed, inverse, hidden, route, kept

    bufs = (h2, dz)

    def hop(array, slot, kind):
        mine = bufs[array].at[rows_at(place(slot, q, c), BLK)]
        far = bufs[array].at[rows_at(place(slot, 1 - q, c), BLK)]
        k = 15 + (slot * 2 + array) * 3 + kind
        if kind == 0:
            return remote(mine, mine, sems, k, q=1 - q)
        if kind == 1:
            return remote(mine, mine, sems, k, c=1 - c)
        return remote(far, far, sems, k, c=1 - c)

    for slot in range(2):
        y_copies[slot].wait_recv()

        def group(g, slot=slot):
            row = slot * (BLK // 16) + g
            rows = rows_at(row * 16, 16)
            branch = y1[rows, :] + yrecv[slot, rows_at(g * 16, 16), :].astype(F32) + b_out
            y1[rows, :] = branch
            mixed[rows, :] = x2[rows, :].astype(F32) + modg[pl.ds(row, 1), 2 * D : 3 * D] * branch
            _, _, _, hidden, route, kept = routed(row)
            there = rows_at(place(slot, q, c) + g * 16, 16)
            h2[there, :] = hidden.astype(BF16)
            gate = modg[pl.ds(row, 1), 5 * D : 6 * D]
            dz[there, :] = (g2[rows, :].astype(F32) * gate * (kept * route)).astype(BF16)

        each_group(group)
        for array in range(2):
            if slot == 0:
                hop(array, slot, 0).start()
            hop(array, slot, 1).start()

    own_up.wait()
    own_down.wait()
    other_down.wait()
    take_up.finish()

    def core_copy(array, side, slot):
        k = 27 + (array * 2 + side) * 2 + slot
        return remote(csend.at[array, side, slot], crecv.at[array, side, slot], sems, k, c=1 - c)

    def chip_copy(array, slot):
        return remote(qsend.at[array, slot], qrecv.at[array, slot], sems, 35 + array * 2 + slot, q=1 - q)

    def far_out(slot):
        for array in range(2):
            core_copy(array, 1, slot).wait_recv()
            qsend[array, slot] = (
                own[array, 2] + crecv[array, 1, slot].astype(F32)
            ).astype(BF16)
            chip_copy(array, slot).start()

    def feed(step, carry):
        side, slot = step // 2, lax.rem(step, 2)
        chip = lax.rem(q + side, 2)
        start = place(slot, chip, 0)
        kept_at = slot + side * (2 - slot)

        @pl.when(step == 0)
        def _():
            for array in range(2):
                hop(array, 0, 1).wait_recv()

        @pl.when(step == 1)
        def _():
            for array in range(2):
                hop(array, 1, 1).wait_recv()

        @pl.when(step == 2)
        def _():
            for array in range(2):
                hop(array, 0, 0).wait_recv()
                hop(array, 0, 2).start()
                hop(array, 1, 0).start()
            for array in range(2):
                hop(array, 0, 2).wait_recv()

        @pl.when(step == 3)
        def _():
            for array in range(2):
                hop(array, 1, 0).wait_recv()
                hop(array, 1, 2).start()
            far_out(0)
            for array in range(2):
                hop(array, 1, 2).wait_recv()

        def tile(part, carry):
            rows = rows_at(start + part * BLK, BLK)
            up_all = wup[...].reshape(D, D)
            down_all = wdown[...].reshape(D, D)
            u = nt(h2[rows, :], up_all) + bias[0:1, :]
            value, slope = gelu_both(u)
            row0 = start // 16 + part * (BLK // 16)
            mask = jnp.concatenate(
                [
                    jnp.broadcast_to(gmask[pl.ds(row0 + k, 1), :], (16, D))
                    for k in range(BLK // 16)
                ],
                axis=0,
            )
            act[rows, :] = (value * mask).astype(BF16)
            da = nt(dz[rows, :], down_all)
            du[rows, :] = (slope * mask * da).astype(BF16)
            z_part = jnp.dot(act[rows, :], down_all, preferred_element_type=F32)
            h_part = jnp.dot(du[rows, :], up_all, preferred_element_type=F32)

            @pl.when(part == c)
            def _():
                own[0, kept_at] = z_part
                own[1, kept_at] = h_part

            @pl.when(part != c)
            def _():
                csend[0, side, slot] = z_part.astype(BF16)
                csend[1, side, slot] = h_part.astype(BF16)

            return carry

        lax.fori_loop(0, 2, tile, 0)
        for array in range(2):
            core_copy(array, side, slot).start()
        return carry

    lax.fori_loop(0, 4, feed, 0)
    far_out(1)

    take_up.sent()

    def weight_grads(left, right, out):
        def chunk(j, carry):
            cols = pl.ds(pl.multiple_of(j * 384, LANES), 384)
            block = tn(left[:, cols], right[...]).astype(BF16)
            for k in range(2):
                at = j * 2 + k
                out[at // 3, rows_at(lax.rem(at, 3) * 192, 192), :] = block[k * 192 : (k + 1) * 192]
            return carry

        lax.fori_loop(0, 3, chunk, 0)

    down_sum = PlaneReduce(wdown, rest[0:6], sems, 59, y, x)
    up_sum = PlaneReduce(wup, rest[6:12], sems, 65, y, x)
    weight_grads(act, dz, wdown)
    down_sum.start()
    weight_grads(du, h2, wup)
    up_sum.start()
    bup_out[...] = jnp.dot(jnp.ones((8, SEQ), BF16), du[...], preferred_element_type=F32)

    sums_out[22:24, :] = jnp.zeros((2, 4 * D), F32)
    shared[22:24, :] = jnp.zeros((2, 3 * D), F32)
    dy_copies = []
    do_copies = []
    for slot in range(2):
        for array in range(2):
            core_copy(array, 0, slot).wait_recv()
            chip_copy(array, slot).wait_recv()

        def back(g, slot=slot):
            row = slot * (BLK // 16) + g
            rows, normed, inverse, hidden, route, kept = routed(row)
            here = rows_at(g * 16, 16)

            def total(array):
                return (
                    own[array, slot, here, :]
                    + crecv[array, 0, slot, here, :].astype(F32)
                    + qrecv[array, slot, here, :].astype(F32)
                )

            gate_one = modg[pl.ds(row, 1), 2 * D : 3 * D]
            gate_two = modg[pl.ds(row, 1), 5 * D : 6 * D]
            scale_two = modg[pl.ds(row, 1), 4 * D : 5 * D]
            grad = g2[rows, :].astype(F32)
            pass_on = kept * route
            branch = total(0) + b_down
            low = (mixed[rows, :] + gate_two * pass_on * branch).astype(BF16)

            @pl.when(p == slot)
            def _():
                fin_out[here, :] = low

            @pl.when(p != slot)
            def _():
                fin_send_out[here, :] = low

            grad_gate_two = grad * pass_on * branch
            gated = grad * gate_two
            logit = (
                jnp.sum(gated * branch, axis=1, keepdims=True) * kept * route * (1.0 - route)
            )
            dh = total(1) + logit * w_route
            e = dh * (1.0 + scale_two)
            dx = grad + inverse * (
                e
                - jnp.mean(e, axis=1, keepdims=True)
                - normed * jnp.mean(e * normed, axis=1, keepdims=True)
            )
            dx_out[rows, :] = dx
            dyb = dx * gate_one
            dy[slot, c, here, :] = dyb.astype(BF16)

            def down(v):
                return jnp.sum(v, axis=0, keepdims=True)

            at = pl.ds(row, 1)
            shared[at, 0:D] = down(dyb)
            shared[at, D : 2 * D] = down(gated * pass_on)
            shared[at, 2 * D : 3 * D] = down(logit * hidden)
            sums_out[at, 0:D] = down(dx * y1[rows, :])
            sums_out[at, D : 2 * D] = down(dh)
            sums_out[at, 2 * D : 3 * D] = down(dh * normed)
            sums_out[at, 3 * D : 4 * D] = down(grad_gate_two)

        each_group(back)
        copy = remote(dy.at[slot, c], dy.at[slot, c], sems, 39 + slot, c=1 - c)
        copy.start()
        dy_copies.append(copy)
        total = (down_sum, up_sum)[slot]
        total.landed()
        total.middle()
    for slot in range(2):
        dy_copies[slot].wait_recv()
        rows = rows_at(place(slot, q, 0), 2 * BLK)
        grads = dy[slot].reshape(2 * BLK, D)
        dofar[slot] = nt(grads, wo_far[...]).astype(BF16)
        copy = remote(dofar.at[slot], do_out.at[rows], sems, 41 + slot, q=1 - q)
        copy.start()
        do_copies.append(copy)
        do_out[rows, :] = nt(grads, wo[...]).astype(BF16)

    for k in range(3):
        small_out[k : k + 1, :] = jnp.sum(shared[:, k * D : (k + 1) * D], axis=0, keepdims=True)

    def out_grad(left):
        return sum(tn(left(slot), dy[slot].reshape(2 * BLK, D)) for slot in range(2))

    gwo_far_out[...] = out_grad(lambda slot: o_in[slot]).astype(BF16)
    gwo_out[...] = out_grad(lambda slot: o[rows_at(place(slot, q, 0), 2 * BLK), :]).astype(BF16)
    for copy in do_copies:
        copy.wait_recv()
    for copy in o_copies + y_copies + dy_copies + do_copies:
        copy.wait_send()
    for k, total in enumerate((down_sum, up_sum)):
        mine, other = own.at[1, k, pl.ds(0, QTR)], ysend.at[k, pl.ds(0, QTR)]
        total.settle(mine, other)
        total.sent()
        waits.append(keep_local(mine, mine_out.at[k], 2 * k))
        waits.append(keep_local(other, other_out.at[k], 2 * k + 1))
    for slot in range(2):
        for array in range(2):
            for kind in range(3):
                hop(array, slot, kind).wait_send()
            for side in range(2):
                core_copy(array, side, slot).wait_send()
            chip_copy(array, slot).wait_send()
    for copy in waits:
        copy.wait()


def middle(*args):
    return pl.pallas_call(
        middle_kernel,
        out_shape=(
            shape_of(BLK, D), shape_of(BLK, D), shape_of(2 * BLK, D, dtype=F32),
            shape_of(SEQ, NH * HD), shape_of(GROUPS, 4 * D, dtype=F32),
            shape_of(8, D, dtype=F32), shape_of(NH * HD, D), shape_of(NH * HD, D),
            shape_of(8, D, dtype=F32), shape_of(2, QTR, D, dtype=F32), shape_of(2, QTR, D),
        ),
        in_specs=[VMEM_SPEC] * 7 + [ANY_SPEC] * 4 + [VMEM_SPEC] * 3,
        out_specs=(VMEM_SPEC,) * 9 + (ANY_SPEC,) * 2,
        scratch_shapes=[
            pltpu.VMEM((2, 2 * BLK, NH * HD), BF16),
            pltpu.VMEM((2, BLK, D), BF16),
            pltpu.VMEM((2, BLK, D), BF16),
            pltpu.VMEM((2 * BLK, D), F32),
            pltpu.VMEM((2 * BLK, D), F32),
            pltpu.VMEM((SEQ, D), BF16),
            pltpu.VMEM((SEQ, D), BF16),
            pltpu.VMEM((SEQ, D), BF16),
            pltpu.VMEM((SEQ, D), BF16),
            pltpu.VMEM((2, WROWS, D), BF16),
            pltpu.VMEM((2, WROWS, D), BF16),
            pltpu.VMEM((2, 3, BLK, D), F32),
            pltpu.VMEM((2, 2, 2, BLK, D), BF16),
            pltpu.VMEM((2, 2, 2, BLK, D), BF16),
            pltpu.VMEM((2, 2, BLK, D), BF16),
            pltpu.VMEM((2, 2, BLK, D), BF16),
            pltpu.VMEM((2, 2, BLK, D), BF16),
            pltpu.VMEM((2, 2 * BLK, NH * HD), BF16),
            pltpu.VMEM((GROUPS, 3 * D), F32),
        ]
        + REDUCE_SCRATCH * 2
        + [
            pltpu.SemaphoreType.DMA((71,)),
            pltpu.SemaphoreType.DMA((71,)),
            pltpu.SemaphoreType.DMA((9,)),
        ],
        compiler_params=pltpu.CompilerParams(
            collective_id=7, has_side_effects=True, vmem_limit_bytes=63 * 2**20
        ),
        name="middle",
    )(*args)


class LineReduce:
    def __init__(self, mine, other, landed, out, sems, k, y, x, p):
        self.mine, self.landed, self.out = mine, landed, out
        self.rows = rows_at((y * 2 + x) * QTR, QTR)
        self.over = remote(other, landed, sems, k, p=1 - p)
        place = out.at[self.rows]
        self.to_x = remote(place, place, sems, k + 1, x=1 - x)
        self.to_y = remote(place, place, sems, k + 2, y=1 - y)
        from_x = out.at[rows_at((y * 2 + 1 - x) * QTR, CUT)]
        from_y = out.at[rows_at(((1 - y) * 2 + x) * QTR + CUT, QTR - CUT)]
        self.on_y = remote(from_x, from_x, sems, k + 3, y=1 - y)
        self.on_x = remote(from_y, from_y, sems, k + 4, x=1 - x)

    def start(self):
        self.over.start()

    def spread(self):
        self.over.wait_recv()
        self.out[self.rows, :] = (self.mine[...] + self.landed[...].astype(F32)).astype(BF16)
        self.to_x.start()
        self.to_y.start()

    def forward(self):
        self.to_x.wait_recv()
        self.on_y.start()
        self.to_y.wait_recv()
        self.on_x.start()

    def finish(self):
        self.on_y.wait_recv()
        self.on_x.wait_recv()

    def sent(self):
        for copy in (self.over, self.to_x, self.to_y, self.on_y, self.on_x):
            copy.wait_send()


def back_kernel(
    d, h1, mine, other, wo_g, wo_in, hot, spread, x2, scale, sums_two, smalls, b_up, slope,
    wide_at, dx_at, ada_at,
    tokens_out, a_out, up_out, down_out, mod_out, cond_out,
    own, csend, crecv, qsend, qrecv, wideg, grads, sums, parcel, parcels, lsum, modline, condbuf,
    tsend, landed, mine_a, other_a, wide, dx, *rest,
):
    send, recv, loc = rest[6:]
    y, x, p, q, c = (lax.axis_index(name) for name in "yxpqc")
    sems = (send, recv)
    pair = [
        {"q": lax.rem(q + k // 2, 2), "c": lax.rem(c + k % 2, 2)} for k in range(1, 4)
    ]
    plane = [{"y": lax.rem(y + k // 2, 2), "x": lax.rem(x + k % 2, 2)} for k in range(1, 4)]
    greet(pair + plane + [{"p": 1 - p}])
    rank = y * 2 + x

    def keep_local(src, dst, k):
        copy = pltpu.make_async_copy(src, dst, loc.at[k])
        copy.start()
        return copy

    def place(slot, chip, core):
        return slot * HALF + chip * (2 * BLK) + core * BLK

    outs = (down_out, up_out, a_out)
    reduce_a = PlaneReduce(grads, rest[:6], sems, 0, y, x)
    owns = (mine.at[0], mine.at[1], mine_a)
    sends = (other.at[0], other.at[1], other_a)
    lines = [
        LineReduce(owns[k], sends[k], landed.at[k], outs[k], sems, 18 + 5 * k, y, x, p)
        for k in range(3)
    ]
    lines[0].start()
    loads = [
        keep_local(wide_at, wide, 0), keep_local(dx_at, dx, 1),
    ]

    def weight_chunk(j, carry):
        cols = pl.ds(pl.multiple_of(j * 256, LANES), 256)
        wideg[rows_at(j * 256, 256), :] = tn(d[:, cols], h1[...]).astype(BF16)
        return carry

    lax.fori_loop(0, 6, weight_chunk, 0)
    for shard in range(2):
        grads[shard, :UNIT_ROWS, :] = tn(
            spread[...], wideg[shard * 6 * LANES : (shard + 1) * 6 * LANES, :]
        ).astype(BF16)
        rows = slice(shard * QTR, (shard + 1) * QTR)
        grads[shard, UNIT_ROWS:, :] = (
            wo_g[rows, :].astype(F32) + wo_in[rows, :].astype(F32)
        ).astype(BF16)
    reduce_a.start()
    ada = wideg.at[:MODS]
    loads.append(keep_local(ada_at, ada, 2))
    lines[0].spread()
    lines[1].start()
    loads[0].wait()
    def core_copy(side, slot):
        return remote(
            csend.at[side, slot], crecv.at[side, slot], sems, 34 + side * 2 + slot, c=1 - c
        )

    def chip_copy(slot):
        return remote(qsend.at[slot], qrecv.at[slot], sems, 38 + slot, q=1 - q)

    def far_out(slot):
        core_copy(1, slot).wait_recv()
        qsend[slot] = (own[1, slot] + crecv[1, slot].astype(F32)).astype(BF16)
        chip_copy(slot).start()

    def through(step, carry):
        side, slot = 1 - step // 2, lax.rem(step, 2)
        start = place(slot, lax.rem(q + side, 2), 0)
        rows = rows_at(start, 2 * BLK)
        part = jnp.dot(d[rows, :], wide[...], preferred_element_type=F32)

        @pl.when(c == 0)
        def _():
            own[side, slot] = part[:BLK]
            csend[side, slot] = part[BLK:].astype(BF16)

        @pl.when(c == 1)
        def _():
            own[side, slot] = part[BLK:]
            csend[side, slot] = part[:BLK].astype(BF16)

        core_copy(side, slot).start()

        @pl.when(step == 1)
        def _():
            far_out(0)

        @pl.when(step == 2)
        def _():
            far_out(1)

        return carry

    lax.fori_loop(0, 4, through, 0)

    ones = jnp.ones((8, SEQ), BF16)
    col_sums = jnp.dot(ones, d[...], preferred_element_type=F32)

    lines[0].forward()
    reduce_a.landed()
    reduce_a.middle()
    lines[1].spread()
    reduce_a.settle(mine_a, other_a)
    lines[2].start()
    lines[1].forward()
    loads[1].wait()

    sums[...] = jnp.zeros_like(sums)
    for slot in range(2):
        core_copy(0, slot).wait_recv()
        chip_copy(slot).wait_recv()

        def group(g, slot=slot):
            row = slot * (BLK // 16) + g
            rows = rows_at(row * 16, 16)
            here = rows_at(g * 16, 16)
            normed, inverse = norm_tile(x2[rows, :].astype(F32))
            dh = (
                own[0, slot, here, :]
                + crecv[0, slot, here, :].astype(F32)
                + qrecv[slot, here, :].astype(F32)
            )
            at = pl.ds(row, 1)
            e = dh * (1.0 + scale[at, :])
            out = dx[rows, :] + inverse * (
                e
                - jnp.mean(e, axis=1, keepdims=True)
                - normed * jnp.mean(e * normed, axis=1, keepdims=True)
            )
            tsend[slot, here, :] = out.astype(BF16)

            @pl.when(slot == p)
            def _():
                tokens_out[p, here, :] = out

            sums[at, 0:D] = jnp.sum(dh, axis=0, keepdims=True)
            sums[at, D : 2 * D] = jnp.sum(dh * normed, axis=0, keepdims=True)

        each_group(group)

    token_copy = remote(tsend.at[1 - p], tsend.at[2], sems, 40, p=1 - p)
    two = jnp.concatenate([sums[...], sums_two[...]], axis=1)
    full = lax.dot_general(
        hot[...], two, (((0,), (0,)), ((), ())), preferred_element_type=F32,
        precision=lax.Precision.HIGHEST,
    )
    for k in range(8):
        there = parcel.at[k // 4, (k // 2) % 2, k % 2]
        there[...] = full[:, k * MODS : (k + 1) * MODS]
        there[11:14, : D // 8] = smalls[0:3, k * (D // 8) : (k + 1) * (D // 8)]
    for shard in range(2):
        heads = col_sums[0:1, shard * 6 * LANES : (shard + 1) * 6 * LANES]
        pieces = [b_up[0:1, shard * WROWS : (shard + 1) * WROWS]]
        for unit in (0, 2, 3, 5):
            pieces.append(heads[:, unit * LANES : unit * LANES + HD])
        parcel[lax.rem(p + shard, 2), q, c, 14:15, :] = jnp.concatenate(pieces, axis=1)
    here = q * 2 + c
    copies = []
    for k, where in enumerate(pair):
        copy = remote(
            parcel.at[:, where["q"], where["c"]], parcels.at[here], sems, 41 + k, **where
        )
        copy.start()
        copies.append(copy)
    own_parcel = keep_local(parcel.at[:, q, c], parcels.at[here], 3)
    own_parcel.wait()
    for copy in copies:
        copy.wait_recv()
    line_sum = sum(parcels[k] for k in range(4))
    lsum[0:2] = line_sum
    over = remote(lsum.at[1 - p], lsum.at[2], sems, 44, p=1 - p)
    over.start()
    copies.append(over)
    lines[2].spread()
    token_copy.start()
    over.wait_recv()
    modline[p] = lsum[p].astype(BF16)
    modline[1 - p] = lsum[2].astype(BF16)
    mods = []
    for k, where in enumerate(plane):
        copy = remote(modline, mod_out.at[rank], sems, 48 + k, **where)
        copy.start()
        mods.append(copy)
    own_mod = keep_local(modline, mod_out.at[rank], 4)

    loads[2].wait()
    condbuf[0] = jnp.dot(
        modline[...].reshape(32, MODS), ada[...], preferred_element_type=F32
    ).astype(BF16)
    conds = []
    for k, where in enumerate(({"c": 1 - c}, {"q": 1 - q}, {"p": 1 - p})):
        copy = remote(condbuf.at[2 * k], condbuf.at[2 * k + 1], sems, 51 + k, **where)
        copy.start()
        conds.append(copy)
        if k == 0:
            lines[2].forward()
        copy.wait_recv()
        total = condbuf[2 * k].astype(F32) + condbuf[2 * k + 1].astype(F32)
        if k < 2:
            condbuf[2 * k + 2] = total.astype(BF16)
    cond_out[...] = total * slope[...]

    token_copy.wait_recv()
    tokens_out[1 - p] = tsend[2].astype(F32)
    for k in range(3):
        lines[k].finish()
    own_mod.wait()
    for copy in mods:
        copy.wait_recv()
    for copy in [token_copy] + copies + mods + conds:
        copy.wait_send()
    for slot in range(2):
        for side in range(2):
            core_copy(side, slot).wait_send()
        chip_copy(slot).wait_send()
    reduce_a.sent()
    for k in range(3):
        lines[k].sent()


def back(*args):
    return pl.pallas_call(
        back_kernel,
        out_shape=(
            shape_of(2, BLK, D, dtype=F32), shape_of(WROWS, D), shape_of(WROWS, D),
            shape_of(WROWS, D), shape_of(4, 2, 16, MODS), shape_of(32, D, dtype=F32),
        ),
        in_specs=[VMEM_SPEC] * 14 + [ANY_SPEC] * 3,
        out_specs=(VMEM_SPEC,) * 6,
        scratch_shapes=[
            pltpu.VMEM((2, 2, BLK, D), F32),
            pltpu.VMEM((2, 2, BLK, D), BF16),
            pltpu.VMEM((2, 2, BLK, D), BF16),
            pltpu.VMEM((2, BLK, D), BF16),
            pltpu.VMEM((2, BLK, D), BF16),
            pltpu.VMEM((WIDE, D), BF16),
            pltpu.VMEM((2, WROWS, D), BF16),
            pltpu.VMEM((GROUPS, 2 * D), F32),
            pltpu.VMEM((2, 2, 2, 16, MODS), F32),
            pltpu.VMEM((4, 2, 16, MODS), F32),
            pltpu.VMEM((3, 16, MODS), F32),
            pltpu.VMEM((2, 16, MODS), BF16),
            pltpu.VMEM((6, 32, D), BF16),
            pltpu.VMEM((3, BLK, D), BF16),
            pltpu.VMEM((3, QTR, D), BF16),
            pltpu.VMEM((QTR, D), F32),
            pltpu.VMEM((QTR, D), BF16),
            pltpu.VMEM((WIDE, D), BF16),
            pltpu.VMEM((2 * BLK, D), F32),
        ]
        + REDUCE_SCRATCH
        + [
            pltpu.SemaphoreType.DMA((54,)),
            pltpu.SemaphoreType.DMA((54,)),
            pltpu.SemaphoreType.DMA((5,)),
        ],
        compiler_params=pltpu.CompilerParams(
            collective_id=8, has_side_effects=True, vmem_limit_bytes=63 * 2**20
        ),
        name="back",
    )(*args)


def swap(values, axis):
    return lax.ppermute(values, axis, SWAP)


def layer_device(
    tokens, cond, lengths, pads, timesteps, head_mask, group_mask, keep, ada_w, ada_b, w_qkv, b_qv,
    w_out, b_out, w_up, b_up, w_down, b_down, w_route, grad_out,
):
    highest = lax.Precision.HIGHEST
    y, x, p, q, c = (lax.axis_index(name) for name in "yxpqc")
    rank = y * 2 + x
    first = p == 0
    shard = p * 4 + q * 2 + c
    partner = shard ^ 4

    spread = np.zeros((6 * LANES, UNIT_ROWS), np.float32)
    for unit in range(6):
        spread[np.arange(HD) + unit * LANES, np.arange(HD) + unit * HD] = 1.0
    spread = jnp.asarray(spread, BF16)
    w_up_rows = jnp.transpose(w_up)
    down_quarter = swap(lax.dynamic_slice_in_dim(w_down, rank * QTR, QTR, 0), "p")
    w_a = jnp.concatenate([jnp.transpose(w_qkv), w_out])
    pairs = b_qv.reshape(2, 2, HD).astype(F32)
    bias_own = jnp.pad(
        jnp.stack([pairs[:, 0], jnp.zeros_like(pairs[:, 0]), pairs[:, 1]], axis=1),
        ((0, 0), (0, 0), (0, LANES - HD)),
    ).reshape(6 * LANES)
    bias_own = jnp.pad(jnp.concatenate([bias_own, b_up.astype(F32)]), (0, BIAS - 1344))
    bias_own = jnp.broadcast_to(bias_own, (8, BIAS))

    def row_of(values):
        return jnp.where(first, values[0], values[1])

    row_len = row_of(lengths)
    row_pad = row_of(pads)
    ends = jnp.cumsum(row_len)
    starts = ends - row_len

    def group_hot(dq, dc):
        base = (q ^ dq) * (2 * BLK) + (c ^ dc) * BLK
        places = base + jnp.arange(2)[:, None] * HALF + jnp.arange(BLK // 16)[None, :] * 16
        inside = (places[..., None] >= starts) & (places[..., None] < ends)
        return jnp.pad(inside.astype(F32), ((0, 0), (0, 0), (0, 5)))

    hot = group_hot(0, 0)
    hot_rows = jnp.pad(hot.reshape(22, 16), ((0, 2), (0, 0)))

    def by_row(values):
        return jnp.transpose(values, (1, 0, 2))

    def items(values):
        return jnp.pad(values, ((0, 0), (0, 5), (0, 0))).reshape(32, -1)

    keep_wide = jnp.broadcast_to(keep.T.astype(BF16)[..., None], (2, BLK, LANES))
    ada_rows = jnp.transpose(ada_w)
    (
        triple, hidden_one, token_low, keep_low, grad_low, mod_groups, w_wide, w_out_all, biases,
        act_all, slope, scale_one, w_down_other,
    ) = front(
        items(cond.astype(F32) + time_embed(timesteps)), by_row(tokens), keep_wide, by_row(grad_out), bias_own, w_a, down_quarter, spread,
        hot_rows, ada_rows, ada_b.astype(F32)[None],
    )
    up_quarter, triple = lax.optimization_barrier(
        (lax.dynamic_slice_in_dim(w_up_rows, rank * QTR, QTR, 0), triple)
    )
    up_quarter = swap(up_quarter, "p")
    w_out_far = swap(w_out_all, "q")

    head_row = row_of(head_mask)
    heads_here = jnp.concatenate(
        [
            lax.dynamic_slice_in_dim(head_row, shard * 2, 2, 1),
            lax.dynamic_slice_in_dim(head_row, partner * 2, 2, 1),
        ],
        axis=1,
    )
    scal = jnp.concatenate(
        [
            starts,
            row_len // UNIT,
            row_len - row_pad,
            heads_here.reshape(-1),
        ]
    ).astype(jnp.int32)
    pack = np.zeros((NH * LANES, NH * HD), np.float32)
    for head in range(NH):
        pack[np.arange(HD) + head * LANES, np.arange(HD) + head * HD] = 1.0
    pack = jnp.asarray(pack, BF16)
    attended, lse = attn_fwd(scal, triple, pack)
    group_row = row_of(group_mask)
    groups_here = jnp.concatenate(
        [
            lax.dynamic_slice_in_dim(group_row, shard * 2, 2, 1),
            lax.dynamic_slice_in_dim(group_row, partner * 2, 2, 1),
        ],
        axis=1,
    ).astype(F32)
    all_places = jnp.arange(SEQ // 16)[:, None] * 16
    all_hot = ((all_places >= starts) & (all_places < ends)).astype(F32)
    group_wide = jnp.repeat(
        jnp.dot(all_hot, groups_here, precision=highest), GW, axis=1
    )
    consts = jnp.pad(jnp.stack([b_out, b_down, w_route]).astype(F32), ((0, 5), (0, 0)))
    b_up_two = jnp.concatenate([biases[0, :, 768:1344], biases[1, :, 768:1344]], axis=1)
    (
        final, final_send, grad_mixed, grad_attended, sums_two, smalls, wo_low, wo_far, b_up_sums,
        mine, other,
    ) = middle(
        attended, token_low.reshape(2 * BLK, D), keep_low.reshape(2 * BLK, LANES), mod_groups,
        grad_low.reshape(2 * BLK, D), w_out_all.reshape(2 * QTR, D),
        w_out_far.reshape(2 * QTR, D), w_up_rows, up_quarter, w_down, w_down_other, b_up_two,
        consts, group_wide,
    )
    wo_in = swap(wo_far, "q")
    final_in = swap(final_send, "p")
    final_pair = jnp.stack([jnp.where(first, final, final_in), jnp.where(first, final_in, final)])
    d_all = attn_bwd(scal, triple, grad_attended, lse, pack)
    token_pair, low_a, low_up, low_down, mod_all, grad_cond = back(
        d_all, hidden_one, mine, other, wo_low, wo_in, hot_rows, spread,
        token_low.reshape(2 * BLK, D), scale_one, sums_two, smalls, b_up_sums,
        slope, w_wide, grad_mixed, ada_rows,
    )
    out_a = low_a.astype(F32)
    act_items = jnp.where(jnp.arange(32)[:, None] % 16 < CROPS, act_all, 0)
    grad_ada_b = jnp.sum(mod_all[:, :, :CROPS], axis=(0, 1, 2), dtype=F32)
    rest = jnp.sum(mod_all[:, :, CROPS:], axis=(0, 1), dtype=F32)
    grad_ada_w = tn(mod_all.reshape(128, MODS), act_items.reshape(128, D))
    return (
        by_row(final_pair), by_row(token_pair), grad_cond.reshape(2, 16, D)[:, :CROPS],
        jnp.transpose(grad_ada_w), grad_ada_b, jnp.transpose(out_a[:UNIT_ROWS]), rest[3, 2 * GW :],
        out_a[UNIT_ROWS:], rest[0, : D // 8], jnp.transpose(low_up.astype(F32)), rest[3, : 2 * GW],
        low_down.astype(F32), rest[1, : D // 8], rest[2, : D // 8],
    )


IN_SPECS = (
    ("heads", "rows", None), ("rows", None, None), ("rows", None), ("rows", None), ("rows", None),
    ("rows", None, None), ("rows", None, None), ("heads", "rows"), (None, "heads"), ("heads",),
    (None, "heads"), ("heads",), ("heads", None), (), (None, "heads"), ("heads",), ("heads", None),
    (), (), ("heads", "rows", None),
)
OUT_SPECS = (
    ("heads", "rows", None), ("heads", "rows", None), ("rows", None, None), (None, "heads"),
    ("heads",), (None, "heads"), ("heads",), ("heads", None), ("heads",), (None, "heads"),
    ("heads",), ("heads", None), ("heads",), ("heads",),
)


def solution(mesh):
    paired = mesh.shape["rows"] == 4 and mesh.shape["heads"] == 8
    if paired:
        mesh = Mesh(mesh.devices.reshape(2, 2, 2, 2, 2), ("y", "x", "p", "q", "c"))
        names = {"rows": ("y", "x"), "heads": ("p", "q", "c"), None: None}
    else:
        names = {"rows": "rows", "heads": "heads", None: None}

    def specs(items):
        return tuple(P(*(names[name] for name in item)) for item in items)

    return jax.shard_map(
        layer_device if paired else per_device,
        mesh=mesh,
        in_specs=specs(IN_SPECS),
        out_specs=specs(OUT_SPECS),
        check_vma=False,
    )
```
